512 devices in a mesh: dp: 16 (over x, y_hi), slab: 32 (over z, y_lo, core).
Axes of the slice: x: 4, y: 8 (y_hi: 4, y_lo: 2; y = y_hi * 2 + y_lo), z: 8, core: 2. Of those that a mesh axis runs over, the one named last changes fastest.
Arguments:
- sensitivity: bfloat16 [12288, 98304], P('dp', 'slab'), may hold values from -6 to 6
- panel_index: int32 [1], replicated, may hold values from 0 to 47
- cell_class: int32 [96, 1024], P('slab'), may hold values from 0 to 7
- tear_layer: int32 [1024], replicated, may hold values from 1 to 95
- coef_table: float32 [3, 2, 8], replicated, may hold values from 0.02 to 0.1
Outputs:
- panel_block: float32 [12288, 128], P(('dp', 'slab'))
The draws below stay inside these ranges and needn't reach their ends.
All inputs are finite; a program needn't handle non-finite values.
Results may differ from the reference program's by a relative error of at most 0.0015.
Values may be sent and summed in bfloat16 or wider, within the bound.
A program may use at most 64 MiB of HBM per device.

```python
import math
import jax
import jax.numpy as jnp
from jax import lax

HX = 32
HY = 32
PANEL = 128
CLASSES = 8
SWEEPS = 3
DATA = 12288
PANELS = 96
NZ = 96
HXY = 1024
CELLS = 98304


def with_ends(result, key, smallest, largest):
    place = [jax.random.randint(jax.random.fold_in(key, axis), (), 0, length) for axis, length in enumerate(result.shape)]
    longest = result.shape.index(max(result.shape))
    neighbour = place[:longest] + [(place[longest] + 1) % result.shape[longest]] + place[longest + 1:]
    return result.at[tuple(place)].set(smallest).at[tuple(neighbour)].set(largest)


def steps_of(rng, shape, shards, smallest, largest):
    loudness = 1.0
    for dim, blocks in shards:
        heights = jax.random.uniform(jax.random.fold_in(jax.random.fold_in(rng, 6), dim), (blocks,), jnp.float32, smallest / len(shards), largest / len(shards))
        loudness = loudness * jnp.repeat(jnp.exp(heights), shape[dim] // blocks).reshape((-1,) + (1,) * (len(shape) - 1 - dim))
    return loudness


def normal_values(own_key, shape, width, most, shards=(), held_as=jnp.bfloat16):
    factor_of = steps_of(own_key, shape, shards, -0.22, 0.18) if shards else 1.0
    values = jax.random.normal(own_key, shape, jnp.float32) * width * factor_of
    return jnp.minimum(jnp.maximum(values, -most), most).astype(held_as)


def setup_inputs(seed: int = 0) -> dict:
    key_of = jax.random.split(jax.random.key(seed), 6)
    return {
        "sensitivity": normal_values(key_of[0], (DATA, CELLS), 1.0, 6.0, ((0, 16), (1, 32))),
        "panel_index": jax.random.randint(key_of[1], (1,), 0, PANELS // 2).astype(jnp.int32),
        "cell_class": with_ends(jax.random.randint(key_of[2], (NZ, HXY), 0, CLASSES), jax.random.fold_in(key_of[2], 1), 0, CLASSES - 1).astype(jnp.int32),
        "tear_layer": with_ends(jax.random.randint(key_of[3], (HXY,), 1, NZ), jax.random.fold_in(key_of[3], 1), 1, NZ - 1).astype(jnp.int32),
        "coef_table": jnp.clip(jnp.exp(jax.random.uniform(key_of[4], (SWEEPS, 2, CLASSES), jnp.float32, math.log(0.02), math.log(0.1))), 0.02, 0.1),
    }


def horizontal(field, width_y):
    count = field.shape[-1]
    padded = jnp.pad(field, ((0, 0), (0, 0), (width_y, width_y)))
    north = padded[..., :count]
    south = padded[..., 2 * width_y:]
    column = jnp.arange(count) % width_y
    west = jnp.where(column > 0, padded[..., width_y - 1:width_y - 1 + count], 0.0)
    east = jnp.where(column < width_y - 1, padded[..., width_y + 1:width_y + 1 + count], 0.0)
    return north + south + west + east - 4.0 * field

def sweep(extended, classes, tear_layer, coef_table, number, first, layers, width_y):
    middle = extended[:, 1:-1]
    upper = extended[:, :-2]
    lower = extended[:, 2:]
    count = middle.shape[1]
    layer = first + 1 + jnp.arange(count, dtype=jnp.int32)
    open_up = (tear_layer[None, :] != layer[:, None]).astype(jnp.float32)
    open_down = (tear_layer[None, :] != (layer + 1)[:, None]).astype(jnp.float32)
    inner = classes[1:-1]
    coef_h = jnp.zeros(inner.shape, jnp.float32)
    coef_v = jnp.zeros(inner.shape, jnp.float32)
    for level in range(coef_table.shape[2]):
        coef_h = jnp.where(inner == level, coef_table[number, 0, level], coef_h)
        coef_v = jnp.where(inner == level, coef_table[number, 1, level], coef_v)
    vertical = open_up * (upper - middle) + open_down * (lower - middle)
    updated = middle + coef_h * horizontal(middle, width_y) + 4.0 * coef_v * vertical
    valid = ((layer >= 0) & (layer < layers)).astype(jnp.float32)[:, None]
    return updated * valid

def reference(sensitivity, panel_index, cell_class, tear_layer, coef_table):
    start = panel_index[0]
    rows = lax.dynamic_slice_in_dim(sensitivity, (start * PANEL).astype(jnp.int32), PANEL, 0)
    field = rows.astype(jnp.float32).reshape(PANEL, NZ, HX * HY)
    padded_class = jnp.pad(cell_class, ((1, 1), (0, 0)))
    for number in range(SWEEPS):
        extended = jnp.pad(field, ((0, 0), (1, 1), (0, 0)))
        field = sweep(extended, padded_class, tear_layer, coef_table, number, -1, NZ, HY)
    smoothed = field.reshape(PANEL, CELLS).astype(jnp.bfloat16)
    full = lax.dot_general(sensitivity, smoothed, (((1,), (1,)), ((), ())), preferred_element_type=jnp.float32)
    full = full * (1.0 / math.sqrt(CELLS))
    row_index = jnp.arange(DATA, dtype=jnp.int32)[:, None]
    col_index = jnp.arange(PANEL, dtype=jnp.int32)[None, :]
    keep = row_index >= start * PANEL + col_index
    return jnp.where(keep, full, 0.0)
```

```python
import functools
import math

import jax
import jax.numpy as jnp
from jax import lax
from jax.experimental import pallas as pl
from jax.experimental.pallas import tpu as pltpu
from jax.sharding import PartitionSpec as P

WIDTH_Y = 32
PANEL = 128
GROUP = 32
PIECE = 8
CHUNK = 384
VMEM_LIMIT = 63 * 1024 * 1024


def kernel(
    slabs,
    panel_hbm,
    table_hbm,
    sens_hbm,
    class_hbm,
    tear_hbm,
    out_ref,
    panel_ref,
    table_ref,
    class_ref,
    tear_ref,
    sens,
    send1,
    recv_early,
    recv_late,
    fwd1,
    pair1,
    chosen1,
    send2,
    recv2,
    raw,
    halo,
    class_halo,
    class_ext,
    coef,
    field,
    gath,
    panel,
    product,
    sibling_in,
    part,
    parts_in,
    load_sem,
    class_send,
    class_recv,
    s1_send,
    s1_recv,
    s2_send,
    s2_recv,
    h_send,
    h_recv,
    g5_send,
    g5_recv,
    g6_send,
    g6_recv,
    sib_send,
    sib_recv,
    rs_send,
    rs_recv,
):
    f32 = jnp.float32
    bf16 = jnp.bfloat16
    dp = lax.axis_index("dp")
    me = lax.axis_index("slab")
    x = lax.div(dp, 4)
    yh = lax.rem(dp, 4)
    groups, _, cells = sens.shape
    chips = slabs // 2
    core = lax.rem(me, 2)
    chip = lax.div(me, 2)
    sibling = me + 1 - 2 * core
    depth, plane = class_ref.shape
    layers = depth * slabs
    out_rows = out_ref.shape[0]
    panels_dev = groups * GROUP // PANEL
    right = lax.rem(x + 1, 4)
    left = lax.rem(x + 3, 4)
    before = lax.rem(me + slabs - 1, slabs)
    after = lax.rem(me + 1, slabs)

    def at(x_to, y_to, slab_to):
        return (x_to * 4 + y_to, slab_to)

    def remote(src, dst, send_sem, recv_sem, target):
        return pltpu.make_async_remote_copy(
            src_ref=src,
            dst_ref=dst,
            send_sem=send_sem,
            recv_sem=recv_sem,
            device_id=target,
            device_id_type=pl.DeviceIdType.MESH,
        )

    loads = 4

    def load(i):
        part_of = pl.ds(i * (groups // loads), groups // loads)
        return pltpu.make_async_copy(sens_hbm.at[part_of], sens.at[part_of], load_sem.at[0])

    small = [
        pltpu.make_async_copy(source, target, load_sem.at[1 + i])
        for i, (source, target) in enumerate(
            [(class_hbm, class_ref), (tear_hbm, tear_ref), (table_hbm, table_ref), (panel_hbm, panel_ref)]
        )
    ]
    for copy in small:
        copy.start()
    for i in range(loads):
        load(i).start()

    barrier = pltpu.get_barrier_semaphore()

    def greet(target):
        pl.semaphore_signal(
            barrier, inc=1, device_id=target, device_id_type=pl.DeviceIdType.MESH
        )

    greet(at(right, yh, me))
    greet(at(left, yh, me))
    for dj in (1, 2, 3):
        greet(at(x, lax.rem(yh + dj, 4), me))

    greet((dp, before))
    greet((dp, after))

    @pl.loop(1, chips)
    def _(d):
        greet((dp, lax.rem(me + 2 * d, slabs)))

    for copy in small:
        copy.wait()
    pltpu.make_async_copy(sens_hbm, sens, load_sem.at[0]).wait()

    start = panel_ref[0]
    owner = lax.div(start, panels_dev)
    x_owner = lax.div(owner, 4)
    y_owner = lax.rem(owner, 4)
    first_group = lax.rem(start, panels_dev) * 4

    @pl.when(x < 2)
    def _():
        for q in range(4):
            rows = sens[first_group + q].astype(f32).reshape(4, PIECE, cells).astype(bf16)
            for j in range(4):
                send1[q, lax.rem(j - yh + 6, 4)] = rows[j]

    pl.semaphore_wait(barrier, 7 + chips - 1)

    class_after = remote(class_ref, class_halo.at[0], class_send.at[0], class_recv.at[0], (dp, after))
    class_before = remote(class_ref, class_halo.at[1], class_send.at[1], class_recv.at[1], (dp, before))
    class_after.start()
    class_before.start()

    def early(q):
        return send1.at[q, 0:2]

    def late(q):
        return send1.at[q, 2:4]

    mate = at(1 - x, yh, me)
    outer = at(3 - x, yh, me)
    copy_far = remote(early(x + 2), fwd1, s1_send.at[0], s1_recv.at[0], outer)
    copy_in = remote(early(1 - x), recv_early.at[x], s1_send.at[1], s1_recv.at[1], mate)
    copy_mate = remote(late(x + 2), pair1.at[x], s1_send.at[2], s1_recv.at[2], mate)
    copy_out = remote(early(3 - x), recv_early.at[x], s1_send.at[3], s1_recv.at[3], outer)
    copy_in_late = remote(late(1 - x), recv_late.at[x], s1_send.at[4], s1_recv.at[4], mate)
    copy_chosen = remote(chosen1, recv_late.at[0], s1_send.at[5], s1_recv.at[5], outer)
    copy_on = remote(fwd1, recv_early.at[3 - x], s1_send.at[1], s1_recv.at[1], at(5 - x, yh, me))

    def arrived(slot, to):
        remote(to, to, s1_send.at[slot], s1_recv.at[slot], at(right, yh, me)).wait_recv()

    @pl.when(x < 2)
    def _():
        for copy in (copy_far, copy_in, copy_mate, copy_out, copy_in_late):
            copy.start()
        recv_early[x] = send1[x, 0:2]
        recv_late[x] = send1[x, 2:4]
        pair1[x] = send1[3 - x, 2:4]

    class_after.wait_recv()
    class_before.wait_recv()
    class_ext[0:2] = class_halo[0, depth - 2 : depth]
    class_ext[2 : 2 + depth] = class_ref[...]
    class_ext[2 + depth : 4 + depth] = class_halo[1, 0:2]
    class_ext[4 + depth :] = jnp.zeros_like(class_ext[4 + depth :])
    classes = class_ext[...]
    layer = me * depth - 2 + lax.broadcasted_iota(jnp.int32, classes.shape, 0)
    valid = (layer >= 0) & (layer < layers)
    tear = jnp.broadcast_to(tear_ref[...], classes.shape)
    open_up = tear != layer
    open_down = tear != layer + 1
    for k in range(table_ref.shape[0]):
        a = jnp.zeros(classes.shape, f32)
        b = jnp.zeros(classes.shape, f32)
        for level in range(table_ref.shape[2]):
            a = jnp.where(classes == level, table_ref[k, 0, level], a)
            b = jnp.where(classes == level, table_ref[k, 1, level], b)
        a = jnp.where(valid, a, 0.0)
        b = jnp.where(valid, 4.0 * b, 0.0)
        up = jnp.where(open_up, b, 0.0)
        down = jnp.where(open_down, b, 0.0)
        coef[k, 0] = 1.0 - 4.0 * a - up - down
        coef[k, 1] = a
        coef[k, 2] = up
        coef[k, 3] = down

    def copy_y(dj):
        return remote(
            send2.at[dj], recv2.at[yh], s2_send.at[dj], s2_recv.at[yh], at(x, lax.rem(yh + dj, 4), me)
        )

    def wait_y(dj):
        j = lax.rem(yh + dj, 4)
        remote(send2.at[dj], recv2.at[j], s2_send.at[dj], s2_recv.at[j], at(x, j, me)).wait_recv()

    @pl.when(x >= 2)
    def _():
        arrived(0, fwd1)
        copy_on.start()
        arrived(3, recv_early.at[3 - x])

    arrived(1, recv_early.at[jnp.where(x < 2, 1 - x, x - 2)])
    chosen = recv_early[x_owner]
    send2[2] = chosen[0]
    copy_y(2).start()
    send2[3] = chosen[1]
    copy_y(3).start()

    @pl.when(x < 2)
    def _():
        arrived(2, pair1.at[1 - x])
        chosen1[...] = pair1[x_owner]
        copy_chosen.start()
        arrived(4, recv_late.at[1 - x])

    @pl.when(x >= 2)
    def _():
        arrived(5, recv_late.at[0])

    chosen = recv_late[jnp.where(x < 2, x_owner, 0)]
    send2[1] = chosen[1]
    copy_y(1).start()
    recv2[yh] = chosen[0]
    for dj in (2, 1, 3):
        wait_y(dj)

    raw[...] = recv2[y_owner]
    halo_after = remote(raw, halo.at[0], h_send.at[0], h_recv.at[0], (dp, after))
    halo_before = remote(raw, halo.at[1], h_send.at[1], h_recv.at[1], (dp, before))
    halo_after.start()
    halo_before.start()

    for g in range(depth):
        field[0, depth + g] = raw[:, g * plane : (g + 1) * plane].astype(f32)
    position = lax.broadcasted_iota(jnp.int32, (PIECE, plane), 1)
    column = lax.rem(position, WIDTH_Y)
    sweeps = table_ref.shape[0]

    def smooth(k, l):
        u = field[k, l]
        north = jnp.where(position >= WIDTH_Y, pltpu.roll(u, WIDTH_Y, 1), 0.0)
        south = jnp.where(position < plane - WIDTH_Y, pltpu.roll(u, plane - WIDTH_Y, 1), 0.0)
        west = jnp.where(column > 0, pltpu.roll(u, 1, 1), 0.0)
        east = jnp.where(column < WIDTH_Y - 1, pltpu.roll(u, plane - 1, 1), 0.0)
        e = l - depth + 2
        updated = (
            coef[k, 0, e : e + 1] * u
            + coef[k, 1, e : e + 1] * ((north + south) + (west + east))
            + coef[k, 2, e : e + 1] * field[k, l - 1]
            + coef[k, 3, e : e + 1] * field[k, l + 1]
        )
        if k + 1 < sweeps:
            field[k + 1, l] = updated
        else:
            g = l - depth
            gath[x, 0, :, g * plane : (g + 1) * plane] = updated.astype(bf16)

    def copy_g5(dj):
        return remote(
            gath.at[x, 0], gath.at[x, 4 - dj], g5_send.at[dj], g5_recv.at[4 - dj], at(x, lax.rem(yh + dj, 4), me)
        )

    def wait_g5(dj):
        remote(gath.at[x, 0], gath.at[x, dj], g5_send.at[dj], g5_recv.at[dj], at(right, yh, me)).wait_recv()

    def copy_g6(way, source, first, last, slot):
        part_of = gath.at[source, first:last]
        return remote(part_of, part_of, g6_send.at[slot], g6_recv.at[slot], at(way, yh, me))

    to_right = [copy_g6(right, x, 0, 1, 0), copy_g6(right, x, 1, 4, 1), copy_g6(right, left, 0, 2, 2)]
    to_left = [copy_g6(left, x, 0, 1, 3), copy_g6(left, x, 1, 4, 4), copy_g6(left, right, 2, 4, 5)]
    far = lax.rem(x + 2, 4)
    from_left = [copy_g6(right, left, 0, 1, 0), copy_g6(right, left, 1, 4, 1), copy_g6(right, far, 0, 2, 2)]
    from_right = [copy_g6(left, right, 0, 1, 3), copy_g6(left, right, 1, 4, 4), copy_g6(left, far, 2, 4, 5)]

    inner = [(0, l) for l in range(depth + 1, 2 * depth - 1)]
    done = set(inner)
    for k, l in inner:
        smooth(k, l)

    halo_after.wait_recv()
    halo_before.wait_recv()
    has_before = jnp.where(me > 0, 1.0, 0.0).astype(f32)
    has_after = jnp.where(me < slabs - 1, 1.0, 0.0).astype(f32)
    for g in range(depth):
        cut = slice(g * plane, (g + 1) * plane)
        field[0, g] = halo[0, :, cut].astype(f32) * has_before
        field[0, 2 * depth + g] = halo[1, :, cut].astype(f32) * has_after

    def smooth_all(k, l):
        if k < 0 or (k, l) in done:
            return
        for near in (l - 1, l, l + 1):
            smooth_all(k - 1, near)
        smooth(k, l)
        done.add((k, l))

    for t in range(depth):
        smooth_all(sweeps - 1, depth + t)
    for dj in (2, 1, 3):
        copy_g5(dj).start()
    to_right[0].start()
    to_left[0].start()
    for dj in (1, 3, 2):
        wait_g5(dj)
    to_right[1].start()
    to_left[1].start()

    def into_panel(source):
        rows = gath[source].astype(f32).reshape(GROUP, cells).astype(bf16)
        panel[pl.ds(pl.multiple_of(source * GROUP, GROUP), GROUP)] = rows

    into_panel(x)
    from_left[0].wait_recv()
    from_right[0].wait_recv()
    from_left[1].wait_recv()
    to_right[2].start()
    from_right[1].wait_recv()
    to_left[2].start()
    into_panel(left)
    into_panel(right)
    from_left[2].wait_recv()
    from_right[2].wait_recv()
    into_panel(far)

    data_rows = groups * GROUP
    chunk = min(CHUNK, data_rows)
    chunks = data_rows // chunk
    blocks = chunk // (2 * out_rows)
    own_chunk = lax.div(chip, blocks)

    def copy_sibling(turn):
        return remote(
            product.at[turn, 1 - core], sibling_in.at[turn], sib_send.at[turn], sib_recv.at[turn], (dp, sibling)
        )

    def copy_part(to):
        return remote(part.at[to], parts_in.at[chip], rs_send.at[0], rs_recv.at[0], (dp, 2 * to + core))

    def chunk_of(turn):
        return lax.rem(own_chunk + 1 + turn, chunks)

    def multiply(turn):
        here = chunk_of(turn)
        rows = sens[pl.ds(here * (chunk // GROUP), chunk // GROUP)].reshape(chunk, cells)
        result = lax.dot_general(rows, panel[...], (((1,), (1,)), ((), ())), preferred_element_type=f32)
        result = result.reshape(blocks, 2, out_rows, PANEL)
        for half in range(2):
            product[turn, half] = result[:, half]
        copy_sibling(turn).start()

    def send_parts(turn):
        here = chunk_of(turn)
        copy_sibling(turn).wait_recv()
        part[pl.ds(here * blocks, blocks)] = (product[turn, core] + sibling_in[turn]).astype(bf16)
        for i in range(blocks):
            to = here * blocks + i

            @pl.when(to != chip)
            def _(to=to):
                copy_part(to).start()

    for turn in range(chunks):
        multiply(turn)
        if turn > 0:
            send_parts(turn - 1)
    send_parts(chunks - 1)
    parts_in[chip] = part[chip]

    class_after.wait_send()
    class_before.wait_send()
    halo_after.wait_send()
    halo_before.wait_send()

    @pl.when(x < 2)
    def _():
        for copy in (copy_far, copy_in, copy_mate, copy_out, copy_in_late, copy_chosen):
            copy.wait_send()

    @pl.when(x >= 2)
    def _():
        copy_on.wait_send()

    for dj in (1, 2, 3):
        copy_y(dj).wait_send()
        copy_g5(dj).wait_send()
    for copy in to_right + to_left:
        copy.wait_send()
    for turn in range(chunks):
        copy_sibling(turn).wait_send()

    others = remote(
        part.at[0 : chips - 1], parts_in.at[0 : chips - 1], rs_send.at[0], rs_recv.at[0], (dp, sibling)
    )
    others.wait_send()
    others.wait_recv()

    total = jnp.zeros(out_ref.shape, f32)
    for i in range(chips):
        total = total + parts_in[i].astype(f32)
    total = total * (1.0 / math.sqrt(layers * plane))
    col = lax.broadcasted_iota(jnp.int32, out_ref.shape, 1)
    shift = PIECE * yh
    total = jnp.where(
        lax.rem(col, GROUP) >= shift,
        pltpu.roll(total, shift, 1),
        pltpu.roll(total, shift + PANEL - GROUP, 1),
    )
    base = dp * data_rows + me * out_rows
    row = base + lax.broadcasted_iota(jnp.int32, out_ref.shape, 0)
    out_ref[...] = jnp.where(row >= start * PANEL + col, total, 0.0)


def body(sensitivity, panel_index, cell_class, tear_layer, coef_table):
    rows, cells = sensitivity.shape
    depth, plane = cell_class.shape
    slabs = lax.axis_size("slab")
    out_rows = rows // slabs
    groups = rows // GROUP
    chips = slabs // 2
    chunks = max(1, rows // CHUNK)
    bf16 = jnp.bfloat16
    dma = pltpu.SemaphoreType.DMA
    sweeps = coef_table.shape[0]
    ext = -(-(depth + 4) // 8) * 8
    return pl.pallas_call(
        functools.partial(kernel, slabs),
        out_shape=jax.ShapeDtypeStruct((out_rows, PANEL), jnp.float32),
        in_specs=[pl.BlockSpec(memory_space=pltpu.HBM)] * 5,
        out_specs=pl.BlockSpec(memory_space=pltpu.VMEM),
        scratch_shapes=[
            pltpu.SMEM(panel_index.shape, jnp.int32),
            pltpu.SMEM(coef_table.shape, jnp.float32),
            pltpu.VMEM((depth, plane), jnp.int32),
            pltpu.VMEM((1, plane), jnp.int32),
            pltpu.VMEM((groups, GROUP, cells), bf16),
            pltpu.VMEM((4, 4, PIECE, cells), bf16),
            pltpu.VMEM((2, 2, PIECE, cells), bf16),
            pltpu.VMEM((2, 2, PIECE, cells), bf16),
            pltpu.VMEM((2, PIECE, cells), bf16),
            pltpu.VMEM((2, 2, PIECE, cells), bf16),
            pltpu.VMEM((2, PIECE, cells), bf16),
            pltpu.VMEM((4, PIECE, cells), bf16),
            pltpu.VMEM((4, PIECE, cells), bf16),
            pltpu.VMEM((PIECE, cells), bf16),
            pltpu.VMEM((2, PIECE, cells), bf16),
            pltpu.VMEM((2, depth, plane), jnp.int32),
            pltpu.VMEM((ext, plane), jnp.int32),
            pltpu.VMEM((sweeps, 4, ext, plane), jnp.float32),
            pltpu.VMEM((sweeps, 3 * depth, PIECE, plane), jnp.float32),
            pltpu.VMEM((4, 4, PIECE, cells), bf16),
            pltpu.VMEM((PANEL, cells), bf16),
            pltpu.VMEM((chunks, 2, rows // chunks // (2 * out_rows), out_rows, PANEL), jnp.float32),
            pltpu.VMEM((chunks, rows // chunks // (2 * out_rows), out_rows, PANEL), jnp.float32),
            pltpu.VMEM((chips, out_rows, PANEL), bf16),
            pltpu.VMEM((chips, out_rows, PANEL), bf16),
            dma((5,)),
            dma((2,)),
            dma((2,)),
            dma((6,)),
            dma((6,)),
            dma((4,)),
            dma((4,)),
            dma((2,)),
            dma((2,)),
            dma((4,)),
            dma((4,)),
            dma((6,)),
            dma((6,)),
            dma((chunks,)),
            dma((chunks,)),
            dma((1,)),
            dma((1,)),
        ],
        compiler_params=pltpu.CompilerParams(
            collective_id=0, has_side_effects=True, vmem_limit_bytes=VMEM_LIMIT
        ),
        cost_estimate=pl.CostEstimate(
            flops=2 * rows * cells * PANEL, bytes_accessed=2 * rows * cells, transcendentals=0
        ),
        name="panel",
    )(
        panel_index,
        coef_table,
        sensitivity.reshape(groups, GROUP, cells),
        cell_class,
        tear_layer.reshape(1, plane),
    )


def solution(mesh):
    return jax.shard_map(
        body,
        mesh=mesh,
        in_specs=(P("dp", "slab"), P(), P("slab", None), P(), P()),
        out_specs=P(("dp", "slab"), None),
        check_vma=False,
    )
```

```python
import functools
import math

import jax
import jax.numpy as jnp
from jax import lax
from jax.experimental import pallas as pl
from jax.experimental.pallas import tpu as pltpu
from jax.sharding import PartitionSpec as P

WIDTH_Y = 32
PANEL = 128
GROUP = 32
PIECE = 8
CHUNK = 384
VMEM_LIMIT = 63 * 1024 * 1024


def kernel(
    slabs,
    panel_hbm,
    table_hbm,
    sens_hbm,
    class_hbm,
    tear_hbm,
    out_ref,
    panel_ref,
    table_ref,
    class_ref,
    tear_ref,
    sens,
    send1,
    recv_early,
    recv_late,
    fwd1,
    pair1,
    chosen1,
    send2,
    recv2,
    raw,
    halo,
    class_halo,
    class_ext,
    coef,
    field,
    gath,
    panel,
    product,
    sibling_in,
    part,
    parts_in,
    load_sem,
    class_send,
    class_recv,
    s1_send,
    s1_recv,
    s2_send,
    s2_recv,
    h_send,
    h_recv,
    g5_send,
    g5_recv,
    g6_send,
    g6_recv,
    sib_send,
    sib_recv,
    rs_send,
    rs_recv,
):
    f32 = jnp.float32
    bf16 = jnp.bfloat16
    dp = lax.axis_index("dp")
    me = lax.axis_index("slab")
    x = lax.div(dp, 4)
    yh = lax.rem(dp, 4)
    groups, _, cells = sens.shape
    chips = slabs // 2
    core = lax.rem(me, 2)
    chip = lax.div(me, 2)
    sibling = me + 1 - 2 * core
    depth, plane = class_ref.shape
    layers = depth * slabs
    out_rows = out_ref.shape[0]
    panels_dev = groups * GROUP // PANEL
    right = lax.rem(x + 1, 4)
    left = lax.rem(x + 3, 4)
    before = lax.rem(me + slabs - 1, slabs)
    after = lax.rem(me + 1, slabs)

    def at(x_to, y_to, slab_to):
        return (x_to * 4 + y_to, slab_to)

    def remote(src, dst, send_sem, recv_sem, target):
        return pltpu.make_async_remote_copy(
            src_ref=src,
            dst_ref=dst,
            send_sem=send_sem,
            recv_sem=recv_sem,
            device_id=target,
            device_id_type=pl.DeviceIdType.MESH,
        )

    loads = 4

    def load(i):
        part_of = pl.ds(i * (groups // loads), groups // loads)
        return pltpu.make_async_copy(sens_hbm.at[part_of], sens.at[part_of], load_sem.at[0])

    small = [
        pltpu.make_async_copy(source, target, load_sem.at[1 + i])
        for i, (source, target) in enumerate(
            [(class_hbm, class_ref), (tear_hbm, tear_ref), (table_hbm, table_ref), (panel_hbm, panel_ref)]
        )
    ]
    for copy in small:
        copy.start()
    for i in range(loads):
        load(i).start()

    barrier = pltpu.get_barrier_semaphore()

    def greet(target):
        pl.semaphore_signal(
            barrier, inc=1, device_id=target, device_id_type=pl.DeviceIdType.MESH
        )

    greet(at(right, yh, me))
    greet(at(left, yh, me))
    for dj in (1, 2, 3):
        greet(at(x, lax.rem(yh + dj, 4), me))

    greet((dp, before))
    greet((dp, after))

    @pl.loop(1, chips)
    def _(d):
        greet((dp, lax.rem(me + 2 * d, slabs)))

    for copy in small:
        copy.wait()
    pltpu.make_async_copy(sens_hbm, sens, load_sem.at[0]).wait()

    start = panel_ref[0]
    owner = lax.div(start, panels_dev)
    x_owner = lax.div(owner, 4)
    y_owner = lax.rem(owner, 4)
    first_group = lax.rem(start, panels_dev) * 4

    @pl.when(x < 2)
    def _():
        for q in range(4):
            rows = sens[first_group + q].astype(f32).reshape(4, PIECE, cells).astype(bf16)
            for j in range(4):
                send1[q, lax.rem(j - yh + 6, 4)] = rows[j]

    pl.semaphore_wait(barrier, 7 + chips - 1)

    class_after = remote(class_ref, class_halo.at[0], class_send.at[0], class_recv.at[0], (dp, after))
    class_before = remote(class_ref, class_halo.at[1], class_send.at[1], class_recv.at[1], (dp, before))
    class_after.start()
    class_before.start()

    def early(q):
        return send1.at[q, 0:2]

    def late(q):
        return send1.at[q, 2:4]

    mate = at(1 - x, yh, me)
    outer = at(3 - x, yh, me)
    copy_far = remote(early(x + 2), fwd1, s1_send.at[0], s1_recv.at[0], outer)
    copy_in = remote(early(1 - x), recv_early.at[x], s1_send.at[1], s1_recv.at[1], mate)
    copy_mate = remote(late(x + 2), pair1.at[x], s1_send.at[2], s1_recv.at[2], mate)
    copy_out = remote(early(3 - x), recv_early.at[x], s1_send.at[3], s1_recv.at[3], outer)
    copy_in_late = remote(late(1 - x), recv_late.at[x], s1_send.at[4], s1_recv.at[4], mate)
    copy_chosen = remote(chosen1, recv_late.at[0], s1_send.at[5], s1_recv.at[5], outer)
    copy_on = remote(fwd1, recv_early.at[3 - x], s1_send.at[1], s1_recv.at[1], at(5 - x, yh, me))

    def arrived(slot, to):
        remote(to, to, s1_send.at[slot], s1_recv.at[slot], at(right, yh, me)).wait_recv()

    @pl.when(x < 2)
    def _():
        for copy in (copy_far, copy_mate, copy_in, copy_out, copy_in_late):
            copy.start()
        recv_early[x] = send1[x, 0:2]
        recv_late[x] = send1[x, 2:4]
        pair1[x] = send1[3 - x, 2:4]

    class_after.wait_recv()
    class_before.wait_recv()
    class_ext[0:2] = class_halo[0, depth - 2 : depth]
    class_ext[2 : 2 + depth] = class_ref[...]
    class_ext[2 + depth : 4 + depth] = class_halo[1, 0:2]
    class_ext[4 + depth :] = jnp.zeros_like(class_ext[4 + depth :])
    classes = class_ext[...]
    layer = me * depth - 2 + lax.broadcasted_iota(jnp.int32, classes.shape, 0)
    valid = (layer >= 0) & (layer < layers)
    tear = jnp.broadcast_to(tear_ref[...], classes.shape)
    open_up = tear != layer
    open_down = tear != layer + 1
    for k in range(table_ref.shape[0]):
        a = jnp.zeros(classes.shape, f32)
        b = jnp.zeros(classes.shape, f32)
        for level in range(table_ref.shape[2]):
            a = jnp.where(classes == level, table_ref[k, 0, level], a)
            b = jnp.where(classes == level, table_ref[k, 1, level], b)
        a = jnp.where(valid, a, 0.0)
        b = jnp.where(valid, 4.0 * b, 0.0)
        up = jnp.where(open_up, b, 0.0)
        down = jnp.where(open_down, b, 0.0)
        coef[k, 0] = 1.0 - 4.0 * a - up - down
        coef[k, 1] = a
        coef[k, 2] = up
        coef[k, 3] = down

    def copy_y(dj):
        return remote(
            send2.at[dj], recv2.at[yh], s2_send.at[dj], s2_recv.at[yh], at(x, lax.rem(yh + dj, 4), me)
        )

    def wait_y(dj):
        j = lax.rem(yh + dj, 4)
        remote(send2.at[dj], recv2.at[j], s2_send.at[dj], s2_recv.at[j], at(x, j, me)).wait_recv()

    @pl.when(x >= 2)
    def _():
        arrived(0, fwd1)
        copy_on.start()
        arrived(3, recv_early.at[3 - x])

    arrived(1, recv_early.at[jnp.where(x < 2, 1 - x, x - 2)])
    chosen = recv_early[x_owner]
    send2[2] = chosen[0]
    copy_y(2).start()
    send2[3] = chosen[1]
    copy_y(3).start()

    @pl.when(x < 2)
    def _():
        arrived(2, pair1.at[1 - x])
        chosen1[...] = pair1[x_owner]
        copy_chosen.start()
        arrived(4, recv_late.at[1 - x])

    @pl.when(x >= 2)
    def _():
        arrived(5, recv_late.at[0])

    chosen = recv_late[jnp.where(x < 2, x_owner, 0)]
    send2[1] = chosen[1]
    copy_y(1).start()
    recv2[yh] = chosen[0]
    for dj in (2, 1, 3):
        wait_y(dj)

    raw[...] = recv2[y_owner]
    halo_after = remote(raw, halo.at[0], h_send.at[0], h_recv.at[0], (dp, after))
    halo_before = remote(raw, halo.at[1], h_send.at[1], h_recv.at[1], (dp, before))
    halo_after.start()
    halo_before.start()

    for g in range(depth):
        field[0, depth + g] = raw[:, g * plane : (g + 1) * plane].astype(f32)
    position = lax.broadcasted_iota(jnp.int32, (PIECE, plane), 1)
    column = lax.rem(position, WIDTH_Y)
    sweeps = table_ref.shape[0]

    def smooth(k, l):
        u = field[k, l]
        north = jnp.where(position >= WIDTH_Y, pltpu.roll(u, WIDTH_Y, 1), 0.0)
        south = jnp.where(position < plane - WIDTH_Y, pltpu.roll(u, plane - WIDTH_Y, 1), 0.0)
        west = jnp.where(column > 0, pltpu.roll(u, 1, 1), 0.0)
        east = jnp.where(column < WIDTH_Y - 1, pltpu.roll(u, plane - 1, 1), 0.0)
        e = l - depth + 2
        updated = (
            coef[k, 0, e : e + 1] * u
            + coef[k, 1, e : e + 1] * ((north + south) + (west + east))
            + coef[k, 2, e : e + 1] * field[k, l - 1]
            + coef[k, 3, e : e + 1] * field[k, l + 1]
        )
        if k + 1 < sweeps:
            field[k + 1, l] = updated
        else:
            g = l - depth
            gath[x, 0, :, g * plane : (g + 1) * plane] = updated.astype(bf16)

    def copy_g5(place, dj, lands):
        target = at(x, lax.rem(yh + dj, 4), me)
        return remote(gath.at[x, 0], gath.at[x, lands], g5_send.at[place], g5_recv.at[lands], target)

    over_y = [copy_g5(3, 2, 3), copy_g5(1, 1, 2), copy_g5(2, 3, 1)]

    def wait_g5(place):
        remote(gath.at[x, 0], gath.at[x, place], g5_send.at[place], g5_recv.at[place], at(right, yh, me)).wait_recv()

    def copy_g6(way, source, first, last, slot):
        part_of = gath.at[source, first:last]
        return remote(part_of, part_of, g6_send.at[slot], g6_recv.at[slot], at(way, yh, me))

    rounds = [(0, 1), (1, 3), (3, 4)]
    far = lax.rem(x + 2, 4)
    to_right = [copy_g6(right, x, *span, i) for i, span in enumerate(rounds)]
    to_left = [copy_g6(left, x, *span, 3 + i) for i, span in enumerate(rounds)]
    from_left = [copy_g6(right, left, *span, i) for i, span in enumerate(rounds)]
    from_right = [copy_g6(left, right, *span, 3 + i) for i, span in enumerate(rounds)]
    relays = [copy_g6(right, left, 0, 2, 6), copy_g6(left, right, 2, 3, 7), copy_g6(left, right, 3, 4, 8)]
    relayed = [copy_g6(right, far, 0, 2, 6), copy_g6(left, far, 2, 3, 7), copy_g6(left, far, 3, 4, 8)]

    inner = [(0, l) for l in range(depth + 1, 2 * depth - 1)]
    done = set(inner)
    for k, l in inner:
        smooth(k, l)

    halo_after.wait_recv()
    halo_before.wait_recv()
    has_before = jnp.where(me > 0, 1.0, 0.0).astype(f32)
    has_after = jnp.where(me < slabs - 1, 1.0, 0.0).astype(f32)
    for g in range(depth):
        cut = slice(g * plane, (g + 1) * plane)
        field[0, g] = halo[0, :, cut].astype(f32) * has_before
        field[0, 2 * depth + g] = halo[1, :, cut].astype(f32) * has_after

    def smooth_all(k, l):
        if k < 0 or (k, l) in done:
            return
        for near in (l - 1, l, l + 1):
            smooth_all(k - 1, near)
        smooth(k, l)
        done.add((k, l))

    for t in range(depth):
        smooth_all(sweeps - 1, depth + t)
    for copy in over_y + [to_right[0], to_left[0]]:
        copy.start()

    def into_panel(source):
        rows = gath[source].astype(f32).reshape(GROUP, cells).astype(bf16)
        panel[pl.ds(pl.multiple_of(source * GROUP, GROUP), GROUP)] = rows

    wait_g5(1)
    wait_g5(2)
    to_right[1].start()
    to_left[1].start()
    wait_g5(3)
    to_right[2].start()
    to_left[2].start()
    from_left[0].wait_recv()
    from_left[1].wait_recv()
    relays[0].start()
    from_right[0].wait_recv()
    from_right[1].wait_recv()
    relays[1].start()
    from_right[2].wait_recv()
    relays[2].start()
    into_panel(x)
    into_panel(right)
    from_left[2].wait_recv()
    into_panel(left)
    for copy in relayed:
        copy.wait_recv()
    into_panel(far)

    data_rows = groups * GROUP
    chunk = min(CHUNK, data_rows)
    chunks = data_rows // chunk
    blocks = chunk // (2 * out_rows)
    own_chunk = lax.div(chip, blocks)

    def copy_sibling(turn):
        return remote(
            product.at[turn, 1 - core], sibling_in.at[turn], sib_send.at[turn], sib_recv.at[turn], (dp, sibling)
        )

    def copy_part(to):
        return remote(part.at[to], parts_in.at[chip], rs_send.at[0], rs_recv.at[0], (dp, 2 * to + core))

    def chunk_of(turn):
        return lax.rem(own_chunk + 1 + turn, chunks)

    def multiply(turn):
        here = chunk_of(turn)
        rows = sens[pl.ds(here * (chunk // GROUP), chunk // GROUP)].reshape(chunk, cells)
        result = lax.dot_general(rows, panel[...], (((1,), (1,)), ((), ())), preferred_element_type=f32)
        result = result.reshape(blocks, 2, out_rows, PANEL)
        for half in range(2):
            product[turn, half] = result[:, half]
        copy_sibling(turn).start()

    def send_parts(turn):
        here = chunk_of(turn)
        copy_sibling(turn).wait_recv()
        part[pl.ds(here * blocks, blocks)] = (product[turn, core] + sibling_in[turn]).astype(bf16)
        for i in range(blocks):
            to = here * blocks + i

            @pl.when(to != chip)
            def _(to=to):
                copy_part(to).start()

    for turn in range(chunks):
        multiply(turn)
        if turn > 0:
            send_parts(turn - 1)
    send_parts(chunks - 1)
    parts_in[chip] = part[chip]

    class_after.wait_send()
    class_before.wait_send()
    halo_after.wait_send()
    halo_before.wait_send()

    @pl.when(x < 2)
    def _():
        for copy in (copy_far, copy_in, copy_mate, copy_out, copy_in_late, copy_chosen):
            copy.wait_send()

    @pl.when(x >= 2)
    def _():
        copy_on.wait_send()

    for dj in (1, 2, 3):
        copy_y(dj).wait_send()
    for copy in over_y + to_right + to_left + relays:
        copy.wait_send()
    for turn in range(chunks):
        copy_sibling(turn).wait_send()

    others = remote(
        part.at[0 : chips - 1], parts_in.at[0 : chips - 1], rs_send.at[0], rs_recv.at[0], (dp, sibling)
    )
    others.wait_send()
    others.wait_recv()

    total = jnp.zeros(out_ref.shape, f32)
    for i in range(chips):
        total = total + parts_in[i].astype(f32)
    total = total * (1.0 / math.sqrt(layers * plane))
    col = lax.broadcasted_iota(jnp.int32, out_ref.shape, 1)
    place = lax.div(lax.rem(col, GROUP), PIECE)
    total = jnp.where(
        place == 2, pltpu.roll(total, PANEL - PIECE, 1), jnp.where(place == 3, pltpu.roll(total, PIECE, 1), total)
    )
    shift = PIECE * yh
    total = jnp.where(
        lax.rem(col, GROUP) >= shift,
        pltpu.roll(total, shift, 1),
        pltpu.roll(total, shift + PANEL - GROUP, 1),
    )
    base = dp * data_rows + me * out_rows
    row = base + lax.broadcasted_iota(jnp.int32, out_ref.shape, 0)
    out_ref[...] = jnp.where(row >= start * PANEL + col, total, 0.0)


def body(sensitivity, panel_index, cell_class, tear_layer, coef_table):
    rows, cells = sensitivity.shape
    depth, plane = cell_class.shape
    slabs = lax.axis_size("slab")
    out_rows = rows // slabs
    groups = rows // GROUP
    chips = slabs // 2
    chunks = max(1, rows // CHUNK)
    bf16 = jnp.bfloat16
    dma = pltpu.SemaphoreType.DMA
    sweeps = coef_table.shape[0]
    ext = -(-(depth + 4) // 8) * 8
    return pl.pallas_call(
        functools.partial(kernel, slabs),
        out_shape=jax.ShapeDtypeStruct((out_rows, PANEL), jnp.float32),
        in_specs=[pl.BlockSpec(memory_space=pltpu.HBM)] * 5,
        out_specs=pl.BlockSpec(memory_space=pltpu.VMEM),
        scratch_shapes=[
            pltpu.SMEM(panel_index.shape, jnp.int32),
            pltpu.SMEM(coef_table.shape, jnp.float32),
            pltpu.VMEM((depth, plane), jnp.int32),
            pltpu.VMEM((1, plane), jnp.int32),
            pltpu.VMEM((groups, GROUP, cells), bf16),
            pltpu.VMEM((4, 4, PIECE, cells), bf16),
            pltpu.VMEM((2, 2, PIECE, cells), bf16),
            pltpu.VMEM((2, 2, PIECE, cells), bf16),
            pltpu.VMEM((2, PIECE, cells), bf16),
            pltpu.VMEM((2, 2, PIECE, cells), bf16),
            pltpu.VMEM((2, PIECE, cells), bf16),
            pltpu.VMEM((4, PIECE, cells), bf16),
            pltpu.VMEM((4, PIECE, cells), bf16),
            pltpu.VMEM((PIECE, cells), bf16),
            pltpu.VMEM((2, PIECE, cells), bf16),
            pltpu.VMEM((2, depth, plane), jnp.int32),
            pltpu.VMEM((ext, plane), jnp.int32),
            pltpu.VMEM((sweeps, 4, ext, plane), jnp.float32),
            pltpu.VMEM((sweeps, 3 * depth, PIECE, plane), jnp.float32),
            pltpu.VMEM((4, 4, PIECE, cells), bf16),
            pltpu.VMEM((PANEL, cells), bf16),
            pltpu.VMEM((chunks, 2, rows // chunks // (2 * out_rows), out_rows, PANEL), jnp.float32),
            pltpu.VMEM((chunks, rows // chunks // (2 * out_rows), out_rows, PANEL), jnp.float32),
            pltpu.VMEM((chips, out_rows, PANEL), bf16),
            pltpu.VMEM((chips, out_rows, PANEL), bf16),
            dma((5,)),
            dma((2,)),
            dma((2,)),
            dma((6,)),
            dma((6,)),
            dma((4,)),
            dma((4,)),
            dma((2,)),
            dma((2,)),
            dma((4,)),
            dma((4,)),
            dma((9,)),
            dma((9,)),
            dma((chunks,)),
            dma((chunks,)),
            dma((1,)),
            dma((1,)),
        ],
        compiler_params=pltpu.CompilerParams(
            collective_id=0, has_side_effects=True, vmem_limit_bytes=VMEM_LIMIT
        ),
        cost_estimate=pl.CostEstimate(
            flops=2 * rows * cells * PANEL, bytes_accessed=2 * rows * cells, transcendentals=0
        ),
        name="panel",
    )(
        panel_index,
        coef_table,
        sensitivity.reshape(groups, GROUP, cells),
        cell_class,
        tear_layer.reshape(1, plane),
    )


def solution(mesh):
    return jax.shard_map(
        body,
        mesh=mesh,
        in_specs=(P("dp", "slab"), P(), P("slab", None), P(), P()),
        out_specs=P(("dp", "slab"), None),
        check_vma=False,
    )
```

```python
import functools
import math

import jax
import jax.numpy as jnp
from jax import lax
from jax.experimental import pallas as pl
from jax.experimental.pallas import tpu as pltpu
from jax.sharding import PartitionSpec as P

WIDTH_Y = 32
PANEL = 128
GROUP = 32
HALF = 16
PIECE = 8
CHUNK = 384
VMEM_LIMIT = 63 * 1024 * 1024


def kernel(
    slabs,
    panel_hbm,
    table_hbm,
    sens_hbm,
    class_hbm,
    tear_hbm,
    out_ref,
    panel_ref,
    table_ref,
    class_ref,
    tear_ref,
    sens,
    send1,
    recv_early,
    recv_late,
    fwd1,
    pair1,
    chosen1,
    send2,
    recv2,
    raw,
    halo,
    class_halo,
    class_ext,
    coef,
    field,
    gath,
    panel,
    product,
    sibling_in,
    part,
    parts_in,
    load_sem,
    class_send,
    class_recv,
    s1_send,
    s1_recv,
    s2_send,
    s2_recv,
    h_send,
    h_recv,
    g5_send,
    g5_recv,
    g6_send,
    g6_recv,
    sib_send,
    sib_recv,
    rs_send,
    rs_recv,
):
    f32 = jnp.float32
    bf16 = jnp.bfloat16
    dp = lax.axis_index("dp")
    me = lax.axis_index("slab")
    x = lax.div(dp, 4)
    yh = lax.rem(dp, 4)
    groups, _, cells = sens.shape
    chips = slabs // 2
    core = lax.rem(me, 2)
    chip = lax.div(me, 2)
    sibling = me + 1 - 2 * core
    depth, plane = class_ref.shape
    layers = depth * slabs
    out_rows = out_ref.shape[0]
    panels_dev = groups * GROUP // PANEL
    right = lax.rem(x + 1, 4)
    left = lax.rem(x + 3, 4)
    before = lax.rem(me + slabs - 1, slabs)
    after = lax.rem(me + 1, slabs)

    def at(x_to, y_to, slab_to):
        return (x_to * 4 + y_to, slab_to)

    def remote(src, dst, send_sem, recv_sem, target):
        return pltpu.make_async_remote_copy(
            src_ref=src,
            dst_ref=dst,
            send_sem=send_sem,
            recv_sem=recv_sem,
            device_id=target,
            device_id_type=pl.DeviceIdType.MESH,
        )

    loads = 4

    def load(i):
        part_of = pl.ds(i * (groups // loads), groups // loads)
        return pltpu.make_async_copy(sens_hbm.at[part_of], sens.at[part_of], load_sem.at[0])

    small = [
        pltpu.make_async_copy(source, target, load_sem.at[1 + i])
        for i, (source, target) in enumerate(
            [(class_hbm, class_ref), (tear_hbm, tear_ref), (table_hbm, table_ref), (panel_hbm, panel_ref)]
        )
    ]
    for copy in small:
        copy.start()
    for i in range(loads):
        load(i).start()

    barrier = pltpu.get_barrier_semaphore()

    def greet(target):
        pl.semaphore_signal(
            barrier, inc=1, device_id=target, device_id_type=pl.DeviceIdType.MESH
        )

    for d in sorted(range(1, chips), key=lambda d: -min(d, chips - d)):
        greet((dp, lax.rem(me + 2 * d, slabs)))

    for dj in (2, 1, 3):
        greet(at(x, lax.rem(yh + dj, 4), me))
    greet((dp, before))
    greet((dp, after))
    greet(at(right, yh, me))
    greet(at(left, yh, me))
    greet(at(lax.rem(x + 2, 4), yh, me))

    for copy in small:
        copy.wait()
    pltpu.make_async_copy(sens_hbm, sens, load_sem.at[0]).wait()

    start = panel_ref[0]
    owner = lax.div(start, panels_dev)
    x_owner = lax.div(owner, 4)
    y_owner = lax.rem(owner, 4)
    first_group = lax.rem(start, panels_dev) * 4

    @pl.when(x < 2)
    def _():
        for q in range(4):
            send1[q] = sens[first_group + q].reshape(2, HALF, cells)

    pl.semaphore_wait(barrier, 8 + chips - 1)

    def early(q):
        return send1.at[q, 0]

    def late(q):
        return send1.at[q, 1]

    mate = at(1 - x, yh, me)
    outer = at(3 - x, yh, me)
    copy_far = remote(early(x + 2), fwd1, s1_send.at[0], s1_recv.at[0], outer)
    copy_in = remote(early(1 - x), recv_early.at[x], s1_send.at[1], s1_recv.at[1], mate)
    copy_mate = remote(late(x + 2), pair1.at[x], s1_send.at[2], s1_recv.at[2], mate)
    copy_out = remote(early(3 - x), recv_early.at[x], s1_send.at[3], s1_recv.at[3], outer)
    copy_in_late = remote(late(1 - x), recv_late.at[x], s1_send.at[4], s1_recv.at[4], mate)
    copy_chosen = remote(chosen1, recv_late.at[0], s1_send.at[5], s1_recv.at[5], outer)
    copy_on = remote(fwd1, recv_early.at[3 - x], s1_send.at[1], s1_recv.at[1], at(5 - x, yh, me))

    def arrived(slot, to):
        remote(to, to, s1_send.at[slot], s1_recv.at[slot], at(right, yh, me)).wait_recv()

    @pl.when(x < 2)
    def _():
        for copy in (copy_far, copy_mate, copy_in, copy_out, copy_in_late):
            copy.start()
        recv_early[x] = send1[x, 0]
        recv_late[x] = send1[x, 1]
        pair1[x] = send1[3 - x, 1]

    class_after = remote(class_ref, class_halo.at[0], class_send.at[0], class_recv.at[0], (dp, after))
    class_before = remote(class_ref, class_halo.at[1], class_send.at[1], class_recv.at[1], (dp, before))
    class_after.start()
    class_before.start()

    class_after.wait_recv()
    class_before.wait_recv()
    class_ext[0:2] = class_halo[0, depth - 2 : depth]
    class_ext[2 : 2 + depth] = class_ref[...]
    class_ext[2 + depth : 4 + depth] = class_halo[1, 0:2]
    class_ext[4 + depth :] = jnp.zeros_like(class_ext[4 + depth :])
    classes = class_ext[...]
    layer = me * depth - 2 + lax.broadcasted_iota(jnp.int32, classes.shape, 0)
    valid = (layer >= 0) & (layer < layers)
    tear = jnp.broadcast_to(tear_ref[...], classes.shape)
    open_up = tear != layer
    open_down = tear != layer + 1
    for k in range(table_ref.shape[0]):
        a = jnp.zeros(classes.shape, f32)
        b = jnp.zeros(classes.shape, f32)
        for level in range(table_ref.shape[2]):
            a = jnp.where(classes == level, table_ref[k, 0, level], a)
            b = jnp.where(classes == level, table_ref[k, 1, level], b)
        a = jnp.where(valid, a, 0.0)
        b = jnp.where(valid, 4.0 * b, 0.0)
        up = jnp.where(open_up, b, 0.0)
        down = jnp.where(open_down, b, 0.0)
        coef[k, 0] = 1.0 - 4.0 * a - up - down
        coef[k, 1] = a
        coef[k, 2] = up
        coef[k, 3] = down

    def copy_y(j):
        return remote(send2.at[j], recv2.at[yh], s2_send.at[j], s2_recv.at[yh], at(x, j, me))

    def wait_y(dj):
        j = lax.rem(yh + dj, 4)
        remote(send2.at[j], recv2.at[j], s2_send.at[j], s2_recv.at[j], at(x, j, me)).wait_recv()

    def scatter_y(rows, first):
        pieces = rows.astype(f32).reshape(2, PIECE, cells).astype(bf16)
        for j in (first, first + 1):

            @pl.when(yh == j)
            def _(j=j):
                recv2[yh] = pieces[j - first]

            @pl.when(yh != j)
            def _(j=j):
                send2[j] = pieces[j - first]
                copy_y(j).start()

    @pl.when(x >= 2)
    def _():
        arrived(0, fwd1)
        copy_on.start()
        arrived(3, recv_early.at[3 - x])

    arrived(1, recv_early.at[jnp.where(x < 2, 1 - x, x - 2)])
    scatter_y(recv_early[x_owner], 0)

    @pl.when(x < 2)
    def _():
        arrived(2, pair1.at[1 - x])
        chosen1[...] = pair1[x_owner]
        copy_chosen.start()
        arrived(4, recv_late.at[1 - x])

    @pl.when(x >= 2)
    def _():
        arrived(5, recv_late.at[0])

    scatter_y(recv_late[jnp.where(x < 2, x_owner, 0)], 2)
    for dj in (2, 1, 3):
        wait_y(dj)

    raw[...] = recv2[y_owner]
    halo_after = remote(raw, halo.at[0], h_send.at[0], h_recv.at[0], (dp, after))
    halo_before = remote(raw, halo.at[1], h_send.at[1], h_recv.at[1], (dp, before))
    halo_after.start()
    halo_before.start()

    for g in range(depth):
        field[0, depth + g] = raw[:, g * plane : (g + 1) * plane].astype(f32)
    position = lax.broadcasted_iota(jnp.int32, (PIECE, plane), 1)
    column = lax.rem(position, WIDTH_Y)
    sweeps = table_ref.shape[0]

    def smooth(k, l):
        u = field[k, l]
        north = jnp.where(position >= WIDTH_Y, pltpu.roll(u, WIDTH_Y, 1), 0.0)
        south = jnp.where(position < plane - WIDTH_Y, pltpu.roll(u, plane - WIDTH_Y, 1), 0.0)
        west = jnp.where(column > 0, pltpu.roll(u, 1, 1), 0.0)
        east = jnp.where(column < WIDTH_Y - 1, pltpu.roll(u, plane - 1, 1), 0.0)
        e = l - depth + 2
        updated = (
            coef[k, 0, e : e + 1] * u
            + coef[k, 1, e : e + 1] * ((north + south) + (west + east))
            + coef[k, 2, e : e + 1] * field[k, l - 1]
            + coef[k, 3, e : e + 1] * field[k, l + 1]
        )
        if k + 1 < sweeps:
            field[k + 1, l] = updated
        else:
            g = l - depth
            gath[x, 0, :, g * plane : (g + 1) * plane] = updated.astype(bf16)

    def copy_g5(place, dj, lands):
        target = at(x, lax.rem(yh + dj, 4), me)
        return remote(gath.at[x, 0], gath.at[x, lands], g5_send.at[place], g5_recv.at[lands], target)

    over_y = [copy_g5(3, 2, 3), copy_g5(1, 1, 2), copy_g5(2, 3, 1)]

    def wait_g5(place):
        remote(gath.at[x, 0], gath.at[x, place], g5_send.at[place], g5_recv.at[place], at(right, yh, me)).wait_recv()

    def copy_g6(way, source, first, last, slot):
        part_of = gath.at[source, first:last]
        return remote(part_of, part_of, g6_send.at[slot], g6_recv.at[slot], at(way, yh, me))

    rounds = [(0, 1), (1, 3), (3, 4)]
    far = lax.rem(x + 2, 4)
    to_right = [copy_g6(right, x, *span, i) for i, span in enumerate(rounds)]
    to_left = [copy_g6(left, x, *span, 3 + i) for i, span in enumerate(rounds)]
    from_left = [copy_g6(right, left, *span, i) for i, span in enumerate(rounds)]
    from_right = [copy_g6(left, right, *span, 3 + i) for i, span in enumerate(rounds)]
    relays = [copy_g6(right, left, 0, 2, 6), copy_g6(left, right, 2, 3, 7)]
    to_far = copy_g6(far, x, 3, 4, 8)
    relayed = [copy_g6(right, far, 0, 2, 6), copy_g6(left, far, 2, 3, 7), copy_g6(far, far, 3, 4, 8)]

    inner = [(0, l) for l in range(depth + 1, 2 * depth - 1)]
    done = set(inner)
    for k, l in inner:
        smooth(k, l)

    halo_after.wait_recv()
    halo_before.wait_recv()
    has_before = jnp.where(me > 0, 1.0, 0.0).astype(f32)
    has_after = jnp.where(me < slabs - 1, 1.0, 0.0).astype(f32)
    for g in range(depth):
        cut = slice(g * plane, (g + 1) * plane)
        field[0, g] = halo[0, :, cut].astype(f32) * has_before
        field[0, 2 * depth + g] = halo[1, :, cut].astype(f32) * has_after

    def smooth_all(k, l):
        if k < 0 or (k, l) in done:
            return
        for near in (l - 1, l, l + 1):
            smooth_all(k - 1, near)
        smooth(k, l)
        done.add((k, l))

    for t in range(depth):
        smooth_all(sweeps - 1, depth + t)
    for copy in over_y + [to_right[0], to_left[0]]:
        copy.start()

    def into_panel(source):
        rows = gath[source].astype(f32).reshape(GROUP, cells).astype(bf16)
        panel[pl.ds(pl.multiple_of(source * GROUP, GROUP), GROUP)] = rows

    wait_g5(1)
    wait_g5(2)
    to_right[1].start()
    to_left[1].start()
    wait_g5(3)
    to_far.start()
    to_right[2].start()
    to_left[2].start()
    from_left[0].wait_recv()
    from_left[1].wait_recv()
    relays[0].start()
    from_right[0].wait_recv()
    from_right[1].wait_recv()
    relays[1].start()
    into_panel(x)
    from_right[2].wait_recv()
    into_panel(right)
    from_left[2].wait_recv()
    into_panel(left)
    for copy in relayed:
        copy.wait_recv()
    into_panel(far)

    data_rows = groups * GROUP
    chunk = min(CHUNK, data_rows)
    chunks = data_rows // chunk
    blocks = chunk // (2 * out_rows)
    own_chunk = lax.div(chip, blocks)

    def copy_sibling(turn):
        return remote(
            product.at[turn, 1 - core], sibling_in.at[turn], sib_send.at[turn], sib_recv.at[turn], (dp, sibling)
        )

    def copy_part(to):
        return remote(part.at[to], parts_in.at[chip], rs_send.at[0], rs_recv.at[0], (dp, 2 * to + core))

    def chunk_of(turn):
        return lax.rem(own_chunk + 1 + turn, chunks)

    def multiply(turn):
        here = chunk_of(turn)
        rows = sens[pl.ds(here * (chunk // GROUP), chunk // GROUP)].reshape(chunk, cells)
        result = lax.dot_general(rows, panel[...], (((1,), (1,)), ((), ())), preferred_element_type=f32)
        result = result.reshape(blocks, 2, out_rows, PANEL)
        for half in range(2):
            product[turn, half] = result[:, half]
        copy_sibling(turn).start()

    def send_parts(turn):
        here = chunk_of(turn)
        copy_sibling(turn).wait_recv()
        part[pl.ds(here * blocks, blocks)] = (product[turn, core] + sibling_in[turn]).astype(bf16)
        for i in range(blocks):
            to = here * blocks + i

            @pl.when(to != chip)
            def _(to=to):
                copy_part(to).start()

    for turn in range(chunks):
        multiply(turn)
        if turn > 0:
            send_parts(turn - 1)
    send_parts(chunks - 1)
    parts_in[chip] = part[chip]

    class_after.wait_send()
    class_before.wait_send()
    halo_after.wait_send()
    halo_before.wait_send()

    @pl.when(x < 2)
    def _():
        for copy in (copy_far, copy_in, copy_mate, copy_out, copy_in_late, copy_chosen):
            copy.wait_send()

    @pl.when(x >= 2)
    def _():
        copy_on.wait_send()

    for j in range(4):

        @pl.when(yh != j)
        def _(j=j):
            copy_y(j).wait_send()

    for copy in over_y + to_right + to_left + relays + [to_far]:
        copy.wait_send()
    for turn in range(chunks):
        copy_sibling(turn).wait_send()

    others = remote(
        part.at[0 : chips - 1], parts_in.at[0 : chips - 1], rs_send.at[0], rs_recv.at[0], (dp, sibling)
    )
    others.wait_send()
    others.wait_recv()

    total = jnp.zeros(out_ref.shape, f32)
    for i in range(chips):
        total = total + parts_in[i].astype(f32)
    total = total * (1.0 / math.sqrt(layers * plane))
    col = lax.broadcasted_iota(jnp.int32, out_ref.shape, 1)
    place = lax.div(lax.rem(col, GROUP), PIECE)
    total = jnp.where(
        place == 2, pltpu.roll(total, PANEL - PIECE, 1), jnp.where(place == 3, pltpu.roll(total, PIECE, 1), total)
    )
    shift = PIECE * yh
    total = jnp.where(
        lax.rem(col, GROUP) >= shift,
        pltpu.roll(total, shift, 1),
        pltpu.roll(total, shift + PANEL - GROUP, 1),
    )
    base = dp * data_rows + me * out_rows
    row = base + lax.broadcasted_iota(jnp.int32, out_ref.shape, 0)
    out_ref[...] = jnp.where(row >= start * PANEL + col, total, 0.0)


def body(sensitivity, panel_index, cell_class, tear_layer, coef_table):
    rows, cells = sensitivity.shape
    depth, plane = cell_class.shape
    slabs = lax.axis_size("slab")
    out_rows = rows // slabs
    groups = rows // GROUP
    chips = slabs // 2
    chunks = max(1, rows // CHUNK)
    bf16 = jnp.bfloat16
    dma = pltpu.SemaphoreType.DMA
    sweeps = coef_table.shape[0]
    ext = -(-(depth + 4) // 8) * 8
    return pl.pallas_call(
        functools.partial(kernel, slabs),
        out_shape=jax.ShapeDtypeStruct((out_rows, PANEL), jnp.float32),
        in_specs=[pl.BlockSpec(memory_space=pltpu.HBM)] * 5,
        out_specs=pl.BlockSpec(memory_space=pltpu.VMEM),
        scratch_shapes=[
            pltpu.SMEM(panel_index.shape, jnp.int32),
            pltpu.SMEM(coef_table.shape, jnp.float32),
            pltpu.VMEM((depth, plane), jnp.int32),
            pltpu.VMEM((1, plane), jnp.int32),
            pltpu.VMEM((groups, GROUP, cells), bf16),
            pltpu.VMEM((4, 2, HALF, cells), bf16),
            pltpu.VMEM((2, HALF, cells), bf16),
            pltpu.VMEM((2, HALF, cells), bf16),
            pltpu.VMEM((HALF, cells), bf16),
            pltpu.VMEM((2, HALF, cells), bf16),
            pltpu.VMEM((HALF, cells), bf16),
            pltpu.VMEM((4, PIECE, cells), bf16),
            pltpu.VMEM((4, PIECE, cells), bf16),
            pltpu.VMEM((PIECE, cells), bf16),
            pltpu.VMEM((2, PIECE, cells), bf16),
            pltpu.VMEM((2, depth, plane), jnp.int32),
            pltpu.VMEM((ext, plane), jnp.int32),
            pltpu.VMEM((sweeps, 4, ext, plane), jnp.float32),
            pltpu.VMEM((sweeps, 3 * depth, PIECE, plane), jnp.float32),
            pltpu.VMEM((4, 4, PIECE, cells), bf16),
            pltpu.VMEM((PANEL, cells), bf16),
            pltpu.VMEM((chunks, 2, rows // chunks // (2 * out_rows), out_rows, PANEL), jnp.float32),
            pltpu.VMEM((chunks, rows // chunks // (2 * out_rows), out_rows, PANEL), jnp.float32),
            pltpu.VMEM((chips, out_rows, PANEL), bf16),
            pltpu.VMEM((chips, out_rows, PANEL), bf16),
            dma((5,)),
            dma((2,)),
            dma((2,)),
            dma((6,)),
            dma((6,)),
            dma((4,)),
            dma((4,)),
            dma((2,)),
            dma((2,)),
            dma((4,)),
            dma((4,)),
            dma((9,)),
            dma((9,)),
            dma((chunks,)),
            dma((chunks,)),
            dma((1,)),
            dma((1,)),
        ],
        compiler_params=pltpu.CompilerParams(
            collective_id=0, has_side_effects=True, vmem_limit_bytes=VMEM_LIMIT
        ),
        cost_estimate=pl.CostEstimate(
            flops=2 * rows * cells * PANEL, bytes_accessed=2 * rows * cells, transcendentals=0
        ),
        name="panel",
    )(
        panel_index,
        coef_table,
        sensitivity.reshape(groups, GROUP, cells),
        cell_class,
        tear_layer.reshape(1, plane),
    )


def solution(mesh):
    return jax.shard_map(
        body,
        mesh=mesh,
        in_specs=(P("dp", "slab"), P(), P("slab", None), P(), P()),
        out_specs=P(("dp", "slab"), None),
        check_vma=False,
    )
```

```python
import functools
import math

import jax
import jax.numpy as jnp
from jax import lax
from jax.experimental import pallas as pl
from jax.experimental.pallas import tpu as pltpu
from jax.sharding import PartitionSpec as P

WIDTH_Y = 32
PANEL = 128
GROUP = 32
HALF = 16
PIECE = 8
CHUNK = 384
VMEM_LIMIT = 63 * 1024 * 1024


def kernel(
    slabs,
    panel_hbm,
    table_hbm,
    sens_hbm,
    class_hbm,
    tear_hbm,
    out_ref,
    panel_ref,
    table_ref,
    class_ref,
    tear_ref,
    sens,
    send1,
    recv_early,
    recv_late,
    fwd1,
    pair1,
    chosen1,
    send2,
    recv2,
    raw,
    halo,
    class_halo,
    class_ext,
    coef,
    field,
    gath,
    panel,
    product,
    sibling_in,
    part,
    load_sem,
    class_send,
    class_recv,
    s1_send,
    s1_recv,
    s2_send,
    s2_recv,
    h_send,
    h_recv,
    g5_send,
    g5_recv,
    g6_send,
    g6_recv,
    sib_send,
    sib_recv,
    rs_send,
    rs_recv,
):
    f32 = jnp.float32
    bf16 = jnp.bfloat16
    dp = lax.axis_index("dp")
    me = lax.axis_index("slab")
    x = lax.div(dp, 4)
    yh = lax.rem(dp, 4)
    groups, _, cells = sens.shape
    chips = slabs // 2
    core = lax.rem(me, 2)
    chip = lax.div(me, 2)
    sibling = me + 1 - 2 * core
    depth, plane = class_ref.shape
    layers = depth * slabs
    out_rows = out_ref.shape[1]
    panels_dev = groups * GROUP // PANEL
    right = lax.rem(x + 1, 4)
    left = lax.rem(x + 3, 4)
    before = lax.rem(me + slabs - 1, slabs)
    after = lax.rem(me + 1, slabs)

    def at(x_to, y_to, slab_to):
        return (x_to * 4 + y_to, slab_to)

    def remote(src, dst, send_sem, recv_sem, target):
        return pltpu.make_async_remote_copy(
            src_ref=src,
            dst_ref=dst,
            send_sem=send_sem,
            recv_sem=recv_sem,
            device_id=target,
            device_id_type=pl.DeviceIdType.MESH,
        )

    loads = 4

    def load(i):
        part_of = pl.ds(i * (groups // loads), groups // loads)
        return pltpu.make_async_copy(sens_hbm.at[part_of], sens.at[part_of], load_sem.at[0])

    small = [
        pltpu.make_async_copy(source, target, load_sem.at[1 + i])
        for i, (source, target) in enumerate(
            [(class_hbm, class_ref), (tear_hbm, tear_ref), (table_hbm, table_ref), (panel_hbm, panel_ref)]
        )
    ]
    for copy in small:
        copy.start()
    for i in range(loads):
        load(i).start()

    barrier = pltpu.get_barrier_semaphore()

    def greet(target):
        pl.semaphore_signal(
            barrier, inc=1, device_id=target, device_id_type=pl.DeviceIdType.MESH
        )

    for d in sorted(range(1, chips), key=lambda d: -min(d, chips - d)):
        greet((dp, lax.rem(me + 2 * d, slabs)))

    for dj in (2, 1, 3):
        greet(at(x, lax.rem(yh + dj, 4), me))
    greet((dp, before))
    greet((dp, after))
    greet(at(right, yh, me))
    greet(at(left, yh, me))

    for copy in small:
        copy.wait()
    pltpu.make_async_copy(sens_hbm, sens, load_sem.at[0]).wait()

    start = panel_ref[0]
    owner = lax.div(start, panels_dev)
    x_owner = lax.div(owner, 4)
    y_owner = lax.rem(owner, 4)
    first_group = lax.rem(start, panels_dev) * 4

    @pl.when(x < 2)
    def _():
        for q in range(4):
            send1[q] = sens[first_group + q].reshape(2, HALF, cells)

    pl.semaphore_wait(barrier, 7 + chips - 1)

    def early(q):
        return send1.at[q, 0]

    def late(q):
        return send1.at[q, 1]

    mate = at(1 - x, yh, me)
    outer = at(3 - x, yh, me)
    copy_far = remote(early(x + 2), fwd1, s1_send.at[0], s1_recv.at[0], outer)
    copy_in = remote(early(1 - x), recv_early.at[x], s1_send.at[1], s1_recv.at[1], mate)
    copy_mate = remote(late(x + 2), pair1.at[x], s1_send.at[2], s1_recv.at[2], mate)
    copy_out = remote(early(3 - x), recv_early.at[x], s1_send.at[3], s1_recv.at[3], outer)
    copy_in_late = remote(late(1 - x), recv_late.at[x], s1_send.at[4], s1_recv.at[4], mate)
    copy_chosen = remote(chosen1, recv_late.at[0], s1_send.at[5], s1_recv.at[5], outer)
    copy_on = remote(fwd1, recv_early.at[3 - x], s1_send.at[1], s1_recv.at[1], at(5 - x, yh, me))

    def arrived(slot, to):
        remote(to, to, s1_send.at[slot], s1_recv.at[slot], at(right, yh, me)).wait_recv()

    @pl.when(x < 2)
    def _():
        for copy in (copy_far, copy_mate, copy_in, copy_out, copy_in_late):
            copy.start()
        recv_early[x] = send1[x, 0]
        recv_late[x] = send1[x, 1]
        pair1[x] = send1[3 - x, 1]

    class_after = remote(class_ref, class_halo.at[0], class_send.at[0], class_recv.at[0], (dp, after))
    class_before = remote(class_ref, class_halo.at[1], class_send.at[1], class_recv.at[1], (dp, before))
    class_after.start()
    class_before.start()

    class_after.wait_recv()
    class_before.wait_recv()
    class_ext[0:2] = class_halo[0, depth - 2 : depth]
    class_ext[2 : 2 + depth] = class_ref[...]
    class_ext[2 + depth : 4 + depth] = class_halo[1, 0:2]
    class_ext[4 + depth :] = jnp.zeros_like(class_ext[4 + depth :])
    classes = class_ext[...]
    layer = me * depth - 2 + lax.broadcasted_iota(jnp.int32, classes.shape, 0)
    valid = (layer >= 0) & (layer < layers)
    tear = jnp.broadcast_to(tear_ref[...], classes.shape)
    open_up = tear != layer
    open_down = tear != layer + 1
    for k in range(table_ref.shape[0]):
        a = jnp.zeros(classes.shape, f32)
        b = jnp.zeros(classes.shape, f32)
        for level in range(table_ref.shape[2]):
            a = jnp.where(classes == level, table_ref[k, 0, level], a)
            b = jnp.where(classes == level, table_ref[k, 1, level], b)
        a = jnp.where(valid, a, 0.0)
        b = jnp.where(valid, 4.0 * b, 0.0)
        up = jnp.where(open_up, b, 0.0)
        down = jnp.where(open_down, b, 0.0)
        coef[k, 0] = 1.0 - 4.0 * a - up - down
        coef[k, 1] = a
        coef[k, 2] = up
        coef[k, 3] = down

    def copy_y(j):
        return remote(send2.at[j], recv2.at[yh], s2_send.at[j], s2_recv.at[yh], at(x, j, me))

    def wait_y(dj):
        j = lax.rem(yh + dj, 4)
        remote(send2.at[j], recv2.at[j], s2_send.at[j], s2_recv.at[j], at(x, j, me)).wait_recv()

    def scatter_y(rows, first):
        pieces = rows.astype(f32).reshape(2, PIECE, cells).astype(bf16)
        for j in (first, first + 1):

            @pl.when(yh == j)
            def _(j=j):
                recv2[yh] = pieces[j - first]

            @pl.when(yh != j)
            def _(j=j):
                send2[j] = pieces[j - first]
                copy_y(j).start()

    @pl.when(x >= 2)
    def _():
        arrived(0, fwd1)
        copy_on.start()
        arrived(3, recv_early.at[3 - x])

    arrived(1, recv_early.at[jnp.where(x < 2, 1 - x, x - 2)])
    halo_after = remote(raw, halo.at[0], h_send.at[0], h_recv.at[0], (dp, after))
    halo_before = remote(raw, halo.at[1], h_send.at[1], h_recv.at[1], (dp, before))

    def start_halo():
        for dj in (1, 2, 3):
            wait_y(dj)
        raw[...] = recv2[y_owner]
        halo_after.start()
        halo_before.start()

    scatter_y(recv_early[x_owner], 0)

    @pl.when(yh < 2)
    def _():
        start_halo()


    @pl.when(x < 2)
    def _():
        arrived(2, pair1.at[1 - x])
        chosen1[...] = pair1[x_owner]
        copy_chosen.start()
        arrived(4, recv_late.at[1 - x])

    @pl.when(x >= 2)
    def _():
        arrived(5, recv_late.at[0])

    scatter_y(recv_late[jnp.where(x < 2, x_owner, 0)], 2)
    @pl.when(yh >= 2)
    def _():
        start_halo()

    for g in range(depth):
        field[0, depth + g] = raw[:, g * plane : (g + 1) * plane].astype(f32)
    position = lax.broadcasted_iota(jnp.int32, (PIECE, plane), 1)
    column = lax.rem(position, WIDTH_Y)
    sweeps = table_ref.shape[0]

    def smooth(k, l):
        u = field[k, l]
        north = jnp.where(position >= WIDTH_Y, pltpu.roll(u, WIDTH_Y, 1), 0.0)
        south = jnp.where(position < plane - WIDTH_Y, pltpu.roll(u, plane - WIDTH_Y, 1), 0.0)
        west = jnp.where(column > 0, pltpu.roll(u, 1, 1), 0.0)
        east = jnp.where(column < WIDTH_Y - 1, pltpu.roll(u, plane - 1, 1), 0.0)
        e = l - depth + 2
        updated = (
            coef[k, 0, e : e + 1] * u
            + coef[k, 1, e : e + 1] * ((north + south) + (west + east))
            + coef[k, 2, e : e + 1] * field[k, l - 1]
            + coef[k, 3, e : e + 1] * field[k, l + 1]
        )
        if k + 1 < sweeps:
            field[k + 1, l] = updated
        else:
            g = l - depth
            gath[x, yh, :, g * plane : (g + 1) * plane] = updated.astype(bf16)

    def copy_g5(dj):
        own = gath.at[x, yh]
        return remote(own, own, g5_send.at[dj], g5_recv.at[yh], at(x, lax.rem(yh + dj, 4), me))

    over_y = [copy_g5(dj) for dj in (2, 1, 3)]

    def wait_g5(j):
        @pl.when(yh != j)
        def _():
            piece = gath.at[x, j]
            remote(piece, piece, g5_send.at[0], g5_recv.at[j], at(right, yh, me)).wait_recv()

    def copy_g6(way, source, first, last, slot):
        part_of = gath.at[source, first:last]
        return remote(part_of, part_of, g6_send.at[slot], g6_recv.at[slot], at(way, yh, me))

    far = lax.rem(x + 2, 4)

    def gather_half(half):
        first = 2 * half
        wait_g5(first)
        wait_g5(first + 1)
        slot = 4 * half
        sent = [
            copy_g6(right, x, first, first + 2, slot),
            copy_g6(left, x, first, first + 2, slot + 1),
            copy_g6(right, left, first, first + 1, slot + 2),
            copy_g6(left, right, first + 1, first + 2, slot + 3),
        ]
        sent[0].start()
        sent[1].start()
        into_panel(x, half)
        copy_g6(right, left, first, first + 2, slot).wait_recv()
        sent[2].start()
        copy_g6(left, right, first, first + 2, slot + 1).wait_recv()
        sent[3].start()
        into_panel(left, half)
        into_panel(right, half)
        return sent

    def gather_far(half):
        first = 2 * half
        slot = 4 * half
        copy_g6(right, far, first, first + 1, slot + 2).wait_recv()
        copy_g6(left, far, first + 1, first + 2, slot + 3).wait_recv()
        into_panel(far, half)

    def into_panel(source, half):
        rows = gath[source, 2 * half : 2 * half + 2].astype(f32).reshape(HALF, cells).astype(bf16)
        panel[pl.ds(pl.multiple_of(source * GROUP + half * HALF, HALF), HALF)] = rows

    inner = [(0, l) for l in range(depth + 1, 2 * depth - 1)]
    done = set(inner)
    for k, l in inner:
        smooth(k, l)

    halo_after.wait_recv()
    halo_before.wait_recv()
    has_before = jnp.where(me > 0, 1.0, 0.0).astype(f32)
    has_after = jnp.where(me < slabs - 1, 1.0, 0.0).astype(f32)
    for g in range(depth):
        cut = slice(g * plane, (g + 1) * plane)
        field[0, g] = halo[0, :, cut].astype(f32) * has_before
        field[0, 2 * depth + g] = halo[1, :, cut].astype(f32) * has_after

    def smooth_all(k, l):
        if k < 0 or (k, l) in done:
            return
        for near in (l - 1, l, l + 1):
            smooth_all(k - 1, near)
        smooth(k, l)
        done.add((k, l))

    for t in range(depth):
        smooth_all(sweeps - 1, depth + t)
    for copy in over_y:
        copy.start()
    over_x = gather_half(0)
    over_x += gather_half(1)
    gather_far(0)
    gather_far(1)

    data_rows = groups * GROUP
    chunk = min(CHUNK, data_rows)
    chunks = data_rows // chunk
    blocks = chunk // (2 * out_rows)
    own_chunk = lax.div(chip, blocks)

    def copy_sibling(turn):
        return remote(
            product.at[turn, 1 - core], sibling_in.at[turn], sib_send.at[turn], sib_recv.at[turn], (dp, sibling)
        )

    def copy_part(to):
        return remote(part.at[to], out_ref.at[chip], rs_send.at[0], rs_recv.at[0], (dp, 2 * to + core))

    def chunk_of(turn):
        return lax.rem(own_chunk + 1 + turn, chunks)

    def multiply(turn):
        here = chunk_of(turn)
        rows = sens[pl.ds(here * (chunk // GROUP), chunk // GROUP)].reshape(chunk, cells)
        result = lax.dot_general(rows, panel[...], (((1,), (1,)), ((), ())), preferred_element_type=f32)
        result = result.reshape(blocks, 2, out_rows, PANEL)
        for half in range(2):
            product[turn, half] = result[:, half]
        copy_sibling(turn).start()

    def send_parts(turn):
        here = chunk_of(turn)
        copy_sibling(turn).wait_recv()
        total = (product[turn, core] + sibling_in[turn]) * (1.0 / math.sqrt(layers * plane))
        block = here * blocks + lax.broadcasted_iota(jnp.int32, total.shape, 0)
        row = dp * data_rows + (2 * block + core) * out_rows + lax.broadcasted_iota(jnp.int32, total.shape, 1)
        col = lax.broadcasted_iota(jnp.int32, total.shape, 2)
        part[pl.ds(here * blocks, blocks)] = jnp.where(row >= start * PANEL + col, total, 0.0).astype(bf16)
        for i in range(blocks):
            to = here * blocks + i

            @pl.when(to != chip)
            def _(to=to):
                copy_part(to).start()

    for turn in range(chunks):
        multiply(turn)
        if turn > 0:
            send_parts(turn - 1)
    send_parts(chunks - 1)
    own_part = pltpu.make_async_copy(part.at[chip], out_ref.at[chip], rs_send.at[1])
    own_part.start()

    class_after.wait_send()
    class_before.wait_send()
    halo_after.wait_send()
    halo_before.wait_send()

    @pl.when(x < 2)
    def _():
        for copy in (copy_far, copy_in, copy_mate, copy_out, copy_in_late, copy_chosen):
            copy.wait_send()

    @pl.when(x >= 2)
    def _():
        copy_on.wait_send()

    for j in range(4):

        @pl.when(yh != j)
        def _(j=j):
            copy_y(j).wait_send()

    for copy in over_y + over_x:
        copy.wait_send()
    for turn in range(chunks):
        copy_sibling(turn).wait_send()

    others = remote(
        part.at[0 : chips - 1], out_ref.at[0 : chips - 1], rs_send.at[0], rs_recv.at[0], (dp, sibling)
    )
    others.wait_send()
    others.wait_recv()
    own_part.wait()


def body(sensitivity, panel_index, cell_class, tear_layer, coef_table):
    rows, cells = sensitivity.shape
    depth, plane = cell_class.shape
    slabs = lax.axis_size("slab")
    out_rows = rows // slabs
    groups = rows // GROUP
    chips = slabs // 2
    chunks = max(1, rows // CHUNK)
    bf16 = jnp.bfloat16
    dma = pltpu.SemaphoreType.DMA
    sweeps = coef_table.shape[0]
    ext = -(-(depth + 4) // 8) * 8
    parts = pl.pallas_call(
        functools.partial(kernel, slabs),
        out_shape=jax.ShapeDtypeStruct((chips, out_rows, PANEL), bf16),
        in_specs=[pl.BlockSpec(memory_space=pltpu.HBM)] * 5,
        out_specs=pl.BlockSpec(memory_space=pltpu.HBM),
        scratch_shapes=[
            pltpu.SMEM(panel_index.shape, jnp.int32),
            pltpu.SMEM(coef_table.shape, jnp.float32),
            pltpu.VMEM((depth, plane), jnp.int32),
            pltpu.VMEM((1, plane), jnp.int32),
            pltpu.VMEM((groups, GROUP, cells), bf16),
            pltpu.VMEM((4, 2, HALF, cells), bf16),
            pltpu.VMEM((2, HALF, cells), bf16),
            pltpu.VMEM((2, HALF, cells), bf16),
            pltpu.VMEM((HALF, cells), bf16),
            pltpu.VMEM((2, HALF, cells), bf16),
            pltpu.VMEM((HALF, cells), bf16),
            pltpu.VMEM((4, PIECE, cells), bf16),
            pltpu.VMEM((4, PIECE, cells), bf16),
            pltpu.VMEM((PIECE, cells), bf16),
            pltpu.VMEM((2, PIECE, cells), bf16),
            pltpu.VMEM((2, depth, plane), jnp.int32),
            pltpu.VMEM((ext, plane), jnp.int32),
            pltpu.VMEM((sweeps, 4, ext, plane), jnp.float32),
            pltpu.VMEM((sweeps, 3 * depth, PIECE, plane), jnp.float32),
            pltpu.VMEM((4, 4, PIECE, cells), bf16),
            pltpu.VMEM((PANEL, cells), bf16),
            pltpu.VMEM((chunks, 2, rows // chunks // (2 * out_rows), out_rows, PANEL), jnp.float32),
            pltpu.VMEM((chunks, rows // chunks // (2 * out_rows), out_rows, PANEL), jnp.float32),
            pltpu.VMEM((chips, out_rows, PANEL), bf16),
            dma((5,)),
            dma((2,)),
            dma((2,)),
            dma((6,)),
            dma((6,)),
            dma((4,)),
            dma((4,)),
            dma((2,)),
            dma((2,)),
            dma((4,)),
            dma((4,)),
            dma((8,)),
            dma((8,)),
            dma((chunks,)),
            dma((chunks,)),
            dma((2,)),
            dma((1,)),
        ],
        compiler_params=pltpu.CompilerParams(
            collective_id=0, has_side_effects=True, vmem_limit_bytes=VMEM_LIMIT
        ),
        cost_estimate=pl.CostEstimate(
            flops=2 * rows * cells * PANEL, bytes_accessed=2 * rows * cells, transcendentals=0
        ),
        name="panel",
    )(
        panel_index,
        coef_table,
        sensitivity.reshape(groups, GROUP, cells),
        cell_class,
        tear_layer.reshape(1, plane),
    )
    return parts.astype(jnp.float32).sum(axis=0)


def solution(mesh):
    return jax.shard_map(
        body,
        mesh=mesh,
        in_specs=(P("dp", "slab"), P(), P("slab", None), P(), P()),
        out_specs=P(("dp", "slab"), None),
        check_vma=False,
    )
```

```python
import functools
import math

import jax
import jax.numpy as jnp
from jax import lax
from jax.experimental import pallas as pl
from jax.experimental.pallas import tpu as pltpu
from jax.sharding import PartitionSpec as P

WIDTH_Y = 32
PANEL = 128
GROUP = 32
HALF = 16
PIECE = 8
CHUNK = 384
VMEM_LIMIT = 63 * 1024 * 1024


def kernel(
    slabs,
    panel_hbm,
    table_hbm,
    sens_hbm,
    class_hbm,
    tear_hbm,
    out_ref,
    panel_ref,
    table_ref,
    class_ref,
    tear_ref,
    sens,
    send1,
    recv_early,
    recv_late,
    fwd1,
    pair1,
    chosen1,
    send2,
    recv2,
    raw,
    halo,
    class_halo,
    class_ext,
    coef,
    field,
    gath,
    product,
    sibling_in,
    part,
    parts_in,
    load_sem,
    class_send,
    class_recv,
    s1_send,
    s1_recv,
    s2_send,
    s2_recv,
    h_send,
    h_recv,
    g5_send,
    g5_recv,
    g6_send,
    g6_recv,
    sib_send,
    sib_recv,
    rs_send,
    rs_recv,
):
    f32 = jnp.float32
    bf16 = jnp.bfloat16
    dp = lax.axis_index("dp")
    me = lax.axis_index("slab")
    x = lax.div(dp, 4)
    yh = lax.rem(dp, 4)
    groups, _, cells = sens.shape
    chips = slabs // 2
    core = lax.rem(me, 2)
    half = cells // 2
    chip = lax.div(me, 2)
    sibling = me + 1 - 2 * core
    depth, plane = class_ref.shape
    layers = depth * slabs
    out_rows = out_ref.shape[0]
    panels_dev = groups * GROUP // PANEL
    right = lax.rem(x + 1, 4)
    left = lax.rem(x + 3, 4)
    before = lax.rem(me + slabs - 1, slabs)
    after = lax.rem(me + 1, slabs)

    def at(x_to, y_to, slab_to):
        return (x_to * 4 + y_to, slab_to)

    def fold(rows):
        return jnp.concatenate([rows[:, :half], rows[:, half:]], axis=0).astype(bf16)

    def unfold(piece):
        piece = piece.astype(f32)
        return jnp.concatenate([piece[:PIECE], piece[PIECE:]], axis=1)

    def remote(src, dst, send_sem, recv_sem, target):
        return pltpu.make_async_remote_copy(
            src_ref=src,
            dst_ref=dst,
            send_sem=send_sem,
            recv_sem=recv_sem,
            device_id=target,
            device_id_type=pl.DeviceIdType.MESH,
        )

    loads = 4

    def load(i):
        part_of = pl.ds(i * (groups // loads), groups // loads)
        return pltpu.make_async_copy(sens_hbm.at[part_of], sens.at[part_of], load_sem.at[0])

    small = [
        pltpu.make_async_copy(source, target, load_sem.at[1 + i])
        for i, (source, target) in enumerate(
            [(class_hbm, class_ref), (tear_hbm, tear_ref), (table_hbm, table_ref), (panel_hbm, panel_ref)]
        )
    ]
    for copy in small:
        copy.start()
    for i in range(loads):
        load(i).start()

    barrier = pltpu.get_barrier_semaphore()

    def greet(target):
        pl.semaphore_signal(
            barrier, inc=1, device_id=target, device_id_type=pl.DeviceIdType.MESH
        )

    for d in sorted(range(1, chips), key=lambda d: -min(d, chips - d)):
        greet((dp, lax.rem(me + 2 * d, slabs)))

    for dj in (2, 1, 3):
        greet(at(x, lax.rem(yh + dj, 4), me))
    greet((dp, before))
    greet((dp, after))
    greet(at(right, yh, me))
    greet(at(left, yh, me))
    greet(at(lax.rem(x + 2, 4), yh, me))

    for copy in small:
        copy.wait()
    pltpu.make_async_copy(sens_hbm, sens, load_sem.at[0]).wait()

    start = panel_ref[0]
    owner = lax.div(start, panels_dev)
    x_owner = lax.div(owner, 4)
    y_owner = lax.rem(owner, 4)
    first_group = lax.rem(start, panels_dev) * 4

    @pl.when(x < 2)
    def _():
        for q in range(4):
            send1[q] = sens[first_group + q].reshape(2, HALF, cells)

    pl.semaphore_wait(barrier, 8 + chips - 1)

    def early(q):
        return send1.at[q, 0]

    def late(q):
        return send1.at[q, 1]

    mate = at(1 - x, yh, me)
    outer = at(3 - x, yh, me)
    copy_far = remote(early(x + 2), fwd1, s1_send.at[0], s1_recv.at[0], outer)
    copy_in = remote(early(1 - x), recv_early.at[x], s1_send.at[1], s1_recv.at[1], mate)
    copy_mate = remote(late(x + 2), pair1.at[x], s1_send.at[2], s1_recv.at[2], mate)
    copy_out = remote(early(3 - x), recv_early.at[x], s1_send.at[3], s1_recv.at[3], outer)
    copy_in_late = remote(late(1 - x), recv_late.at[x], s1_send.at[4], s1_recv.at[4], mate)
    copy_chosen = remote(chosen1, recv_late.at[0], s1_send.at[5], s1_recv.at[5], outer)
    copy_on = remote(fwd1, recv_early.at[3 - x], s1_send.at[1], s1_recv.at[1], at(5 - x, yh, me))

    def arrived(slot, to):
        remote(to, to, s1_send.at[slot], s1_recv.at[slot], at(right, yh, me)).wait_recv()

    @pl.when(x < 2)
    def _():
        for copy in (copy_far, copy_mate, copy_in, copy_out, copy_in_late):
            copy.start()
        recv_early[x] = send1[x, 0]
        recv_late[x] = send1[x, 1]
        pair1[x] = send1[3 - x, 1]

    class_after = remote(class_ref, class_halo.at[0], class_send.at[0], class_recv.at[0], (dp, after))
    class_before = remote(class_ref, class_halo.at[1], class_send.at[1], class_recv.at[1], (dp, before))
    class_after.start()
    class_before.start()

    class_after.wait_recv()
    class_before.wait_recv()
    class_ext[0:2] = class_halo[0, depth - 2 : depth]
    class_ext[2 : 2 + depth] = class_ref[...]
    class_ext[2 + depth : 4 + depth] = class_halo[1, 0:2]
    class_ext[4 + depth :] = jnp.zeros_like(class_ext[4 + depth :])
    classes = class_ext[...]
    layer = me * depth - 2 + lax.broadcasted_iota(jnp.int32, classes.shape, 0)
    valid = (layer >= 0) & (layer < layers)
    tear = jnp.broadcast_to(tear_ref[...], classes.shape)
    open_up = tear != layer
    open_down = tear != layer + 1
    for k in range(table_ref.shape[0]):
        a = jnp.zeros(classes.shape, f32)
        b = jnp.zeros(classes.shape, f32)
        for level in range(table_ref.shape[2]):
            a = jnp.where(classes == level, table_ref[k, 0, level], a)
            b = jnp.where(classes == level, table_ref[k, 1, level], b)
        a = jnp.where(valid, a, 0.0)
        b = jnp.where(valid, 4.0 * b, 0.0)
        up = jnp.where(open_up, b, 0.0)
        down = jnp.where(open_down, b, 0.0)
        coef[k, 0] = 1.0 - 4.0 * a - up - down
        coef[k, 1] = a
        coef[k, 2] = up
        coef[k, 3] = down

    def copy_y(j):
        return remote(send2.at[j], recv2.at[yh], s2_send.at[j], s2_recv.at[yh], at(x, j, me))

    def wait_y(dj):
        j = lax.rem(yh + dj, 4)
        remote(send2.at[j], recv2.at[j], s2_send.at[j], s2_recv.at[j], at(x, j, me)).wait_recv()

    def scatter_y(rows, first):
        rows = rows.astype(f32)
        pieces = [fold(rows[:PIECE]), fold(rows[PIECE:])]
        for j in (first, first + 1):

            @pl.when(yh == j)
            def _(j=j):
                recv2[yh] = pieces[j - first]

            @pl.when(yh != j)
            def _(j=j):
                send2[j] = pieces[j - first]
                copy_y(j).start()

    @pl.when(x >= 2)
    def _():
        arrived(0, fwd1)
        copy_on.start()
        arrived(3, recv_early.at[3 - x])

    arrived(1, recv_early.at[jnp.where(x < 2, 1 - x, x - 2)])
    scatter_y(recv_early[x_owner], 0)

    @pl.when(x < 2)
    def _():
        arrived(2, pair1.at[1 - x])
        chosen1[...] = pair1[x_owner]
        copy_chosen.start()
        arrived(4, recv_late.at[1 - x])

    @pl.when(x >= 2)
    def _():
        arrived(5, recv_late.at[0])

    scatter_y(recv_late[jnp.where(x < 2, x_owner, 0)], 2)
    for dj in (2, 1, 3):
        wait_y(dj)

    raw[...] = recv2[y_owner]
    halo_after = remote(raw, halo.at[0], h_send.at[0], h_recv.at[0], (dp, after))
    halo_before = remote(raw, halo.at[1], h_send.at[1], h_recv.at[1], (dp, before))
    halo_after.start()
    halo_before.start()

    own_rows = unfold(raw[...])
    for g in range(depth):
        field[0, depth + g] = own_rows[:, g * plane : (g + 1) * plane]
    position = lax.broadcasted_iota(jnp.int32, (PIECE, plane), 1)
    column = lax.rem(position, WIDTH_Y)
    sweeps = table_ref.shape[0]

    def smooth(k, l):
        u = field[k, l]
        north = jnp.where(position >= WIDTH_Y, pltpu.roll(u, WIDTH_Y, 1), 0.0)
        south = jnp.where(position < plane - WIDTH_Y, pltpu.roll(u, plane - WIDTH_Y, 1), 0.0)
        west = jnp.where(column > 0, pltpu.roll(u, 1, 1), 0.0)
        east = jnp.where(column < WIDTH_Y - 1, pltpu.roll(u, plane - 1, 1), 0.0)
        e = l - depth + 2
        updated = (
            coef[k, 0, e : e + 1] * u
            + coef[k, 1, e : e + 1] * ((north + south) + (west + east))
            + coef[k, 2, e : e + 1] * field[k, l - 1]
            + coef[k, 3, e : e + 1] * field[k, l + 1]
        )
        if k + 1 < sweeps:
            field[k + 1, l] = updated
        else:
            g = l - depth
            field[0, 3 * depth + g] = updated

    def copy_g5(place, dj, lands):
        target = at(x, lax.rem(yh + dj, 4), me)
        return remote(gath.at[x, 0], gath.at[x, lands], g5_send.at[place], g5_recv.at[lands], target)

    over_y = [copy_g5(3, 2, 3), copy_g5(1, 1, 2), copy_g5(2, 3, 1)]

    def wait_g5(place):
        remote(gath.at[x, 0], gath.at[x, place], g5_send.at[place], g5_recv.at[place], at(right, yh, me)).wait_recv()

    def copy_g6(way, source, first, last, slot):
        part_of = gath.at[source, first:last]
        return remote(part_of, part_of, g6_send.at[slot], g6_recv.at[slot], at(way, yh, me))

    rounds = [(0, 1), (1, 3), (3, 4)]
    far = lax.rem(x + 2, 4)
    to_right = [copy_g6(right, x, *span, i) for i, span in enumerate(rounds)]
    to_left = [copy_g6(left, x, *span, 3 + i) for i, span in enumerate(rounds)]
    from_left = [copy_g6(right, left, *span, i) for i, span in enumerate(rounds)]
    from_right = [copy_g6(left, right, *span, 3 + i) for i, span in enumerate(rounds)]
    relays = [copy_g6(right, left, 0, 2, 6), copy_g6(left, right, 2, 3, 7)]
    to_far = copy_g6(far, x, 3, 4, 8)
    relayed = [copy_g6(right, far, 0, 2, 6), copy_g6(left, far, 2, 3, 7), copy_g6(far, far, 3, 4, 8)]

    inner = [(0, l) for l in range(depth + 1, 2 * depth - 1)]
    done = set(inner)
    for k, l in inner:
        smooth(k, l)

    halo_after.wait_recv()
    halo_before.wait_recv()
    has_before = jnp.where(me > 0, 1.0, 0.0).astype(f32)
    has_after = jnp.where(me < slabs - 1, 1.0, 0.0).astype(f32)
    rows_before = unfold(halo[0]) * has_before
    rows_after = unfold(halo[1]) * has_after
    for g in range(depth):
        field[0, g] = rows_before[:, g * plane : (g + 1) * plane]
        field[0, 2 * depth + g] = rows_after[:, g * plane : (g + 1) * plane]

    def smooth_all(k, l):
        if k < 0 or (k, l) in done:
            return
        for near in (l - 1, l, l + 1):
            smooth_all(k - 1, near)
        smooth(k, l)
        done.add((k, l))

    for t in range(depth):
        smooth_all(sweeps - 1, depth + t)
    gath[x, 0] = fold(jnp.concatenate([field[0, 3 * depth + g] for g in range(depth)], axis=1))
    for copy in over_y + [to_right[0], to_left[0]]:
        copy.start()

    wait_g5(1)
    wait_g5(2)
    to_right[1].start()
    to_left[1].start()
    wait_g5(3)
    to_far.start()
    to_right[2].start()
    to_left[2].start()
    from_left[0].wait_recv()
    from_left[1].wait_recv()
    relays[0].start()
    from_right[0].wait_recv()
    from_right[1].wait_recv()
    relays[1].start()
    for copy in (from_left[2], from_right[2], *relayed):
        copy.wait_recv()

    data_rows = groups * GROUP
    chunk = min(CHUNK, data_rows)
    chunks = data_rows // chunk
    blocks = chunk // (2 * out_rows)
    own_chunk = lax.div(chip, blocks)

    def copy_sibling(turn):
        return remote(
            product.at[turn, 1 - core], sibling_in.at[turn], sib_send.at[turn], sib_recv.at[turn], (dp, sibling)
        )

    def copy_part(to):
        return remote(part.at[to], parts_in.at[chip], rs_send.at[0], rs_recv.at[0], (dp, 2 * to + core))

    def chunk_of(turn):
        return lax.rem(own_chunk + 1 + turn, chunks)

    def multiply(turn):
        here = chunk_of(turn)
        part_of = pl.ds(here * (chunk // GROUP), chunk // GROUP)
        pieces = gath[...].reshape(2 * PANEL, half)
        first, second = [
            lax.dot_general(
                sens[part_of, :, h * half : (h + 1) * half].reshape(chunk, half),
                pieces,
                (((1,), (1,)), ((), ())),
                preferred_element_type=f32,
            )
            for h in range(2)
        ]
        lane = lax.broadcasted_iota(jnp.int32, (chunk, PANEL), 1)
        result = jnp.where(
            lax.rem(lane, 2 * PIECE) < PIECE,
            first[:, :PANEL] + pltpu.roll(second[:, :PANEL], PANEL - PIECE, 1),
            pltpu.roll(first[:, PANEL:], PIECE, 1) + second[:, PANEL:],
        )
        result = result.reshape(blocks, 2, out_rows, PANEL)
        for c in range(2):
            product[turn, c] = result[:, c]
        copy_sibling(turn).start()

    def send_parts(turn):
        here = chunk_of(turn)
        copy_sibling(turn).wait_recv()
        part[pl.ds(here * blocks, blocks)] = (product[turn, core] + sibling_in[turn]).astype(bf16)
        for i in range(blocks):
            to = here * blocks + i

            @pl.when(to != chip)
            def _(to=to):
                copy_part(to).start()

    for turn in range(chunks):
        multiply(turn)
        if turn > 0:
            send_parts(turn - 1)
    send_parts(chunks - 1)
    parts_in[chip] = part[chip]

    class_after.wait_send()
    class_before.wait_send()
    halo_after.wait_send()
    halo_before.wait_send()

    @pl.when(x < 2)
    def _():
        for copy in (copy_far, copy_in, copy_mate, copy_out, copy_in_late, copy_chosen):
            copy.wait_send()

    @pl.when(x >= 2)
    def _():
        copy_on.wait_send()

    for j in range(4):

        @pl.when(yh != j)
        def _(j=j):
            copy_y(j).wait_send()

    for copy in over_y + to_right + to_left + relays + [to_far]:
        copy.wait_send()
    for turn in range(chunks):
        copy_sibling(turn).wait_send()

    others = remote(
        part.at[0 : chips - 1], parts_in.at[0 : chips - 1], rs_send.at[0], rs_recv.at[0], (dp, sibling)
    )
    others.wait_send()
    others.wait_recv()

    total = jnp.zeros(out_ref.shape, f32)
    for i in range(chips):
        total = total + parts_in[i].astype(f32)
    total = total * (1.0 / math.sqrt(layers * plane))
    lane = lax.broadcasted_iota(jnp.int32, (PANEL, PANEL), 0)
    wanted = lax.broadcasted_iota(jnp.int32, (PANEL, PANEL), 1)
    from_x = lax.div(wanted, GROUP)
    dj = lax.rem(lax.div(wanted, PIECE) + 4 - yh, 4)
    place = jnp.where(dj == 2, 3, jnp.where(dj == 3, 2, dj))
    held = 64 * lax.rem(from_x, 2) + 16 * place + 8 * lax.div(from_x, 2) + lax.rem(wanted, PIECE)
    total = jnp.dot(
        total, (lane == held).astype(f32), precision=lax.Precision.HIGHEST, preferred_element_type=f32
    )
    col = lax.broadcasted_iota(jnp.int32, out_ref.shape, 1)
    base = dp * data_rows + me * out_rows
    row = base + lax.broadcasted_iota(jnp.int32, out_ref.shape, 0)
    out_ref[...] = jnp.where(row >= start * PANEL + col, total, 0.0)


def body(sensitivity, panel_index, cell_class, tear_layer, coef_table):
    rows, cells = sensitivity.shape
    depth, plane = cell_class.shape
    slabs = lax.axis_size("slab")
    out_rows = rows // slabs
    groups = rows // GROUP
    chips = slabs // 2
    chunks = max(1, rows // CHUNK)
    bf16 = jnp.bfloat16
    dma = pltpu.SemaphoreType.DMA
    sweeps = coef_table.shape[0]
    ext = -(-(depth + 4) // 8) * 8
    return pl.pallas_call(
        functools.partial(kernel, slabs),
        out_shape=jax.ShapeDtypeStruct((out_rows, PANEL), jnp.float32),
        in_specs=[pl.BlockSpec(memory_space=pltpu.HBM)] * 5,
        out_specs=pl.BlockSpec(memory_space=pltpu.VMEM),
        scratch_shapes=[
            pltpu.SMEM(panel_index.shape, jnp.int32),
            pltpu.SMEM(coef_table.shape, jnp.float32),
            pltpu.VMEM((depth, plane), jnp.int32),
            pltpu.VMEM((1, plane), jnp.int32),
            pltpu.VMEM((groups, GROUP, cells), bf16),
            pltpu.VMEM((4, 2, HALF, cells), bf16),
            pltpu.VMEM((2, HALF, cells), bf16),
            pltpu.VMEM((2, HALF, cells), bf16),
            pltpu.VMEM((HALF, cells), bf16),
            pltpu.VMEM((2, HALF, cells), bf16),
            pltpu.VMEM((HALF, cells), bf16),
            pltpu.VMEM((4, 2 * PIECE, cells // 2), bf16),
            pltpu.VMEM((4, 2 * PIECE, cells // 2), bf16),
            pltpu.VMEM((2 * PIECE, cells // 2), bf16),
            pltpu.VMEM((2, 2 * PIECE, cells // 2), bf16),
            pltpu.VMEM((2, depth, plane), jnp.int32),
            pltpu.VMEM((ext, plane), jnp.int32),
            pltpu.VMEM((sweeps, 4, ext, plane), jnp.float32),
            pltpu.VMEM((sweeps, 4 * depth, PIECE, plane), jnp.float32),
            pltpu.VMEM((4, 4, 2 * PIECE, cells // 2), bf16),
            pltpu.VMEM((chunks, 2, rows // chunks // (2 * out_rows), out_rows, PANEL), jnp.float32),
            pltpu.VMEM((chunks, rows // chunks // (2 * out_rows), out_rows, PANEL), jnp.float32),
            pltpu.VMEM((chips, out_rows, PANEL), bf16),
            pltpu.VMEM((chips, out_rows, PANEL), bf16),
            dma((5,)),
            dma((2,)),
            dma((2,)),
            dma((6,)),
            dma((6,)),
            dma((4,)),
            dma((4,)),
            dma((2,)),
            dma((2,)),
            dma((4,)),
            dma((4,)),
            dma((9,)),
            dma((9,)),
            dma((chunks,)),
            dma((chunks,)),
            dma((1,)),
            dma((1,)),
        ],
        compiler_params=pltpu.CompilerParams(
            collective_id=0, has_side_effects=True, vmem_limit_bytes=VMEM_LIMIT
        ),
        cost_estimate=pl.CostEstimate(
            flops=2 * rows * cells * PANEL, bytes_accessed=2 * rows * cells, transcendentals=0
        ),
        name="panel",
    )(
        panel_index,
        coef_table,
        sensitivity.reshape(groups, GROUP, cells),
        cell_class,
        tear_layer.reshape(1, plane),
    )


def solution(mesh):
    return jax.shard_map(
        body,
        mesh=mesh,
        in_specs=(P("dp", "slab"), P(), P("slab", None), P(), P()),
        out_specs=P(("dp", "slab"), None),
        check_vma=False,
    )
```

```python
import functools
import math

import jax
import jax.numpy as jnp
from jax import lax
from jax.experimental import pallas as pl
from jax.experimental.pallas import tpu as pltpu
from jax.sharding import PartitionSpec as P

WIDTH_Y = 32
PANEL = 128
GROUP = 32
PIECE = 8
CHUNK = 192
VMEM_LIMIT = 63 * 1024 * 1024


def kernel(
    slabs,
    panel_hbm,
    table_hbm,
    sens_hbm,
    class_hbm,
    tear_hbm,
    out_ref,
    panel_ref,
    table_ref,
    class_ref,
    tear_ref,
    sens,
    send1,
    recv_early,
    recv_late,
    fwd1,
    pair1,
    chosen1,
    send2,
    recv2,
    raw,
    halo,
    class_halo,
    class_ext,
    coef,
    field,
    gath,
    product,
    sibling_in,
    part,
    parts_in,
    load_sem,
    class_send,
    class_recv,
    s1_send,
    s1_recv,
    s2_send,
    s2_recv,
    h_send,
    h_recv,
    g5_send,
    g5_recv,
    g6_send,
    g6_recv,
    sib_send,
    sib_recv,
    rs_send,
    rs_recv,
):
    f32 = jnp.float32
    bf16 = jnp.bfloat16
    dp = lax.axis_index("dp")
    me = lax.axis_index("slab")
    x = lax.div(dp, 4)
    yh = lax.rem(dp, 4)
    groups, _, cells = sens.shape
    chips = slabs // 2
    core = lax.rem(me, 2)
    half = cells // 2
    chip = lax.div(me, 2)
    sibling = me + 1 - 2 * core
    depth, plane = class_ref.shape
    layers = depth * slabs
    out_rows = out_ref.shape[0]
    panels_dev = groups * GROUP // PANEL
    right = lax.rem(x + 1, 4)
    left = lax.rem(x + 3, 4)
    before = lax.rem(me + slabs - 1, slabs)
    after = lax.rem(me + 1, slabs)

    def at(x_to, y_to, slab_to):
        return (x_to * 4 + y_to, slab_to)

    def fold(rows):
        return jnp.concatenate([rows[:, :half], rows[:, half:]], axis=0).astype(bf16)

    def unfold(piece):
        piece = piece.astype(f32)
        return jnp.concatenate([piece[:PIECE], piece[PIECE:]], axis=1)

    def remote(src, dst, send_sem, recv_sem, target):
        return pltpu.make_async_remote_copy(
            src_ref=src,
            dst_ref=dst,
            send_sem=send_sem,
            recv_sem=recv_sem,
            device_id=target,
            device_id_type=pl.DeviceIdType.MESH,
        )

    loads = 4

    def load(i):
        part_of = pl.ds(i * (groups // loads), groups // loads)
        return pltpu.make_async_copy(sens_hbm.at[part_of], sens.at[part_of], load_sem.at[0])

    small = [
        pltpu.make_async_copy(source, target, load_sem.at[1 + i])
        for i, (source, target) in enumerate(
            [(class_hbm, class_ref), (tear_hbm, tear_ref), (table_hbm, table_ref), (panel_hbm, panel_ref)]
        )
    ]
    barrier = pltpu.get_barrier_semaphore()

    def start_loads():
        for i in range(loads):
            load(i).start()

    def wait_loads():
        pltpu.make_async_copy(sens_hbm, sens, load_sem.at[0]).wait()

    for copy in small:
        copy.start()

    @pl.when(x < 2)
    def _():
        start_loads()

    def greet(target):
        pl.semaphore_signal(
            barrier, inc=1, device_id=target, device_id_type=pl.DeviceIdType.MESH
        )

    for d in sorted(range(1, chips), key=lambda d: -min(d, chips - d)):
        greet((dp, lax.rem(me + 2 * d, slabs)))

    for dj in (2, 1, 3):
        greet(at(x, lax.rem(yh + dj, 4), me))
    greet((dp, before))
    greet((dp, after))
    greet(at(right, yh, me))
    greet(at(left, yh, me))
    greet(at(lax.rem(x + 2, 4), yh, me))

    @pl.when(x >= 2)
    def _():
        start_loads()

    for copy in small:
        copy.wait()

    start = panel_ref[0]
    owner = lax.div(start, panels_dev)
    x_owner = lax.div(owner, 4)
    y_owner = lax.rem(owner, 4)
    first_group = lax.rem(start, panels_dev) * 4

    @pl.when(x < 2)
    def _():
        wait_loads()
        for q in range(4):
            rows = sens[first_group + q].astype(f32)
            for j in range(4):
                send1[q, lax.rem(j - yh + 6, 4)] = fold(rows[j * PIECE : (j + 1) * PIECE])

    pl.semaphore_wait(barrier, 8 + chips - 1)

    def early(q):
        return send1.at[q, 0:2]

    def late(q):
        return send1.at[q, 2:4]

    mate = at(1 - x, yh, me)
    outer = at(3 - x, yh, me)
    copy_far = remote(early(x + 2), fwd1, s1_send.at[0], s1_recv.at[0], outer)
    copy_in = remote(early(1 - x), recv_early.at[x], s1_send.at[1], s1_recv.at[1], mate)
    copy_mate = remote(late(x + 2), pair1.at[x], s1_send.at[2], s1_recv.at[2], mate)
    copy_out = remote(early(3 - x), recv_early.at[x], s1_send.at[3], s1_recv.at[3], outer)
    copy_in_late = remote(late(1 - x), recv_late.at[x], s1_send.at[4], s1_recv.at[4], mate)
    copy_chosen = remote(chosen1, recv_late.at[0], s1_send.at[5], s1_recv.at[5], outer)
    copy_on = remote(fwd1, recv_early.at[3 - x], s1_send.at[1], s1_recv.at[1], at(5 - x, yh, me))

    def arrived(slot, to):
        remote(to, to, s1_send.at[slot], s1_recv.at[slot], at(right, yh, me)).wait_recv()

    @pl.when(x < 2)
    def _():
        for copy in (copy_far, copy_mate, copy_in, copy_out, copy_in_late):
            copy.start()
        recv_early[x] = send1[x, 0:2]
        recv_late[x] = send1[x, 2:4]
        pair1[x] = send1[3 - x, 2:4]

    class_after = remote(class_ref, class_halo.at[0], class_send.at[0], class_recv.at[0], (dp, after))
    class_before = remote(class_ref, class_halo.at[1], class_send.at[1], class_recv.at[1], (dp, before))
    class_after.start()
    class_before.start()

    class_after.wait_recv()
    class_before.wait_recv()
    class_ext[0:2] = class_halo[0, depth - 2 : depth]
    class_ext[2 : 2 + depth] = class_ref[...]
    class_ext[2 + depth : 4 + depth] = class_halo[1, 0:2]
    class_ext[4 + depth :] = jnp.zeros_like(class_ext[4 + depth :])
    classes = class_ext[...]
    layer = me * depth - 2 + lax.broadcasted_iota(jnp.int32, classes.shape, 0)
    valid = (layer >= 0) & (layer < layers)
    tear = jnp.broadcast_to(tear_ref[...], classes.shape)
    open_up = tear != layer
    open_down = tear != layer + 1
    for k in range(table_ref.shape[0]):
        a = jnp.zeros(classes.shape, f32)
        b = jnp.zeros(classes.shape, f32)
        for level in range(table_ref.shape[2]):
            a = jnp.where(classes == level, table_ref[k, 0, level], a)
            b = jnp.where(classes == level, table_ref[k, 1, level], b)
        a = jnp.where(valid, a, 0.0)
        b = jnp.where(valid, 4.0 * b, 0.0)
        up = jnp.where(open_up, b, 0.0)
        down = jnp.where(open_down, b, 0.0)
        coef[k, 0] = 1.0 - 4.0 * a - up - down
        coef[k, 1] = a
        coef[k, 2] = up
        coef[k, 3] = down

    def copy_y(dj):
        return remote(
            send2.at[dj], recv2.at[yh], s2_send.at[dj], s2_recv.at[yh], at(x, lax.rem(yh + dj, 4), me)
        )

    def wait_y(dj):
        j = lax.rem(yh + dj, 4)
        remote(send2.at[dj], recv2.at[j], s2_send.at[dj], s2_recv.at[j], at(x, j, me)).wait_recv()

    @pl.when(x >= 2)
    def _():
        arrived(0, fwd1)
        copy_on.start()
        arrived(3, recv_early.at[3 - x])

    arrived(1, recv_early.at[jnp.where(x < 2, 1 - x, x - 2)])
    chosen = recv_early[x_owner]
    send2[2] = chosen[0]
    copy_y(2).start()
    send2[3] = chosen[1]
    copy_y(3).start()

    @pl.when(x < 2)
    def _():
        arrived(2, pair1.at[1 - x])
        chosen1[...] = pair1[x_owner]
        copy_chosen.start()
        arrived(4, recv_late.at[1 - x])

    @pl.when(x >= 2)
    def _():
        arrived(5, recv_late.at[0])

    chosen = recv_late[jnp.where(x < 2, x_owner, 0)]
    send2[1] = chosen[1]
    copy_y(1).start()
    recv2[yh] = chosen[0]
    for dj in (2, 1, 3):
        wait_y(dj)

    raw[...] = recv2[y_owner]
    halo_after = remote(raw, halo.at[0], h_send.at[0], h_recv.at[0], (dp, after))
    halo_before = remote(raw, halo.at[1], h_send.at[1], h_recv.at[1], (dp, before))
    halo_after.start()
    halo_before.start()

    own_rows = unfold(raw[...])
    for g in range(depth):
        field[0, depth + g] = own_rows[:, g * plane : (g + 1) * plane]
    position = lax.broadcasted_iota(jnp.int32, (PIECE, plane), 1)
    column = lax.rem(position, WIDTH_Y)
    sweeps = table_ref.shape[0]

    def smooth(k, l):
        u = field[k, l]
        north = jnp.where(position >= WIDTH_Y, pltpu.roll(u, WIDTH_Y, 1), 0.0)
        south = jnp.where(position < plane - WIDTH_Y, pltpu.roll(u, plane - WIDTH_Y, 1), 0.0)
        west = jnp.where(column > 0, pltpu.roll(u, 1, 1), 0.0)
        east = jnp.where(column < WIDTH_Y - 1, pltpu.roll(u, plane - 1, 1), 0.0)
        e = l - depth + 2
        updated = (
            coef[k, 0, e : e + 1] * u
            + coef[k, 1, e : e + 1] * ((north + south) + (west + east))
            + coef[k, 2, e : e + 1] * field[k, l - 1]
            + coef[k, 3, e : e + 1] * field[k, l + 1]
        )
        if k + 1 < sweeps:
            field[k + 1, l] = updated
        else:
            g = l - depth
            field[0, 3 * depth + g] = updated

    def copy_g5(place, dj, lands):
        target = at(x, lax.rem(yh + dj, 4), me)
        return remote(gath.at[x, 0], gath.at[x, lands], g5_send.at[place], g5_recv.at[lands], target)

    over_y = [copy_g5(3, 2, 3), copy_g5(1, 1, 2), copy_g5(2, 3, 1)]

    def wait_g5(place):
        remote(gath.at[x, 0], gath.at[x, place], g5_send.at[place], g5_recv.at[place], at(right, yh, me)).wait_recv()

    def copy_g6(way, source, first, last, slot):
        part_of = gath.at[source, first:last]
        return remote(part_of, part_of, g6_send.at[slot], g6_recv.at[slot], at(way, yh, me))

    rounds = [(0, 1), (1, 3), (3, 4)]
    far = lax.rem(x + 2, 4)
    to_right = [copy_g6(right, x, *span, i) for i, span in enumerate(rounds)]
    to_left = [copy_g6(left, x, *span, 3 + i) for i, span in enumerate(rounds)]
    from_left = [copy_g6(right, left, *span, i) for i, span in enumerate(rounds)]
    from_right = [copy_g6(left, right, *span, 3 + i) for i, span in enumerate(rounds)]
    relays = [copy_g6(right, left, 0, 2, 6), copy_g6(left, right, 2, 3, 7)]
    to_far = copy_g6(far, x, 3, 4, 8)
    relayed = [copy_g6(right, far, 0, 2, 6), copy_g6(left, far, 2, 3, 7), copy_g6(far, far, 3, 4, 8)]

    inner = [(0, l) for l in range(depth + 1, 2 * depth - 1)]
    done = set(inner)
    for k, l in inner:
        smooth(k, l)

    halo_after.wait_recv()
    halo_before.wait_recv()
    has_before = jnp.where(me > 0, 1.0, 0.0).astype(f32)
    has_after = jnp.where(me < slabs - 1, 1.0, 0.0).astype(f32)
    rows_before = unfold(halo[0]) * has_before
    rows_after = unfold(halo[1]) * has_after
    for g in range(depth):
        field[0, g] = rows_before[:, g * plane : (g + 1) * plane]
        field[0, 2 * depth + g] = rows_after[:, g * plane : (g + 1) * plane]

    def smooth_all(k, l):
        if k < 0 or (k, l) in done:
            return
        for near in (l - 1, l, l + 1):
            smooth_all(k - 1, near)
        smooth(k, l)
        done.add((k, l))

    for t in range(depth):
        smooth_all(sweeps - 1, depth + t)
    gath[x, 0] = fold(jnp.concatenate([field[0, 3 * depth + g] for g in range(depth)], axis=1))
    for copy in over_y + [to_right[0], to_left[0]]:
        copy.start()

    wait_g5(1)
    wait_g5(2)
    to_right[1].start()
    to_left[1].start()
    wait_g5(3)
    to_far.start()
    to_right[2].start()
    to_left[2].start()
    from_left[0].wait_recv()
    from_left[1].wait_recv()
    relays[0].start()
    from_right[0].wait_recv()
    from_right[1].wait_recv()
    relays[1].start()
    for copy in (from_left[2], from_right[2], *relayed):
        copy.wait_recv()

    @pl.when(x >= 2)
    def _():
        wait_loads()

    data_rows = groups * GROUP
    chunk = min(CHUNK, data_rows)
    chunks = data_rows // chunk
    blocks = chunk // (2 * out_rows)
    own_chunk = lax.div(chip, blocks)

    def copy_sibling(turn):
        return remote(
            product.at[turn, 1 - core], sibling_in.at[turn], sib_send.at[turn], sib_recv.at[turn], (dp, sibling)
        )

    def copy_part(to):
        return remote(part.at[to], parts_in.at[chip], rs_send.at[0], rs_recv.at[0], (dp, 2 * to + core))

    def chunk_of(turn):
        return lax.rem(own_chunk + 1 + turn, chunks)

    def multiply(turn):
        here = chunk_of(turn)
        part_of = pl.ds(here * (chunk // GROUP), chunk // GROUP)
        pieces = gath[...].reshape(2 * PANEL, half)
        first, second = [
            lax.dot_general(
                sens[part_of, :, h * half : (h + 1) * half].reshape(chunk, half),
                pieces,
                (((1,), (1,)), ((), ())),
                preferred_element_type=f32,
            )
            for h in range(2)
        ]
        lane = lax.broadcasted_iota(jnp.int32, (chunk, PANEL), 1)
        result = jnp.where(
            lax.rem(lane, 2 * PIECE) < PIECE,
            first[:, :PANEL] + pltpu.roll(second[:, :PANEL], PANEL - PIECE, 1),
            pltpu.roll(first[:, PANEL:], PIECE, 1) + second[:, PANEL:],
        )
        result = result.reshape(blocks, 2, out_rows, PANEL)
        for c in range(2):
            product[turn, c] = result[:, c]
        copy_sibling(turn).start()

    def send_parts(turn):
        here = chunk_of(turn)
        copy_sibling(turn).wait_recv()
        part[pl.ds(here * blocks, blocks)] = (product[turn, core] + sibling_in[turn]).astype(bf16)
        for i in range(blocks):
            to = here * blocks + i

            @pl.when(to != chip)
            def _(to=to):
                copy_part(to).start()

    for turn in range(chunks):
        multiply(turn)
        if turn > 0:
            send_parts(turn - 1)
    send_parts(chunks - 1)
    parts_in[chip] = part[chip]

    class_after.wait_send()
    class_before.wait_send()
    halo_after.wait_send()
    halo_before.wait_send()

    @pl.when(x < 2)
    def _():
        for copy in (copy_far, copy_in, copy_mate, copy_out, copy_in_late, copy_chosen):
            copy.wait_send()

    @pl.when(x >= 2)
    def _():
        copy_on.wait_send()

    for dj in (1, 2, 3):
        copy_y(dj).wait_send()
    for copy in over_y + to_right + to_left + relays + [to_far]:
        copy.wait_send()
    for turn in range(chunks):
        copy_sibling(turn).wait_send()

    others = remote(
        part.at[0 : chips - 1], parts_in.at[0 : chips - 1], rs_send.at[0], rs_recv.at[0], (dp, sibling)
    )
    others.wait_send()
    others.wait_recv()

    total = jnp.zeros(out_ref.shape, f32)
    for i in range(chips):
        total = total + parts_in[i].astype(f32)
    total = total * (1.0 / math.sqrt(layers * plane))
    lane = lax.broadcasted_iota(jnp.int32, (PANEL, PANEL), 0)
    wanted = lax.broadcasted_iota(jnp.int32, (PANEL, PANEL), 1)
    from_x = lax.div(wanted, GROUP)
    dj = lax.rem(lax.div(wanted, PIECE) + 4 - yh, 4)
    place = jnp.where(dj == 2, 3, jnp.where(dj == 3, 2, dj))
    held = 64 * lax.rem(from_x, 2) + 16 * place + 8 * lax.div(from_x, 2) + lax.rem(wanted, PIECE)
    total = jnp.dot(
        total, (lane == held).astype(f32), precision=lax.Precision.HIGHEST, preferred_element_type=f32
    )
    col = lax.broadcasted_iota(jnp.int32, out_ref.shape, 1)
    base = dp * data_rows + me * out_rows
    row = base + lax.broadcasted_iota(jnp.int32, out_ref.shape, 0)
    out_ref[...] = jnp.where(row >= start * PANEL + col, total, 0.0)


def body(sensitivity, panel_index, cell_class, tear_layer, coef_table):
    rows, cells = sensitivity.shape
    depth, plane = cell_class.shape
    slabs = lax.axis_size("slab")
    out_rows = rows // slabs
    groups = rows // GROUP
    chips = slabs // 2
    chunks = max(1, rows // CHUNK)
    bf16 = jnp.bfloat16
    dma = pltpu.SemaphoreType.DMA
    sweeps = coef_table.shape[0]
    ext = -(-(depth + 4) // 8) * 8
    return pl.pallas_call(
        functools.partial(kernel, slabs),
        out_shape=jax.ShapeDtypeStruct((out_rows, PANEL), jnp.float32),
        in_specs=[pl.BlockSpec(memory_space=pltpu.HBM)] * 5,
        out_specs=pl.BlockSpec(memory_space=pltpu.VMEM),
        scratch_shapes=[
            pltpu.SMEM(panel_index.shape, jnp.int32),
            pltpu.SMEM(coef_table.shape, jnp.float32),
            pltpu.VMEM((depth, plane), jnp.int32),
            pltpu.VMEM((1, plane), jnp.int32),
            pltpu.VMEM((groups, GROUP, cells), bf16),
            pltpu.VMEM((4, 4, 2 * PIECE, cells // 2), bf16),
            pltpu.VMEM((2, 2, 2 * PIECE, cells // 2), bf16),
            pltpu.VMEM((2, 2, 2 * PIECE, cells // 2), bf16),
            pltpu.VMEM((2, 2 * PIECE, cells // 2), bf16),
            pltpu.VMEM((2, 2, 2 * PIECE, cells // 2), bf16),
            pltpu.VMEM((2, 2 * PIECE, cells // 2), bf16),
            pltpu.VMEM((4, 2 * PIECE, cells // 2), bf16),
            pltpu.VMEM((4, 2 * PIECE, cells // 2), bf16),
            pltpu.VMEM((2 * PIECE, cells // 2), bf16),
            pltpu.VMEM((2, 2 * PIECE, cells // 2), bf16),
            pltpu.VMEM((2, depth, plane), jnp.int32),
            pltpu.VMEM((ext, plane), jnp.int32),
            pltpu.VMEM((sweeps, 4, ext, plane), jnp.float32),
            pltpu.VMEM((sweeps, 4 * depth, PIECE, plane), jnp.float32),
            pltpu.VMEM((4, 4, 2 * PIECE, cells // 2), bf16),
            pltpu.VMEM((chunks, 2, rows // chunks // (2 * out_rows), out_rows, PANEL), jnp.float32),
            pltpu.VMEM((chunks, rows // chunks // (2 * out_rows), out_rows, PANEL), jnp.float32),
            pltpu.VMEM((chips, out_rows, PANEL), bf16),
            pltpu.VMEM((chips, out_rows, PANEL), bf16),
            dma((5,)),
            dma((2,)),
            dma((2,)),
            dma((6,)),
            dma((6,)),
            dma((4,)),
            dma((4,)),
            dma((2,)),
            dma((2,)),
            dma((4,)),
            dma((4,)),
            dma((9,)),
            dma((9,)),
            dma((chunks,)),
            dma((chunks,)),
            dma((1,)),
            dma((1,)),
        ],
        compiler_params=pltpu.CompilerParams(
            collective_id=0, has_side_effects=True, vmem_limit_bytes=VMEM_LIMIT
        ),
        cost_estimate=pl.CostEstimate(
            flops=2 * rows * cells * PANEL, bytes_accessed=2 * rows * cells, transcendentals=0
        ),
        name="panel",
    )(
        panel_index,
        coef_table,
        sensitivity.reshape(groups, GROUP, cells),
        cell_class,
        tear_layer.reshape(1, plane),
    )


def solution(mesh):
    return jax.shard_map(
        body,
        mesh=mesh,
        in_specs=(P("dp", "slab"), P(), P("slab", None), P(), P()),
        out_specs=P(("dp", "slab"), None),
        check_vma=False,
    )
```

```python
import functools
import math

import jax
import jax.numpy as jnp
from jax import lax
from jax.experimental import pallas as pl
from jax.experimental.pallas import tpu as pltpu
from jax.sharding import PartitionSpec as P

WIDTH_Y = 32
PANEL = 128
GROUP = 32
PIECE = 8
CHUNK = 192
VMEM_LIMIT = 63 * 1024 * 1024


def kernel(
    slabs,
    panel_hbm,
    table_hbm,
    sens_hbm,
    class_hbm,
    tear_hbm,
    out_ref,
    panel_ref,
    table_ref,
    class_ref,
    tear_ref,
    sens,
    send1,
    recv_early,
    recv_late,
    fwd1,
    pair1,
    chosen1,
    send2,
    recv2,
    raw,
    halo,
    class_halo,
    class_ext,
    coef,
    field,
    gath,
    product,
    sibling_in,
    part,
    load_sem,
    class_send,
    class_recv,
    s1_send,
    s1_recv,
    s2_send,
    s2_recv,
    h_send,
    h_recv,
    g5_send,
    g5_recv,
    g6_send,
    g6_recv,
    sib_send,
    sib_recv,
    rs_send,
    rs_recv,
):
    f32 = jnp.float32
    bf16 = jnp.bfloat16
    dp = lax.axis_index("dp")
    me = lax.axis_index("slab")
    x = lax.div(dp, 4)
    yh = lax.rem(dp, 4)
    groups, _, cells = sens.shape
    chips = slabs // 2
    core = lax.rem(me, 2)
    half = cells // 2
    chip = lax.div(me, 2)
    sibling = me + 1 - 2 * core
    depth, plane = class_ref.shape
    layers = depth * slabs
    out_rows = out_ref.shape[1]
    panels_dev = groups * GROUP // PANEL
    right = lax.rem(x + 1, 4)
    left = lax.rem(x + 3, 4)
    before = lax.rem(me + slabs - 1, slabs)
    after = lax.rem(me + 1, slabs)

    def at(x_to, y_to, slab_to):
        return (x_to * 4 + y_to, slab_to)

    def fold(rows):
        return jnp.concatenate([rows[:, :half], rows[:, half:]], axis=0).astype(bf16)

    def unfold(piece):
        piece = piece.astype(f32)
        return jnp.concatenate([piece[:PIECE], piece[PIECE:]], axis=1)

    def remote(src, dst, send_sem, recv_sem, target):
        return pltpu.make_async_remote_copy(
            src_ref=src,
            dst_ref=dst,
            send_sem=send_sem,
            recv_sem=recv_sem,
            device_id=target,
            device_id_type=pl.DeviceIdType.MESH,
        )

    loads = 4

    def load(i):
        part_of = pl.ds(i * (groups // loads), groups // loads)
        return pltpu.make_async_copy(sens_hbm.at[part_of], sens.at[part_of], load_sem.at[0])

    small = [
        pltpu.make_async_copy(source, target, load_sem.at[1 + i])
        for i, (source, target) in enumerate(
            [(class_hbm, class_ref), (tear_hbm, tear_ref), (table_hbm, table_ref), (panel_hbm, panel_ref)]
        )
    ]
    barrier = pltpu.get_barrier_semaphore()

    def start_loads():
        for i in range(loads):
            load(i).start()

    def wait_loads():
        pltpu.make_async_copy(sens_hbm, sens, load_sem.at[0]).wait()

    for copy in small:
        copy.start()

    @pl.when(x < 2)
    def _():
        start_loads()

    def greet(target):
        pl.semaphore_signal(
            barrier, inc=1, device_id=target, device_id_type=pl.DeviceIdType.MESH
        )

    for d in sorted(range(1, chips), key=lambda d: -min(d, chips - d)):
        greet((dp, lax.rem(me + 2 * d, slabs)))

    for dj in (2, 1, 3):
        greet(at(x, lax.rem(yh + dj, 4), me))
    greet((dp, before))
    greet((dp, after))
    greet(at(right, yh, me))
    greet(at(left, yh, me))
    greet(at(lax.rem(x + 2, 4), yh, me))

    @pl.when(x >= 2)
    def _():
        start_loads()

    for copy in small:
        copy.wait()

    start = panel_ref[0]
    owner = lax.div(start, panels_dev)
    x_owner = lax.div(owner, 4)
    y_owner = lax.rem(owner, 4)
    first_group = lax.rem(start, panels_dev) * 4

    @pl.when(x < 2)
    def _():
        wait_loads()
        for q in range(4):
            rows = sens[first_group + q].astype(f32)
            for j in range(4):
                send1[q, lax.rem(j - yh + 6, 4)] = fold(rows[j * PIECE : (j + 1) * PIECE])

    pl.semaphore_wait(barrier, 8 + chips - 1)

    def early(q):
        return send1.at[q, 0:2]

    def late(q):
        return send1.at[q, 2:4]

    mate = at(1 - x, yh, me)
    outer = at(3 - x, yh, me)
    copy_far = remote(early(x + 2), fwd1, s1_send.at[0], s1_recv.at[0], outer)
    copy_in = remote(early(1 - x), recv_early.at[x], s1_send.at[1], s1_recv.at[1], mate)
    copy_mate = remote(late(x + 2), pair1.at[x], s1_send.at[2], s1_recv.at[2], mate)
    copy_out = remote(early(3 - x), recv_early.at[x], s1_send.at[3], s1_recv.at[3], outer)
    copy_in_late = remote(late(1 - x), recv_late.at[x], s1_send.at[4], s1_recv.at[4], mate)
    copy_chosen = remote(chosen1, recv_late.at[0], s1_send.at[5], s1_recv.at[5], outer)
    copy_on = remote(fwd1, recv_early.at[3 - x], s1_send.at[1], s1_recv.at[1], at(5 - x, yh, me))

    def arrived(slot, to):
        remote(to, to, s1_send.at[slot], s1_recv.at[slot], at(right, yh, me)).wait_recv()

    @pl.when(x < 2)
    def _():
        for copy in (copy_far, copy_mate, copy_in, copy_out, copy_in_late):
            copy.start()
        recv_early[x] = send1[x, 0:2]
        recv_late[x] = send1[x, 2:4]
        pair1[x] = send1[3 - x, 2:4]

    class_after = remote(class_ref, class_halo.at[0], class_send.at[0], class_recv.at[0], (dp, after))
    class_before = remote(class_ref, class_halo.at[1], class_send.at[1], class_recv.at[1], (dp, before))
    class_after.start()
    class_before.start()

    class_after.wait_recv()
    class_before.wait_recv()
    class_ext[0:2] = class_halo[0, depth - 2 : depth]
    class_ext[2 : 2 + depth] = class_ref[...]
    class_ext[2 + depth : 4 + depth] = class_halo[1, 0:2]
    class_ext[4 + depth :] = jnp.zeros_like(class_ext[4 + depth :])
    classes = class_ext[...]
    layer = me * depth - 2 + lax.broadcasted_iota(jnp.int32, classes.shape, 0)
    valid = (layer >= 0) & (layer < layers)
    tear = jnp.broadcast_to(tear_ref[...], classes.shape)
    open_up = tear != layer
    open_down = tear != layer + 1
    for k in range(table_ref.shape[0]):
        a = jnp.zeros(classes.shape, f32)
        b = jnp.zeros(classes.shape, f32)
        for level in range(table_ref.shape[2]):
            a = jnp.where(classes == level, table_ref[k, 0, level], a)
            b = jnp.where(classes == level, table_ref[k, 1, level], b)
        a = jnp.where(valid, a, 0.0)
        b = jnp.where(valid, 4.0 * b, 0.0)
        up = jnp.where(open_up, b, 0.0)
        down = jnp.where(open_down, b, 0.0)
        coef[k, 0] = 1.0 - 4.0 * a - up - down
        coef[k, 1] = a
        coef[k, 2] = up
        coef[k, 3] = down

    def copy_y(dj):
        return remote(
            send2.at[dj], recv2.at[yh], s2_send.at[dj], s2_recv.at[yh], at(x, lax.rem(yh + dj, 4), me)
        )

    def wait_y(dj):
        j = lax.rem(yh + dj, 4)
        remote(send2.at[dj], recv2.at[j], s2_send.at[dj], s2_recv.at[j], at(x, j, me)).wait_recv()

    @pl.when(x >= 2)
    def _():
        arrived(0, fwd1)
        copy_on.start()
        arrived(3, recv_early.at[3 - x])

    arrived(1, recv_early.at[jnp.where(x < 2, 1 - x, x - 2)])
    chosen = recv_early[x_owner]
    send2[2] = chosen[0]
    copy_y(2).start()
    send2[3] = chosen[1]
    copy_y(3).start()

    @pl.when(x < 2)
    def _():
        arrived(2, pair1.at[1 - x])
        chosen1[...] = pair1[x_owner]
        copy_chosen.start()
        arrived(4, recv_late.at[1 - x])

    @pl.when(x >= 2)
    def _():
        arrived(5, recv_late.at[0])

    chosen = recv_late[jnp.where(x < 2, x_owner, 0)]
    send2[1] = chosen[1]
    copy_y(1).start()
    recv2[yh] = chosen[0]
    for dj in (2, 1, 3):
        wait_y(dj)

    raw[...] = recv2[y_owner]
    halo_after = remote(raw, halo.at[0], h_send.at[0], h_recv.at[0], (dp, after))
    halo_before = remote(raw, halo.at[1], h_send.at[1], h_recv.at[1], (dp, before))
    halo_after.start()
    halo_before.start()

    own_rows = unfold(raw[...])
    for g in range(depth):
        field[0, depth + g] = own_rows[:, g * plane : (g + 1) * plane]
    position = lax.broadcasted_iota(jnp.int32, (PIECE, plane), 1)
    column = lax.rem(position, WIDTH_Y)
    sweeps = table_ref.shape[0]

    def smooth(k, l):
        u = field[k, l]
        north = jnp.where(position >= WIDTH_Y, pltpu.roll(u, WIDTH_Y, 1), 0.0)
        south = jnp.where(position < plane - WIDTH_Y, pltpu.roll(u, plane - WIDTH_Y, 1), 0.0)
        west = jnp.where(column > 0, pltpu.roll(u, 1, 1), 0.0)
        east = jnp.where(column < WIDTH_Y - 1, pltpu.roll(u, plane - 1, 1), 0.0)
        e = l - depth + 2
        updated = (
            coef[k, 0, e : e + 1] * u
            + coef[k, 1, e : e + 1] * ((north + south) + (west + east))
            + coef[k, 2, e : e + 1] * field[k, l - 1]
            + coef[k, 3, e : e + 1] * field[k, l + 1]
        )
        if k + 1 < sweeps:
            field[k + 1, l] = updated
        else:
            g = l - depth
            field[0, 3 * depth + g] = updated

    def copy_g5(place, dj, lands):
        target = at(x, lax.rem(yh + dj, 4), me)
        return remote(gath.at[x, 0], gath.at[x, lands], g5_send.at[place], g5_recv.at[lands], target)

    over_y = [copy_g5(3, 2, 3), copy_g5(1, 1, 2), copy_g5(2, 3, 1)]

    def wait_g5(place):
        remote(gath.at[x, 0], gath.at[x, place], g5_send.at[place], g5_recv.at[place], at(right, yh, me)).wait_recv()

    def copy_g6(way, source, first, last, slot):
        part_of = gath.at[source, first:last]
        return remote(part_of, part_of, g6_send.at[slot], g6_recv.at[slot], at(way, yh, me))

    rounds = [(0, 1), (1, 3), (3, 4)]
    far = lax.rem(x + 2, 4)
    to_right = [copy_g6(right, x, *span, i) for i, span in enumerate(rounds)]
    to_left = [copy_g6(left, x, *span, 3 + i) for i, span in enumerate(rounds)]
    from_left = [copy_g6(right, left, *span, i) for i, span in enumerate(rounds)]
    from_right = [copy_g6(left, right, *span, 3 + i) for i, span in enumerate(rounds)]
    to_far = [copy_g6(far, x, 1, 3, 6), copy_g6(far, x, 3, 4, 7)]
    relay = copy_g6(left, right, 0, 1, 8)
    from_far = [copy_g6(far, far, 1, 3, 6), copy_g6(far, far, 3, 4, 7), copy_g6(left, far, 0, 1, 8)]

    inner = [(0, l) for l in range(depth + 1, 2 * depth - 1)]
    done = set(inner)
    for k, l in inner:
        smooth(k, l)

    halo_after.wait_recv()
    halo_before.wait_recv()
    has_before = jnp.where(me > 0, 1.0, 0.0).astype(f32)
    has_after = jnp.where(me < slabs - 1, 1.0, 0.0).astype(f32)
    rows_before = unfold(halo[0]) * has_before
    rows_after = unfold(halo[1]) * has_after
    for g in range(depth):
        field[0, g] = rows_before[:, g * plane : (g + 1) * plane]
        field[0, 2 * depth + g] = rows_after[:, g * plane : (g + 1) * plane]

    def smooth_all(k, l):
        if k < 0 or (k, l) in done:
            return
        for near in (l - 1, l, l + 1):
            smooth_all(k - 1, near)
        smooth(k, l)
        done.add((k, l))

    for t in range(depth):
        smooth_all(sweeps - 1, depth + t)
    gath[x, 0] = fold(jnp.concatenate([field[0, 3 * depth + g] for g in range(depth)], axis=1))
    for copy in over_y + [to_right[0], to_left[0]]:
        copy.start()

    wait_g5(1)
    wait_g5(2)
    to_far[0].start()
    to_right[1].start()
    to_left[1].start()
    from_right[0].wait_recv()
    relay.start()
    wait_g5(3)
    to_far[1].start()
    to_right[2].start()
    to_left[2].start()
    for copy in (from_left[0], *from_left[1:], *from_right[1:], *from_far):
        copy.wait_recv()

    @pl.when(x >= 2)
    def _():
        wait_loads()

    data_rows = groups * GROUP
    chunk = min(CHUNK, data_rows)
    chunks = data_rows // chunk
    blocks = chunk // (2 * out_rows)
    own_chunk = lax.div(chip, blocks)

    def copy_sibling(turn):
        return remote(
            product.at[turn, 1 - core], sibling_in.at[turn], sib_send.at[turn], sib_recv.at[turn], (dp, sibling)
        )

    def copy_part(to):
        return remote(part.at[to], out_ref.at[chip], rs_send.at[0], rs_recv.at[0], (dp, 2 * to + core))

    def chunk_of(turn):
        return lax.rem(own_chunk + 1 + turn, chunks)

    def multiply(turn):
        here = chunk_of(turn)
        part_of = pl.ds(here * (chunk // GROUP), chunk // GROUP)
        pieces = gath[...].reshape(2 * PANEL, half)
        first, second = [
            lax.dot_general(
                sens[part_of, :, h * half : (h + 1) * half].reshape(chunk, half),
                pieces,
                (((1,), (1,)), ((), ())),
                preferred_element_type=f32,
            )
            for h in range(2)
        ]
        lane = lax.broadcasted_iota(jnp.int32, (chunk, PANEL), 1)
        result = jnp.where(
            lax.rem(lane, 2 * PIECE) < PIECE,
            first[:, :PANEL] + pltpu.roll(second[:, :PANEL], PANEL - PIECE, 1),
            pltpu.roll(first[:, PANEL:], PIECE, 1) + second[:, PANEL:],
        )
        result = result.reshape(blocks, 2, out_rows, PANEL)
        for c in range(2):
            product[turn, c] = result[:, c]
        copy_sibling(turn).start()

    def send_parts(turn):
        here = chunk_of(turn)
        copy_sibling(turn).wait_recv()
        total = (product[turn, core] + sibling_in[turn]) * (1.0 / math.sqrt(layers * plane))
        lane = lax.broadcasted_iota(jnp.int32, (PANEL, PANEL), 0)
        wanted = lax.broadcasted_iota(jnp.int32, (PANEL, PANEL), 1)
        from_x = lax.div(wanted, GROUP)
        dj = lax.rem(lax.div(wanted, PIECE) + 4 - yh, 4)
        place = jnp.where(dj == 2, 3, jnp.where(dj == 3, 2, dj))
        held = 64 * lax.rem(from_x, 2) + 16 * place + 8 * lax.div(from_x, 2) + lax.rem(wanted, PIECE)
        total = jnp.dot(
            total.reshape(blocks * out_rows, PANEL),
            (lane == held).astype(f32),
            precision=lax.Precision.HIGHEST,
            preferred_element_type=f32,
        ).reshape(blocks, out_rows, PANEL)
        block = here * blocks + lax.broadcasted_iota(jnp.int32, total.shape, 0)
        row = dp * data_rows + (2 * block + core) * out_rows + lax.broadcasted_iota(jnp.int32, total.shape, 1)
        col = lax.broadcasted_iota(jnp.int32, total.shape, 2)
        part[pl.ds(here * blocks, blocks)] = jnp.where(row >= start * PANEL + col, total, 0.0).astype(bf16)
        for i in range(blocks):
            to = here * blocks + i

            @pl.when(to != chip)
            def _(to=to):
                copy_part(to).start()

    for turn in range(chunks):
        multiply(turn)
        if turn > 0:
            send_parts(turn - 1)
    send_parts(chunks - 1)
    own_part = pltpu.make_async_copy(part.at[chip], out_ref.at[chip], rs_send.at[1])
    own_part.start()

    class_after.wait_send()
    class_before.wait_send()
    halo_after.wait_send()
    halo_before.wait_send()

    @pl.when(x < 2)
    def _():
        for copy in (copy_far, copy_in, copy_mate, copy_out, copy_in_late, copy_chosen):
            copy.wait_send()

    @pl.when(x >= 2)
    def _():
        copy_on.wait_send()

    for dj in (1, 2, 3):
        copy_y(dj).wait_send()
    for copy in over_y + to_right + to_left + to_far + [relay]:
        copy.wait_send()
    for turn in range(chunks):
        copy_sibling(turn).wait_send()

    others = remote(
        part.at[0 : chips - 1], out_ref.at[0 : chips - 1], rs_send.at[0], rs_recv.at[0], (dp, sibling)
    )
    others.wait_send()
    others.wait_recv()
    own_part.wait()


def body(sensitivity, panel_index, cell_class, tear_layer, coef_table):
    rows, cells = sensitivity.shape
    depth, plane = cell_class.shape
    slabs = lax.axis_size("slab")
    out_rows = rows // slabs
    groups = rows // GROUP
    chips = slabs // 2
    chunks = max(1, rows // CHUNK)
    bf16 = jnp.bfloat16
    dma = pltpu.SemaphoreType.DMA
    sweeps = coef_table.shape[0]
    ext = -(-(depth + 4) // 8) * 8
    parts = pl.pallas_call(
        functools.partial(kernel, slabs),
        out_shape=jax.ShapeDtypeStruct((chips, out_rows, PANEL), bf16),
        in_specs=[pl.BlockSpec(memory_space=pltpu.HBM)] * 5,
        out_specs=pl.BlockSpec(memory_space=pltpu.HBM),
        scratch_shapes=[
            pltpu.SMEM(panel_index.shape, jnp.int32),
            pltpu.SMEM(coef_table.shape, jnp.float32),
            pltpu.VMEM((depth, plane), jnp.int32),
            pltpu.VMEM((1, plane), jnp.int32),
            pltpu.VMEM((groups, GROUP, cells), bf16),
            pltpu.VMEM((4, 4, 2 * PIECE, cells // 2), bf16),
            pltpu.VMEM((2, 2, 2 * PIECE, cells // 2), bf16),
            pltpu.VMEM((2, 2, 2 * PIECE, cells // 2), bf16),
            pltpu.VMEM((2, 2 * PIECE, cells // 2), bf16),
            pltpu.VMEM((2, 2, 2 * PIECE, cells // 2), bf16),
            pltpu.VMEM((2, 2 * PIECE, cells // 2), bf16),
            pltpu.VMEM((4, 2 * PIECE, cells // 2), bf16),
            pltpu.VMEM((4, 2 * PIECE, cells // 2), bf16),
            pltpu.VMEM((2 * PIECE, cells // 2), bf16),
            pltpu.VMEM((2, 2 * PIECE, cells // 2), bf16),
            pltpu.VMEM((2, depth, plane), jnp.int32),
            pltpu.VMEM((ext, plane), jnp.int32),
            pltpu.VMEM((sweeps, 4, ext, plane), jnp.float32),
            pltpu.VMEM((sweeps, 4 * depth, PIECE, plane), jnp.float32),
            pltpu.VMEM((4, 4, 2 * PIECE, cells // 2), bf16),
            pltpu.VMEM((chunks, 2, rows // chunks // (2 * out_rows), out_rows, PANEL), jnp.float32),
            pltpu.VMEM((chunks, rows // chunks // (2 * out_rows), out_rows, PANEL), jnp.float32),
            pltpu.VMEM((chips, out_rows, PANEL), bf16),
            dma((5,)),
            dma((2,)),
            dma((2,)),
            dma((6,)),
            dma((6,)),
            dma((4,)),
            dma((4,)),
            dma((2,)),
            dma((2,)),
            dma((4,)),
            dma((4,)),
            dma((9,)),
            dma((9,)),
            dma((chunks,)),
            dma((chunks,)),
            dma((2,)),
            dma((1,)),
        ],
        compiler_params=pltpu.CompilerParams(
            collective_id=0, has_side_effects=True, vmem_limit_bytes=VMEM_LIMIT
        ),
        cost_estimate=pl.CostEstimate(
            flops=2 * rows * cells * PANEL, bytes_accessed=2 * rows * cells, transcendentals=0
        ),
        name="panel",
    )(
        panel_index,
        coef_table,
        sensitivity.reshape(groups, GROUP, cells),
        cell_class,
        tear_layer.reshape(1, plane),
    )
    return parts.astype(jnp.float32).sum(axis=0)


def solution(mesh):
    return jax.shard_map(
        body,
        mesh=mesh,
        in_specs=(P("dp", "slab"), P(), P("slab", None), P(), P()),
        out_specs=P(("dp", "slab"), None),
        check_vma=False,
    )
```

```python
import functools
import math

import jax
import jax.numpy as jnp
from jax import lax
from jax.experimental import pallas as pl
from jax.experimental.pallas import tpu as pltpu
from jax.sharding import PartitionSpec as P

WIDTH_Y = 32
PANEL = 128
GROUP = 32
PIECE = 8
CHUNK = 192
VMEM_LIMIT = 63 * 1024 * 1024


def kernel(
    slabs,
    panel_hbm,
    table_hbm,
    sens_hbm,
    class_hbm,
    tear_hbm,
    out_ref,
    panel_ref,
    table_ref,
    class_ref,
    tear_ref,
    sens,
    send1,
    recv_early,
    recv_late,
    fwd1,
    pair1,
    chosen1,
    send2,
    recv2,
    raw,
    halo,
    class_halo,
    class_ext,
    coef,
    field,
    gath,
    product,
    sibling_in,
    part,
    load_sem,
    class_send,
    class_recv,
    s1_send,
    s1_recv,
    s2_send,
    s2_recv,
    h_send,
    h_recv,
    g5_send,
    g5_recv,
    g6_send,
    g6_recv,
    sib_send,
    sib_recv,
    rs_send,
    rs_recv,
):
    f32 = jnp.float32
    bf16 = jnp.bfloat16
    dp = lax.axis_index("dp")
    me = lax.axis_index("slab")
    x = lax.div(dp, 4)
    yh = lax.rem(dp, 4)
    groups, _, cells = sens.shape
    chips = slabs // 2
    core = lax.rem(me, 2)
    half = cells // 2
    chip = lax.div(me, 2)
    sibling = me + 1 - 2 * core
    depth, plane = class_ref.shape
    layers = depth * slabs
    out_rows = out_ref.shape[1]
    panels_dev = groups * GROUP // PANEL
    right = lax.rem(x + 1, 4)
    left = lax.rem(x + 3, 4)
    before = lax.rem(me + slabs - 1, slabs)
    after = lax.rem(me + 1, slabs)

    def at(x_to, y_to, slab_to):
        return (x_to * 4 + y_to, slab_to)

    def fold(rows):
        return jnp.concatenate([rows[:, :half], rows[:, half:]], axis=0).astype(bf16)

    def unfold(piece):
        piece = piece.astype(f32)
        return jnp.concatenate([piece[:PIECE], piece[PIECE:]], axis=1)

    def remote(src, dst, send_sem, recv_sem, target):
        return pltpu.make_async_remote_copy(
            src_ref=src,
            dst_ref=dst,
            send_sem=send_sem,
            recv_sem=recv_sem,
            device_id=target,
            device_id_type=pl.DeviceIdType.MESH,
        )

    loads = 4

    def load(i):
        part_of = pl.ds(i * (groups // loads), groups // loads)
        return pltpu.make_async_copy(sens_hbm.at[part_of], sens.at[part_of], load_sem.at[0])

    small = [
        pltpu.make_async_copy(source, target, load_sem.at[1 + i])
        for i, (source, target) in enumerate(
            [(class_hbm, class_ref), (tear_hbm, tear_ref), (table_hbm, table_ref), (panel_hbm, panel_ref)]
        )
    ]
    barrier = pltpu.get_barrier_semaphore()

    def start_loads():
        for i in range(loads):
            load(i).start()

    def wait_loads():
        pltpu.make_async_copy(sens_hbm, sens, load_sem.at[0]).wait()

    for copy in small:
        copy.start()

    @pl.when(x < 2)
    def _():
        start_loads()

    def greet(target):
        pl.semaphore_signal(
            barrier, inc=1, device_id=target, device_id_type=pl.DeviceIdType.MESH
        )

    @pl.loop(1, chips)
    def _(d):
        greet((dp, lax.rem(me + 2 * d, slabs)))

    for dj in (2, 1, 3):
        greet(at(x, lax.rem(yh + dj, 4), me))
    greet((dp, before))
    greet((dp, after))
    greet(at(right, yh, me))
    greet(at(left, yh, me))
    greet(at(lax.rem(x + 2, 4), yh, me))

    @pl.when(x >= 2)
    def _():
        start_loads()

    for copy in small:
        copy.wait()

    start = panel_ref[0]
    owner = lax.div(start, panels_dev)
    x_owner = lax.div(owner, 4)
    y_owner = lax.rem(owner, 4)
    first_group = lax.rem(start, panels_dev) * 4

    @pl.when(x < 2)
    def _():
        wait_loads()

        @pl.loop(0, 4)
        def _(q):
            rows = sens[first_group + q].astype(f32)
            for j in range(4):
                send1[q, lax.rem(j - yh + 6, 4)] = fold(rows[j * PIECE : (j + 1) * PIECE])

    pl.semaphore_wait(barrier, 8 + chips - 1)

    def early(q):
        return send1.at[q, 0:2]

    def late(q):
        return send1.at[q, 2:4]

    mate = at(1 - x, yh, me)
    outer = at(3 - x, yh, me)
    copy_far = remote(early(x + 2), fwd1, s1_send.at[0], s1_recv.at[0], outer)
    copy_in = remote(early(1 - x), recv_early.at[x], s1_send.at[1], s1_recv.at[1], mate)
    copy_mate = remote(late(x + 2), pair1.at[x], s1_send.at[2], s1_recv.at[2], mate)
    copy_out = remote(early(3 - x), recv_early.at[x], s1_send.at[3], s1_recv.at[3], outer)
    copy_in_late = remote(late(1 - x), recv_late.at[x], s1_send.at[4], s1_recv.at[4], mate)
    copy_chosen = remote(chosen1, recv_late.at[0], s1_send.at[5], s1_recv.at[5], outer)
    copy_on = remote(fwd1, recv_early.at[3 - x], s1_send.at[1], s1_recv.at[1], at(5 - x, yh, me))

    def arrived(slot, to):
        remote(to, to, s1_send.at[slot], s1_recv.at[slot], at(right, yh, me)).wait_recv()

    @pl.when(x < 2)
    def _():
        for copy in (copy_far, copy_mate, copy_in, copy_out, copy_in_late):
            copy.start()
        recv_early[x] = send1[x, 0:2]
        recv_late[x] = send1[x, 2:4]
        pair1[x] = send1[3 - x, 2:4]

    class_after = remote(class_ref, class_halo.at[0], class_send.at[0], class_recv.at[0], (dp, after))
    class_before = remote(class_ref, class_halo.at[1], class_send.at[1], class_recv.at[1], (dp, before))
    class_after.start()
    class_before.start()

    class_after.wait_recv()
    class_before.wait_recv()
    class_ext[0:2] = class_halo[0, depth - 2 : depth]
    class_ext[2 : 2 + depth] = class_ref[...]
    class_ext[2 + depth : 4 + depth] = class_halo[1, 0:2]
    class_ext[4 + depth :] = jnp.zeros_like(class_ext[4 + depth :])
    classes = class_ext[...]
    layer = me * depth - 2 + lax.broadcasted_iota(jnp.int32, classes.shape, 0)
    valid = (layer >= 0) & (layer < layers)
    tear = jnp.broadcast_to(tear_ref[...], classes.shape)
    open_up = tear != layer
    open_down = tear != layer + 1
    @pl.loop(0, table_ref.shape[0])
    def _(k):
        a = jnp.zeros(classes.shape, f32)
        b = jnp.zeros(classes.shape, f32)
        for level in range(table_ref.shape[2]):
            a = jnp.where(classes == level, table_ref[k, 0, level], a)
            b = jnp.where(classes == level, table_ref[k, 1, level], b)
        a = jnp.where(valid, a, 0.0)
        b = jnp.where(valid, 4.0 * b, 0.0)
        up = jnp.where(open_up, b, 0.0)
        down = jnp.where(open_down, b, 0.0)
        coef[k, 0] = 1.0 - 4.0 * a - up - down
        coef[k, 1] = a
        coef[k, 2] = up
        coef[k, 3] = down

    def copy_y(dj):
        return remote(
            send2.at[dj], recv2.at[yh], s2_send.at[dj], s2_recv.at[yh], at(x, lax.rem(yh + dj, 4), me)
        )

    def wait_y(dj):
        j = lax.rem(yh + dj, 4)
        remote(send2.at[dj], recv2.at[j], s2_send.at[dj], s2_recv.at[j], at(x, j, me)).wait_recv()

    @pl.when(x >= 2)
    def _():
        arrived(0, fwd1)
        copy_on.start()
        arrived(3, recv_early.at[3 - x])

    arrived(1, recv_early.at[jnp.where(x < 2, 1 - x, x - 2)])
    chosen = recv_early[x_owner]
    send2[2] = chosen[0]
    copy_y(2).start()
    send2[3] = chosen[1]
    copy_y(3).start()

    @pl.when(x < 2)
    def _():
        arrived(2, pair1.at[1 - x])
        chosen1[...] = pair1[x_owner]
        copy_chosen.start()
        arrived(4, recv_late.at[1 - x])

    @pl.when(x >= 2)
    def _():
        arrived(5, recv_late.at[0])

    chosen = recv_late[jnp.where(x < 2, x_owner, 0)]
    send2[1] = chosen[1]
    copy_y(1).start()
    recv2[yh] = chosen[0]
    for dj in (2, 1, 3):
        wait_y(dj)

    raw[...] = recv2[y_owner]
    halo_after = remote(raw, halo.at[0], h_send.at[0], h_recv.at[0], (dp, after))
    halo_before = remote(raw, halo.at[1], h_send.at[1], h_recv.at[1], (dp, before))
    halo_after.start()
    halo_before.start()

    own_rows = unfold(raw[...])
    for g in range(depth):
        field[0, depth + g] = own_rows[:, g * plane : (g + 1) * plane]
    position = lax.broadcasted_iota(jnp.int32, (PIECE, plane), 1)
    column = lax.rem(position, WIDTH_Y)
    sweeps = table_ref.shape[0]

    def smooth(k, l):
        u = field[k, l]
        north = jnp.where(position >= WIDTH_Y, pltpu.roll(u, WIDTH_Y, 1), 0.0)
        south = jnp.where(position < plane - WIDTH_Y, pltpu.roll(u, plane - WIDTH_Y, 1), 0.0)
        west = jnp.where(column > 0, pltpu.roll(u, 1, 1), 0.0)
        east = jnp.where(column < WIDTH_Y - 1, pltpu.roll(u, plane - 1, 1), 0.0)
        row = pl.ds(l - depth + 2, 1)
        updated = (
            coef[k, 0, row] * u
            + coef[k, 1, row] * ((north + south) + (west + east))
            + coef[k, 2, row] * field[k, l - 1]
            + coef[k, 3, row] * field[k, l + 1]
        )
        if k + 1 < sweeps:
            field[k + 1, l] = updated
        else:
            g = l - depth
            field[0, 3 * depth + g] = updated

    def copy_g5(place, dj, lands):
        target = at(x, lax.rem(yh + dj, 4), me)
        return remote(gath.at[x, 0], gath.at[x, lands], g5_send.at[place], g5_recv.at[lands], target)

    over_y = [copy_g5(3, 2, 3), copy_g5(1, 1, 2), copy_g5(2, 3, 1)]

    def wait_g5(place):
        remote(gath.at[x, 0], gath.at[x, place], g5_send.at[place], g5_recv.at[place], at(right, yh, me)).wait_recv()

    def copy_g6(way, source, first, last, slot):
        part_of = gath.at[source, first:last]
        return remote(part_of, part_of, g6_send.at[slot], g6_recv.at[slot], at(way, yh, me))

    rounds = [(0, 1), (1, 3), (3, 4)]
    far = lax.rem(x + 2, 4)
    to_right = [copy_g6(right, x, *span, i) for i, span in enumerate(rounds)]
    to_left = [copy_g6(left, x, *span, 3 + i) for i, span in enumerate(rounds)]
    from_left = [copy_g6(right, left, *span, i) for i, span in enumerate(rounds)]
    from_right = [copy_g6(left, right, *span, 3 + i) for i, span in enumerate(rounds)]
    to_far = [copy_g6(far, x, 1, 3, 6), copy_g6(far, x, 3, 4, 7)]
    relay = copy_g6(left, right, 0, 1, 8)
    from_far = [copy_g6(far, far, 1, 3, 6), copy_g6(far, far, 3, 4, 7), copy_g6(left, far, 0, 1, 8)]

    halo_after.wait_recv()
    halo_before.wait_recv()
    has_before = jnp.where(me > 0, 1.0, 0.0).astype(f32)
    has_after = jnp.where(me < slabs - 1, 1.0, 0.0).astype(f32)
    rows_before = unfold(halo[0]) * has_before
    rows_after = unfold(halo[1]) * has_after
    for g in range(depth):
        field[0, g] = rows_before[:, g * plane : (g + 1) * plane]
        field[0, 2 * depth + g] = rows_after[:, g * plane : (g + 1) * plane]

    for k in range(sweeps):

        @pl.loop(k + 1, 3 * depth - k - 1)
        def _(l, k=k):
            smooth(k, l)

    gath[x, 0] = fold(jnp.concatenate([field[0, 3 * depth + g] for g in range(depth)], axis=1))
    for copy in over_y + [to_right[0], to_left[0]]:
        copy.start()

    wait_g5(1)
    wait_g5(2)
    to_far[0].start()
    to_right[1].start()
    to_left[1].start()
    from_right[0].wait_recv()
    relay.start()
    wait_g5(3)
    to_far[1].start()
    to_right[2].start()
    to_left[2].start()
    for copy in (from_left[0], *from_left[1:], *from_right[1:], *from_far):
        copy.wait_recv()

    @pl.when(x >= 2)
    def _():
        wait_loads()

    data_rows = groups * GROUP
    chunk = min(CHUNK, data_rows)
    chunks = data_rows // chunk
    blocks = chunk // (2 * out_rows)
    own_chunk = lax.div(chip, blocks)

    def copy_sibling(turn):
        return remote(
            product.at[turn, 1 - core], sibling_in.at[turn], sib_send.at[turn], sib_recv.at[turn], (dp, sibling)
        )

    def copy_part(to):
        return remote(part.at[to], out_ref.at[chip], rs_send.at[0], rs_recv.at[0], (dp, 2 * to + core))

    def chunk_of(turn):
        return lax.rem(own_chunk + 1 + turn, chunks)

    def multiply(turn):
        here = chunk_of(turn)
        part_of = pl.ds(here * (chunk // GROUP), chunk // GROUP)
        pieces = gath[...].reshape(2 * PANEL, half)
        first, second = [
            lax.dot_general(
                sens[part_of, :, h * half : (h + 1) * half].reshape(chunk, half),
                pieces,
                (((1,), (1,)), ((), ())),
                preferred_element_type=f32,
            )
            for h in range(2)
        ]
        lane = lax.broadcasted_iota(jnp.int32, (chunk, PANEL), 1)
        result = jnp.where(
            lax.rem(lane, 2 * PIECE) < PIECE,
            first[:, :PANEL] + pltpu.roll(second[:, :PANEL], PANEL - PIECE, 1),
            pltpu.roll(first[:, PANEL:], PIECE, 1) + second[:, PANEL:],
        )
        result = result.reshape(blocks, 2, out_rows, PANEL)
        for c in range(2):
            product[turn, c] = result[:, c]
        copy_sibling(turn).start()

    def send_parts(turn):
        here = chunk_of(turn)
        copy_sibling(turn).wait_recv()
        total = (product[turn, core] + sibling_in[turn]) * (1.0 / math.sqrt(layers * plane))
        lane = lax.broadcasted_iota(jnp.int32, (PANEL, PANEL), 0)
        wanted = lax.broadcasted_iota(jnp.int32, (PANEL, PANEL), 1)
        from_x = lax.div(wanted, GROUP)
        dj = lax.rem(lax.div(wanted, PIECE) + 4 - yh, 4)
        place = jnp.where(dj == 2, 3, jnp.where(dj == 3, 2, dj))
        held = 64 * lax.rem(from_x, 2) + 16 * place + 8 * lax.div(from_x, 2) + lax.rem(wanted, PIECE)
        total = jnp.dot(
            total.reshape(blocks * out_rows, PANEL),
            (lane == held).astype(f32),
            precision=lax.Precision.HIGHEST,
            preferred_element_type=f32,
        ).reshape(blocks, out_rows, PANEL)
        block = here * blocks + lax.broadcasted_iota(jnp.int32, total.shape, 0)
        row = dp * data_rows + (2 * block + core) * out_rows + lax.broadcasted_iota(jnp.int32, total.shape, 1)
        col = lax.broadcasted_iota(jnp.int32, total.shape, 2)
        part[pl.ds(here * blocks, blocks)] = jnp.where(row >= start * PANEL + col, total, 0.0).astype(bf16)

        @pl.loop(0, blocks)
        def _(i):
            to = here * blocks + i

            @pl.when(to != chip)
            def _():
                copy_part(to).start()

    @pl.loop(0, chunks + 1)
    def _(turn):
        @pl.when(turn < chunks)
        def _():
            multiply(turn)

        @pl.when(turn > 0)
        def _():
            send_parts(turn - 1)

    own_part = pltpu.make_async_copy(part.at[chip], out_ref.at[chip], rs_send.at[1])
    own_part.start()

    class_after.wait_send()
    class_before.wait_send()
    halo_after.wait_send()
    halo_before.wait_send()

    @pl.when(x < 2)
    def _():
        for copy in (copy_far, copy_in, copy_mate, copy_out, copy_in_late, copy_chosen):
            copy.wait_send()

    @pl.when(x >= 2)
    def _():
        copy_on.wait_send()

    for dj in (1, 2, 3):
        copy_y(dj).wait_send()
    for copy in over_y + to_right + to_left + to_far + [relay]:
        copy.wait_send()
    for turn in range(chunks):
        copy_sibling(turn).wait_send()

    others = remote(
        part.at[0 : chips - 1], out_ref.at[0 : chips - 1], rs_send.at[0], rs_recv.at[0], (dp, sibling)
    )
    others.wait_send()
    others.wait_recv()
    own_part.wait()


def body(sensitivity, panel_index, cell_class, tear_layer, coef_table):
    rows, cells = sensitivity.shape
    depth, plane = cell_class.shape
    slabs = lax.axis_size("slab")
    out_rows = rows // slabs
    groups = rows // GROUP
    chips = slabs // 2
    chunks = max(1, rows // CHUNK)
    bf16 = jnp.bfloat16
    dma = pltpu.SemaphoreType.DMA
    sweeps = coef_table.shape[0]
    ext = -(-(depth + 4) // 8) * 8
    parts = pl.pallas_call(
        functools.partial(kernel, slabs),
        out_shape=jax.ShapeDtypeStruct((chips, out_rows, PANEL), bf16),
        in_specs=[pl.BlockSpec(memory_space=pltpu.HBM)] * 5,
        out_specs=pl.BlockSpec(memory_space=pltpu.HBM),
        scratch_shapes=[
            pltpu.SMEM(panel_index.shape, jnp.int32),
            pltpu.SMEM(coef_table.shape, jnp.float32),
            pltpu.VMEM((depth, plane), jnp.int32),
            pltpu.VMEM((1, plane), jnp.int32),
            pltpu.VMEM((groups, GROUP, cells), bf16),
            pltpu.VMEM((4, 4, 2 * PIECE, cells // 2), bf16),
            pltpu.VMEM((2, 2, 2 * PIECE, cells // 2), bf16),
            pltpu.VMEM((2, 2, 2 * PIECE, cells // 2), bf16),
            pltpu.VMEM((2, 2 * PIECE, cells // 2), bf16),
            pltpu.VMEM((2, 2, 2 * PIECE, cells // 2), bf16),
            pltpu.VMEM((2, 2 * PIECE, cells // 2), bf16),
            pltpu.VMEM((4, 2 * PIECE, cells // 2), bf16),
            pltpu.VMEM((4, 2 * PIECE, cells // 2), bf16),
            pltpu.VMEM((2 * PIECE, cells // 2), bf16),
            pltpu.VMEM((2, 2 * PIECE, cells // 2), bf16),
            pltpu.VMEM((2, depth, plane), jnp.int32),
            pltpu.VMEM((ext, plane), jnp.int32),
            pltpu.VMEM((sweeps, 4, ext, plane), jnp.float32),
            pltpu.VMEM((sweeps, 4 * depth, PIECE, plane), jnp.float32),
            pltpu.VMEM((4, 4, 2 * PIECE, cells // 2), bf16),
            pltpu.VMEM((chunks, 2, rows // chunks // (2 * out_rows), out_rows, PANEL), jnp.float32),
            pltpu.VMEM((chunks, rows // chunks // (2 * out_rows), out_rows, PANEL), jnp.float32),
            pltpu.VMEM((chips, out_rows, PANEL), bf16),
            dma((5,)),
            dma((2,)),
            dma((2,)),
            dma((6,)),
            dma((6,)),
            dma((4,)),
            dma((4,)),
            dma((2,)),
            dma((2,)),
            dma((4,)),
            dma((4,)),
            dma((9,)),
            dma((9,)),
            dma((chunks,)),
            dma((chunks,)),
            dma((2,)),
            dma((1,)),
        ],
        compiler_params=pltpu.CompilerParams(
            collective_id=0, has_side_effects=True, vmem_limit_bytes=VMEM_LIMIT
        ),
        cost_estimate=pl.CostEstimate(
            flops=2 * rows * cells * PANEL, bytes_accessed=2 * rows * cells, transcendentals=0
        ),
        name="panel",
    )(
        panel_index,
        coef_table,
        sensitivity.reshape(groups, GROUP, cells),
        cell_class,
        tear_layer.reshape(1, plane),
    )
    return parts.astype(jnp.float32).sum(axis=0)


def solution(mesh):
    return jax.shard_map(
        body,
        mesh=mesh,
        in_specs=(P("dp", "slab"), P(), P("slab", None), P(), P()),
        out_specs=P(("dp", "slab"), None),
        check_vma=False,
    )
```

```python
import functools
import math

import jax
import jax.numpy as jnp
from jax import lax
from jax.experimental import pallas as pl
from jax.experimental.pallas import tpu as pltpu
from jax.sharding import PartitionSpec as P

WIDTH_Y = 32
PANEL = 128
GROUP = 32
PIECE = 8
CHUNK = 192
VMEM_LIMIT = 63 * 1024 * 1024


def kernel(
    slabs,
    panel_hbm,
    table_hbm,
    sens_hbm,
    class_hbm,
    tear_hbm,
    out_ref,
    panel_ref,
    table_ref,
    class_ref,
    tear_ref,
    sens,
    send1,
    recv_early,
    recv_late,
    fwd1,
    pair1,
    chosen1,
    send2,
    recv2,
    raw,
    halo,
    class_halo,
    class_ext,
    coef,
    field,
    gath,
    product,
    sibling_in,
    part,
    load_sem,
    class_send,
    class_recv,
    s1_send,
    s1_recv,
    s2_send,
    s2_recv,
    h_send,
    h_recv,
    g5_send,
    g5_recv,
    g6_send,
    g6_recv,
    sib_send,
    sib_recv,
    rs_send,
    rs_recv,
):
    f32 = jnp.float32
    bf16 = jnp.bfloat16
    dp = lax.axis_index("dp")
    me = lax.axis_index("slab")
    x = lax.div(dp, 4)
    yh = lax.rem(dp, 4)
    groups, _, cells = sens.shape
    chips = slabs // 2
    core = lax.rem(me, 2)
    half = cells // 2
    chip = lax.div(me, 2)
    sibling = me + 1 - 2 * core
    depth, plane = class_ref.shape
    layers = depth * slabs
    out_rows = out_ref.shape[1]
    panels_dev = groups * GROUP // PANEL
    right = lax.rem(x + 1, 4)
    left = lax.rem(x + 3, 4)
    before = lax.rem(me + slabs - 1, slabs)
    after = lax.rem(me + 1, slabs)

    def at(x_to, y_to, slab_to):
        return (x_to * 4 + y_to, slab_to)

    def fold(rows):
        return jnp.concatenate([rows[:, :half], rows[:, half:]], axis=0).astype(bf16)

    def unfold(piece):
        piece = piece.astype(f32)
        return jnp.concatenate([piece[:PIECE], piece[PIECE:]], axis=1)

    def remote(src, dst, send_sem, recv_sem, target):
        return pltpu.make_async_remote_copy(
            src_ref=src,
            dst_ref=dst,
            send_sem=send_sem,
            recv_sem=recv_sem,
            device_id=target,
            device_id_type=pl.DeviceIdType.MESH,
        )

    loads = 4

    def load(i):
        part_of = pl.ds(i * (groups // loads), groups // loads)
        return pltpu.make_async_copy(sens_hbm.at[part_of], sens.at[part_of], load_sem.at[0])

    small = [
        pltpu.make_async_copy(source, target, load_sem.at[1 + i])
        for i, (source, target) in enumerate(
            [(class_hbm, class_ref), (tear_hbm, tear_ref), (table_hbm, table_ref), (panel_hbm, panel_ref)]
        )
    ]
    barrier = pltpu.get_barrier_semaphore()

    def start_loads():
        for i in range(loads):
            load(i).start()

    def wait_loads():
        pltpu.make_async_copy(sens_hbm, sens, load_sem.at[0]).wait()

    for copy in small:
        copy.start()

    @pl.when(x < 2)
    def _():
        start_loads()

    def greet(target):
        pl.semaphore_signal(
            barrier, inc=1, device_id=target, device_id_type=pl.DeviceIdType.MESH
        )

    for d in sorted(range(1, chips), key=lambda d: -min(d, chips - d)):
        greet((dp, lax.rem(me + 2 * d, slabs)))

    for dj in (2, 1, 3):
        greet(at(x, lax.rem(yh + dj, 4), me))
    greet((dp, before))
    greet((dp, after))
    greet(at(right, yh, me))
    greet(at(left, yh, me))
    greet(at(lax.rem(x + 2, 4), yh, me))

    @pl.when(x >= 2)
    def _():
        start_loads()

    for copy in small:
        copy.wait()

    start = panel_ref[0]
    owner = lax.div(start, panels_dev)
    x_owner = lax.div(owner, 4)
    y_owner = lax.rem(owner, 4)
    first_group = lax.rem(start, panels_dev) * 4

    @pl.when(x < 2)
    def _():
        wait_loads()
        for q in range(4):
            rows = sens[first_group + q].astype(f32)
            for j in range(4):
                send1[q, lax.rem(j - yh + 6, 4)] = fold(rows[j * PIECE : (j + 1) * PIECE])

    pl.semaphore_wait(barrier, 8 + chips - 1)

    def early(q):
        return send1.at[q, 0:2]

    def late(q):
        return send1.at[q, 2:4]

    mate = at(1 - x, yh, me)
    outer = at(3 - x, yh, me)
    copy_far = remote(early(x + 2), fwd1, s1_send.at[0], s1_recv.at[0], outer)
    copy_in = remote(early(1 - x), recv_early.at[x], s1_send.at[1], s1_recv.at[1], mate)
    copy_mate = remote(late(x + 2), pair1.at[x], s1_send.at[2], s1_recv.at[2], mate)
    copy_out = remote(early(3 - x), recv_early.at[x], s1_send.at[3], s1_recv.at[3], outer)
    copy_in_late = remote(late(1 - x), recv_late.at[x], s1_send.at[4], s1_recv.at[4], mate)
    copy_chosen = remote(chosen1, recv_late.at[0], s1_send.at[5], s1_recv.at[5], outer)
    copy_on = remote(fwd1, recv_early.at[3 - x], s1_send.at[1], s1_recv.at[1], at(5 - x, yh, me))

    def arrived(slot, to):
        remote(to, to, s1_send.at[slot], s1_recv.at[slot], at(right, yh, me)).wait_recv()

    @pl.when(x < 2)
    def _():
        for copy in (copy_far, copy_mate, copy_in, copy_out, copy_in_late):
            copy.start()
        recv_early[x] = send1[x, 0:2]
        recv_late[x] = send1[x, 2:4]
        pair1[x] = send1[3 - x, 2:4]

    class_after = remote(class_ref, class_halo.at[0], class_send.at[0], class_recv.at[0], (dp, after))
    class_before = remote(class_ref, class_halo.at[1], class_send.at[1], class_recv.at[1], (dp, before))
    class_after.start()
    class_before.start()

    class_after.wait_recv()
    class_before.wait_recv()
    class_ext[0:2] = class_halo[0, depth - 2 : depth]
    class_ext[2 : 2 + depth] = class_ref[...]
    class_ext[2 + depth : 4 + depth] = class_halo[1, 0:2]
    class_ext[4 + depth :] = jnp.zeros_like(class_ext[4 + depth :])
    classes = class_ext[...]
    layer = me * depth - 2 + lax.broadcasted_iota(jnp.int32, classes.shape, 0)
    valid = (layer >= 0) & (layer < layers)
    tear = jnp.broadcast_to(tear_ref[...], classes.shape)
    open_up = tear != layer
    open_down = tear != layer + 1
    for k in range(table_ref.shape[0]):
        a = jnp.zeros(classes.shape, f32)
        b = jnp.zeros(classes.shape, f32)
        for level in range(table_ref.shape[2]):
            a = jnp.where(classes == level, table_ref[k, 0, level], a)
            b = jnp.where(classes == level, table_ref[k, 1, level], b)
        a = jnp.where(valid, a, 0.0)
        b = jnp.where(valid, 4.0 * b, 0.0)
        up = jnp.where(open_up, b, 0.0)
        down = jnp.where(open_down, b, 0.0)
        coef[k, 0] = 1.0 - 4.0 * a - up - down
        coef[k, 1] = a
        coef[k, 2] = up
        coef[k, 3] = down

    def copy_y(dj):
        return remote(
            send2.at[dj], recv2.at[yh], s2_send.at[dj], s2_recv.at[yh], at(x, lax.rem(yh + dj, 4), me)
        )

    def wait_y(dj):
        j = lax.rem(yh + dj, 4)
        remote(send2.at[dj], recv2.at[j], s2_send.at[dj], s2_recv.at[j], at(x, j, me)).wait_recv()

    @pl.when(x >= 2)
    def _():
        arrived(0, fwd1)
        copy_on.start()
        arrived(3, recv_early.at[3 - x])

    arrived(1, recv_early.at[jnp.where(x < 2, 1 - x, x - 2)])
    chosen = recv_early[x_owner]
    send2[2] = chosen[0]
    copy_y(2).start()
    send2[3] = chosen[1]
    copy_y(3).start()

    @pl.when(x < 2)
    def _():
        arrived(2, pair1.at[1 - x])
        chosen1[...] = pair1[x_owner]
        copy_chosen.start()
        arrived(4, recv_late.at[1 - x])

    @pl.when(x >= 2)
    def _():
        arrived(5, recv_late.at[0])

    chosen = recv_late[jnp.where(x < 2, x_owner, 0)]
    send2[1] = chosen[1]
    copy_y(1).start()
    recv2[yh] = chosen[0]
    for dj in (2, 1, 3):
        wait_y(dj)

    raw[...] = recv2[y_owner]
    halo_after = remote(raw, halo.at[0], h_send.at[0], h_recv.at[0], (dp, after))
    halo_before = remote(raw, halo.at[1], h_send.at[1], h_recv.at[1], (dp, before))
    halo_after.start()
    halo_before.start()

    own_rows = unfold(raw[...])
    for g in range(depth):
        field[0, depth + g] = own_rows[:, g * plane : (g + 1) * plane]
    position = lax.broadcasted_iota(jnp.int32, (PIECE, plane), 1)
    column = lax.rem(position, WIDTH_Y)
    sweeps = table_ref.shape[0]

    def smooth(k, l):
        u = field[k, l]
        north = jnp.where(position >= WIDTH_Y, pltpu.roll(u, WIDTH_Y, 1), 0.0)
        south = jnp.where(position < plane - WIDTH_Y, pltpu.roll(u, plane - WIDTH_Y, 1), 0.0)
        west = jnp.where(column > 0, pltpu.roll(u, 1, 1), 0.0)
        east = jnp.where(column < WIDTH_Y - 1, pltpu.roll(u, plane - 1, 1), 0.0)
        e = l - depth + 2
        updated = (
            coef[k, 0, e : e + 1] * u
            + coef[k, 1, e : e + 1] * ((north + south) + (west + east))
            + coef[k, 2, e : e + 1] * field[k, l - 1]
            + coef[k, 3, e : e + 1] * field[k, l + 1]
        )
        if k + 1 < sweeps:
            field[k + 1, l] = updated
        else:
            g = l - depth
            field[0, 3 * depth + g] = updated

    def copy_g5(place, dj, lands):
        target = at(x, lax.rem(yh + dj, 4), me)
        return remote(gath.at[x, 0], gath.at[x, lands], g5_send.at[place], g5_recv.at[lands], target)

    over_y = [copy_g5(1, 1, 2), copy_g5(2, 3, 1), copy_g5(3, 2, 3)]

    def wait_g5(place):
        remote(gath.at[x, 0], gath.at[x, place], g5_send.at[place], g5_recv.at[place], at(right, yh, me)).wait_recv()

    def copy_g6(way, source, first, last, slot):
        part_of = gath.at[source, first:last]
        return remote(part_of, part_of, g6_send.at[slot], g6_recv.at[slot], at(way, yh, me))

    rounds = [(0, 1), (1, 3), (3, 4)]
    far = lax.rem(x + 2, 4)
    to_right = [copy_g6(right, x, *span, i) for i, span in enumerate(rounds)]
    to_left = [copy_g6(left, x, *span, 3 + i) for i, span in enumerate(rounds)]
    from_left = [copy_g6(right, left, *span, i) for i, span in enumerate(rounds)]
    from_right = [copy_g6(left, right, *span, 3 + i) for i, span in enumerate(rounds)]
    relays = [copy_g6(right, left, 0, 2, 6), copy_g6(left, right, 2, 3, 7)]
    to_far = copy_g6(far, x, 3, 4, 8)
    relayed = [copy_g6(right, far, 0, 2, 6), copy_g6(left, far, 2, 3, 7), copy_g6(far, far, 3, 4, 8)]

    inner = [(0, l) for l in range(depth + 1, 2 * depth - 1)]
    done = set(inner)
    for k, l in inner:
        smooth(k, l)

    halo_after.wait_recv()
    halo_before.wait_recv()
    has_before = jnp.where(me > 0, 1.0, 0.0).astype(f32)
    has_after = jnp.where(me < slabs - 1, 1.0, 0.0).astype(f32)
    rows_before = unfold(halo[0]) * has_before
    rows_after = unfold(halo[1]) * has_after
    for g in range(depth):
        field[0, g] = rows_before[:, g * plane : (g + 1) * plane]
        field[0, 2 * depth + g] = rows_after[:, g * plane : (g + 1) * plane]

    def smooth_all(k, l):
        if k < 0 or (k, l) in done:
            return
        for near in (l - 1, l, l + 1):
            smooth_all(k - 1, near)
        smooth(k, l)
        done.add((k, l))

    for t in range(depth):
        smooth_all(sweeps - 1, depth + t)
    gath[x, 0] = fold(jnp.concatenate([field[0, 3 * depth + g] for g in range(depth)], axis=1))
    for copy in [*over_y[:2], to_right[0], to_left[0], over_y[2]]:
        copy.start()

    wait_g5(1)
    wait_g5(2)
    to_right[1].start()
    to_left[1].start()
    wait_g5(3)
    to_far.start()
    to_right[2].start()
    to_left[2].start()
    from_left[0].wait_recv()
    from_left[1].wait_recv()
    relays[0].start()
    from_right[0].wait_recv()
    from_right[1].wait_recv()
    relays[1].start()
    for copy in (from_left[2], from_right[2], *relayed):
        copy.wait_recv()

    @pl.when(x >= 2)
    def _():
        wait_loads()

    data_rows = groups * GROUP
    chunk = min(CHUNK, data_rows)
    chunks = data_rows // chunk
    blocks = chunk // (2 * out_rows)
    own_chunk = lax.div(chip, blocks)

    def copy_sibling(turn):
        return remote(
            product.at[turn, 1 - core], sibling_in.at[turn], sib_send.at[turn], sib_recv.at[turn], (dp, sibling)
        )

    def copy_part(to):
        return remote(part.at[to], out_ref.at[chip], rs_send.at[0], rs_recv.at[0], (dp, 2 * to + core))

    def chunk_of(turn):
        return lax.rem(own_chunk + 1 + turn, chunks)

    def multiply(turn):
        here = chunk_of(turn)
        part_of = pl.ds(here * (chunk // GROUP), chunk // GROUP)
        pieces = gath[...].reshape(2 * PANEL, half)
        first, second = [
            lax.dot_general(
                sens[part_of, :, h * half : (h + 1) * half].reshape(chunk, half),
                pieces,
                (((1,), (1,)), ((), ())),
                preferred_element_type=f32,
            )
            for h in range(2)
        ]
        lane = lax.broadcasted_iota(jnp.int32, (chunk, PANEL), 1)
        result = jnp.where(
            lax.rem(lane, 2 * PIECE) < PIECE,
            first[:, :PANEL] + pltpu.roll(second[:, :PANEL], PANEL - PIECE, 1),
            pltpu.roll(first[:, PANEL:], PIECE, 1) + second[:, PANEL:],
        )
        result = result.reshape(blocks, 2, out_rows, PANEL)
        for c in range(2):
            product[turn, c] = result[:, c]
        copy_sibling(turn).start()

    def send_parts(turn):
        here = chunk_of(turn)
        copy_sibling(turn).wait_recv()
        total = (product[turn, core] + sibling_in[turn]) * (1.0 / math.sqrt(layers * plane))
        lane = lax.broadcasted_iota(jnp.int32, (PANEL, PANEL), 0)
        wanted = lax.broadcasted_iota(jnp.int32, (PANEL, PANEL), 1)
        from_x = lax.div(wanted, GROUP)
        dj = lax.rem(lax.div(wanted, PIECE) + 4 - yh, 4)
        place = jnp.where(dj == 2, 3, jnp.where(dj == 3, 2, dj))
        held = 64 * lax.rem(from_x, 2) + 16 * place + 8 * lax.div(from_x, 2) + lax.rem(wanted, PIECE)
        total = jnp.dot(
            total.reshape(blocks * out_rows, PANEL),
            (lane == held).astype(f32),
            precision=lax.Precision.HIGHEST,
            preferred_element_type=f32,
        ).reshape(blocks, out_rows, PANEL)
        block = here * blocks + lax.broadcasted_iota(jnp.int32, total.shape, 0)
        row = dp * data_rows + (2 * block + core) * out_rows + lax.broadcasted_iota(jnp.int32, total.shape, 1)
        col = lax.broadcasted_iota(jnp.int32, total.shape, 2)
        part[pl.ds(here * blocks, blocks)] = jnp.where(row >= start * PANEL + col, total, 0.0).astype(bf16)
        for i in range(blocks):
            to = here * blocks + i

            @pl.when(to != chip)
            def _(to=to):
                copy_part(to).start()

    for turn in range(chunks):
        multiply(turn)
        if turn > 0:
            send_parts(turn - 1)
    send_parts(chunks - 1)
    own_part = pltpu.make_async_copy(part.at[chip], out_ref.at[chip], rs_send.at[1])
    own_part.start()

    class_after.wait_send()
    class_before.wait_send()
    halo_after.wait_send()
    halo_before.wait_send()

    @pl.when(x < 2)
    def _():
        for copy in (copy_far, copy_in, copy_mate, copy_out, copy_in_late, copy_chosen):
            copy.wait_send()

    @pl.when(x >= 2)
    def _():
        copy_on.wait_send()

    for dj in (1, 2, 3):
        copy_y(dj).wait_send()
    for copy in over_y + to_right + to_left + relays + [to_far]:
        copy.wait_send()
    for turn in range(chunks):
        copy_sibling(turn).wait_send()

    others = remote(
        part.at[0 : chips - 1], out_ref.at[0 : chips - 1], rs_send.at[0], rs_recv.at[0], (dp, sibling)
    )
    others.wait_send()
    others.wait_recv()
    own_part.wait()


def body(sensitivity, panel_index, cell_class, tear_layer, coef_table):
    rows, cells = sensitivity.shape
    depth, plane = cell_class.shape
    slabs = lax.axis_size("slab")
    out_rows = rows // slabs
    groups = rows // GROUP
    chips = slabs // 2
    chunks = max(1, rows // CHUNK)
    bf16 = jnp.bfloat16
    dma = pltpu.SemaphoreType.DMA
    sweeps = coef_table.shape[0]
    ext = -(-(depth + 4) // 8) * 8
    parts = pl.pallas_call(
        functools.partial(kernel, slabs),
        out_shape=jax.ShapeDtypeStruct((chips, out_rows, PANEL), bf16),
        in_specs=[pl.BlockSpec(memory_space=pltpu.HBM)] * 5,
        out_specs=pl.BlockSpec(memory_space=pltpu.HBM),
        scratch_shapes=[
            pltpu.SMEM(panel_index.shape, jnp.int32),
            pltpu.SMEM(coef_table.shape, jnp.float32),
            pltpu.VMEM((depth, plane), jnp.int32),
            pltpu.VMEM((1, plane), jnp.int32),
            pltpu.VMEM((groups, GROUP, cells), bf16),
            pltpu.VMEM((4, 4, 2 * PIECE, cells // 2), bf16),
            pltpu.VMEM((2, 2, 2 * PIECE, cells // 2), bf16),
            pltpu.VMEM((2, 2, 2 * PIECE, cells // 2), bf16),
            pltpu.VMEM((2, 2 * PIECE, cells // 2), bf16),
            pltpu.VMEM((2, 2, 2 * PIECE, cells // 2), bf16),
            pltpu.VMEM((2, 2 * PIECE, cells // 2), bf16),
            pltpu.VMEM((4, 2 * PIECE, cells // 2), bf16),
            pltpu.VMEM((4, 2 * PIECE, cells // 2), bf16),
            pltpu.VMEM((2 * PIECE, cells // 2), bf16),
            pltpu.VMEM((2, 2 * PIECE, cells // 2), bf16),
            pltpu.VMEM((2, depth, plane), jnp.int32),
            pltpu.VMEM((ext, plane), jnp.int32),
            pltpu.VMEM((sweeps, 4, ext, plane), jnp.float32),
            pltpu.VMEM((sweeps, 4 * depth, PIECE, plane), jnp.float32),
            pltpu.VMEM((4, 4, 2 * PIECE, cells // 2), bf16),
            pltpu.VMEM((chunks, 2, rows // chunks // (2 * out_rows), out_rows, PANEL), jnp.float32),
            pltpu.VMEM((chunks, rows // chunks // (2 * out_rows), out_rows, PANEL), jnp.float32),
            pltpu.VMEM((chips, out_rows, PANEL), bf16),
            dma((5,)),
            dma((2,)),
            dma((2,)),
            dma((6,)),
            dma((6,)),
            dma((4,)),
            dma((4,)),
            dma((2,)),
            dma((2,)),
            dma((4,)),
            dma((4,)),
            dma((9,)),
            dma((9,)),
            dma((chunks,)),
            dma((chunks,)),
            dma((2,)),
            dma((1,)),
        ],
        compiler_params=pltpu.CompilerParams(
            collective_id=0, has_side_effects=True, vmem_limit_bytes=VMEM_LIMIT
        ),
        cost_estimate=pl.CostEstimate(
            flops=2 * rows * cells * PANEL, bytes_accessed=2 * rows * cells, transcendentals=0
        ),
        name="panel",
    )(
        panel_index,
        coef_table,
        sensitivity.reshape(groups, GROUP, cells),
        cell_class,
        tear_layer.reshape(1, plane),
    )
    return parts.astype(jnp.float32).sum(axis=0)


def solution(mesh):
    return jax.shard_map(
        body,
        mesh=mesh,
        in_specs=(P("dp", "slab"), P(), P("slab", None), P(), P()),
        out_specs=P(("dp", "slab"), None),
        check_vma=False,
    )
```

```python
import functools
import math

import jax
import jax.numpy as jnp
from jax import lax
from jax.experimental import pallas as pl
from jax.experimental.pallas import tpu as pltpu
from jax.sharding import PartitionSpec as P

WIDTH_Y = 32
PANEL = 128
GROUP = 32
PIECE = 8
CHUNK = 192
VMEM_LIMIT = 63 * 1024 * 1024


def kernel(
    slabs,
    panel_hbm,
    table_hbm,
    sens_hbm,
    class_hbm,
    tear_hbm,
    out_ref,
    panel_ref,
    table_ref,
    class_ref,
    tear_ref,
    sens,
    send1,
    recv_early,
    recv_late,
    fwd1,
    pair1,
    chosen1,
    send2,
    recv2,
    raw,
    halo,
    class_halo,
    class_ext,
    coef,
    field,
    gath,
    product,
    sibling_in,
    part,
    load_sem,
    class_send,
    class_recv,
    s1_send,
    s1_recv,
    s2_send,
    s2_recv,
    h_send,
    h_recv,
    g5_send,
    g5_recv,
    g6_send,
    g6_recv,
    sib_send,
    sib_recv,
    rs_send,
    rs_recv,
):
    f32 = jnp.float32
    bf16 = jnp.bfloat16
    dp = lax.axis_index("dp")
    me = lax.axis_index("slab")
    x = lax.div(dp, 4)
    yh = lax.rem(dp, 4)
    groups, _, cells = sens.shape
    chips = slabs // 2
    core = lax.rem(me, 2)
    half = cells // 2
    chip = lax.div(me, 2)
    sibling = me + 1 - 2 * core
    depth, plane = class_ref.shape
    layers = depth * slabs
    out_rows = out_ref.shape[1]
    panels_dev = groups * GROUP // PANEL
    right = lax.rem(x + 1, 4)
    left = lax.rem(x + 3, 4)
    before = lax.rem(me + slabs - 1, slabs)
    after = lax.rem(me + 1, slabs)

    def at(x_to, y_to, slab_to):
        return (x_to * 4 + y_to, slab_to)

    def fold(rows):
        return jnp.concatenate([rows[:, :half], rows[:, half:]], axis=0).astype(bf16)

    def unfold(piece):
        piece = piece.astype(f32)
        return jnp.concatenate([piece[:PIECE], piece[PIECE:]], axis=1)

    def remote(src, dst, send_sem, recv_sem, target):
        return pltpu.make_async_remote_copy(
            src_ref=src,
            dst_ref=dst,
            send_sem=send_sem,
            recv_sem=recv_sem,
            device_id=target,
            device_id_type=pl.DeviceIdType.MESH,
        )

    loads = 4

    def load(i):
        part_of = pl.ds(i * (groups // loads), groups // loads)
        return pltpu.make_async_copy(sens_hbm.at[part_of], sens.at[part_of], load_sem.at[0])

    small = [
        pltpu.make_async_copy(source, target, load_sem.at[1 + i])
        for i, (source, target) in enumerate(
            [(class_hbm, class_ref), (tear_hbm, tear_ref), (table_hbm, table_ref), (panel_hbm, panel_ref)]
        )
    ]
    barrier = pltpu.get_barrier_semaphore()

    def start_loads():
        for i in range(loads):
            load(i).start()

    def wait_loads():
        pltpu.make_async_copy(sens_hbm, sens, load_sem.at[0]).wait()

    for copy in small:
        copy.start()

    @pl.when(x < 2)
    def _():
        start_loads()

    def greet(target):
        pl.semaphore_signal(
            barrier, inc=1, device_id=target, device_id_type=pl.DeviceIdType.MESH
        )

    for d in sorted(range(1, chips), key=lambda d: -min(d, chips - d)):
        greet((dp, lax.rem(me + 2 * d, slabs)))

    for dj in (2, 1, 3):
        greet(at(x, lax.rem(yh + dj, 4), me))
    greet((dp, before))
    greet((dp, after))
    greet(at(right, yh, me))
    greet(at(left, yh, me))
    greet(at(lax.rem(x + 2, 4), yh, me))

    @pl.when(x >= 2)
    def _():
        start_loads()

    for copy in small:
        copy.wait()

    start = panel_ref[0]
    owner = lax.div(start, panels_dev)
    x_owner = lax.div(owner, 4)
    y_owner = lax.rem(owner, 4)
    first_group = lax.rem(start, panels_dev) * 4

    @pl.when(x < 2)
    def _():
        wait_loads()
        for q in range(4):
            rows = sens[first_group + q].astype(f32)
            for j in range(4):
                send1[q, lax.rem(j - yh + 6, 4)] = fold(rows[j * PIECE : (j + 1) * PIECE])

    pl.semaphore_wait(barrier, 8 + chips - 1)

    def early(q):
        return send1.at[q, 0:2]

    def late(q):
        return send1.at[q, 2:4]

    mate = at(1 - x, yh, me)
    outer = at(3 - x, yh, me)
    copy_far = remote(early(x + 2), fwd1, s1_send.at[0], s1_recv.at[0], outer)
    copy_in = remote(early(1 - x), recv_early.at[x], s1_send.at[1], s1_recv.at[1], mate)
    copy_mate = remote(late(x + 2), pair1.at[x], s1_send.at[2], s1_recv.at[2], mate)
    copy_out = remote(early(3 - x), recv_early.at[x], s1_send.at[3], s1_recv.at[3], outer)
    copy_in_late = remote(late(1 - x), recv_late.at[x], s1_send.at[4], s1_recv.at[4], mate)
    copy_chosen = remote(chosen1, recv_late.at[0], s1_send.at[5], s1_recv.at[5], outer)
    copy_on = remote(fwd1, recv_early.at[3 - x], s1_send.at[1], s1_recv.at[1], at(5 - x, yh, me))

    def arrived(slot, to):
        remote(to, to, s1_send.at[slot], s1_recv.at[slot], at(right, yh, me)).wait_recv()

    @pl.when(x < 2)
    def _():
        for copy in (copy_far, copy_mate, copy_in, copy_out, copy_in_late):
            copy.start()
        recv_early[x] = send1[x, 0:2]
        recv_late[x] = send1[x, 2:4]
        pair1[x] = send1[3 - x, 2:4]

    class_after = remote(class_ref, class_halo.at[0], class_send.at[0], class_recv.at[0], (dp, after))
    class_before = remote(class_ref, class_halo.at[1], class_send.at[1], class_recv.at[1], (dp, before))
    class_after.start()
    class_before.start()

    class_after.wait_recv()
    class_before.wait_recv()
    class_ext[0:2] = class_halo[0, depth - 2 : depth]
    class_ext[2 : 2 + depth] = class_ref[...]
    class_ext[2 + depth : 4 + depth] = class_halo[1, 0:2]
    class_ext[4 + depth :] = jnp.zeros_like(class_ext[4 + depth :])
    classes = class_ext[...]
    layer = me * depth - 2 + lax.broadcasted_iota(jnp.int32, classes.shape, 0)
    valid = (layer >= 0) & (layer < layers)
    tear = jnp.broadcast_to(tear_ref[...], classes.shape)
    open_up = tear != layer
    open_down = tear != layer + 1
    for k in range(table_ref.shape[0]):
        a = jnp.zeros(classes.shape, f32)
        b = jnp.zeros(classes.shape, f32)
        for level in range(table_ref.shape[2]):
            a = jnp.where(classes == level, table_ref[k, 0, level], a)
            b = jnp.where(classes == level, table_ref[k, 1, level], b)
        a = jnp.where(valid, a, 0.0)
        b = jnp.where(valid, 4.0 * b, 0.0)
        up = jnp.where(open_up, b, 0.0)
        down = jnp.where(open_down, b, 0.0)
        coef[k, 0] = 1.0 - 4.0 * a - up - down
        coef[k, 1] = a
        coef[k, 2] = up
        coef[k, 3] = down

    def copy_y(dj):
        return remote(
            send2.at[dj], recv2.at[yh], s2_send.at[dj], s2_recv.at[yh], at(x, lax.rem(yh + dj, 4), me)
        )

    def wait_y(dj):
        j = lax.rem(yh + dj, 4)
        remote(send2.at[dj], recv2.at[j], s2_send.at[dj], s2_recv.at[j], at(x, j, me)).wait_recv()

    @pl.when(x >= 2)
    def _():
        arrived(0, fwd1)
        copy_on.start()
        arrived(3, recv_early.at[3 - x])

    arrived(1, recv_early.at[jnp.where(x < 2, 1 - x, x - 2)])
    chosen = recv_early[x_owner]
    send2[2] = chosen[0]
    copy_y(2).start()
    send2[3] = chosen[1]
    copy_y(3).start()

    @pl.when(x < 2)
    def _():
        arrived(2, pair1.at[1 - x])
        chosen1[...] = pair1[x_owner]
        copy_chosen.start()
        arrived(4, recv_late.at[1 - x])

    @pl.when(x >= 2)
    def _():
        arrived(5, recv_late.at[0])

    chosen = recv_late[jnp.where(x < 2, x_owner, 0)]
    send2[1] = chosen[1]
    copy_y(1).start()
    recv2[yh] = chosen[0]
    for dj in (2, 1, 3):
        wait_y(dj)

    raw[...] = recv2[y_owner]
    halo_after = remote(raw, halo.at[0], h_send.at[0], h_recv.at[0], (dp, after))
    halo_before = remote(raw, halo.at[1], h_send.at[1], h_recv.at[1], (dp, before))
    halo_after.start()
    halo_before.start()

    own_rows = unfold(raw[...])
    for g in range(depth):
        field[0, depth + g] = own_rows[:, g * plane : (g + 1) * plane]
    position = lax.broadcasted_iota(jnp.int32, (PIECE, plane), 1)
    column = lax.rem(position, WIDTH_Y)
    sweeps = table_ref.shape[0]

    def smooth(k, l):
        u = field[k, l]
        north = jnp.where(position >= WIDTH_Y, pltpu.roll(u, WIDTH_Y, 1), 0.0)
        south = jnp.where(position < plane - WIDTH_Y, pltpu.roll(u, plane - WIDTH_Y, 1), 0.0)
        west = jnp.where(column > 0, pltpu.roll(u, 1, 1), 0.0)
        east = jnp.where(column < WIDTH_Y - 1, pltpu.roll(u, plane - 1, 1), 0.0)
        e = l - depth + 2
        updated = (
            coef[k, 0, e : e + 1] * u
            + coef[k, 1, e : e + 1] * ((north + south) + (west + east))
            + coef[k, 2, e : e + 1] * field[k, l - 1]
            + coef[k, 3, e : e + 1] * field[k, l + 1]
        )
        if k + 1 < sweeps:
            field[k + 1, l] = updated
        else:
            g = l - depth
            field[0, 3 * depth + g] = updated

    def copy_g5(place, dj, lands):
        target = at(x, lax.rem(yh + dj, 4), me)
        return remote(gath.at[x, 0], gath.at[x, lands], g5_send.at[place], g5_recv.at[lands], target)

    over_y = [copy_g5(1, 1, 2), copy_g5(2, 3, 1), copy_g5(3, 2, 3)]

    def wait_g5(place):
        remote(gath.at[x, 0], gath.at[x, place], g5_send.at[place], g5_recv.at[place], at(right, yh, me)).wait_recv()

    def copy_g6(way, source, first, last, slot):
        part_of = gath.at[source, first:last]
        return remote(part_of, part_of, g6_send.at[slot], g6_recv.at[slot], at(way, yh, me))

    rounds = [(0, 1), (1, 3), (3, 4)]
    far = lax.rem(x + 2, 4)
    to_right = [copy_g6(right, x, *span, i) for i, span in enumerate(rounds)]
    to_left = [copy_g6(left, x, *span, 3 + i) for i, span in enumerate(rounds)]
    from_left = [copy_g6(right, left, *span, i) for i, span in enumerate(rounds)]
    from_right = [copy_g6(left, right, *span, 3 + i) for i, span in enumerate(rounds)]
    relays = [copy_g6(right, left, 0, 1, 6), copy_g6(right, left, 1, 2, 9), copy_g6(left, right, 2, 3, 7)]
    to_far = copy_g6(far, x, 3, 4, 8)
    relayed = [
        copy_g6(right, far, 0, 1, 6),
        copy_g6(right, far, 1, 2, 9),
        copy_g6(left, far, 2, 3, 7),
        copy_g6(far, far, 3, 4, 8),
    ]

    inner = [(0, l) for l in range(depth + 1, 2 * depth - 1)]
    done = set(inner)
    for k, l in inner:
        smooth(k, l)

    halo_after.wait_recv()
    halo_before.wait_recv()
    has_before = jnp.where(me > 0, 1.0, 0.0).astype(f32)
    has_after = jnp.where(me < slabs - 1, 1.0, 0.0).astype(f32)
    rows_before = unfold(halo[0]) * has_before
    rows_after = unfold(halo[1]) * has_after
    for g in range(depth):
        field[0, g] = rows_before[:, g * plane : (g + 1) * plane]
        field[0, 2 * depth + g] = rows_after[:, g * plane : (g + 1) * plane]

    def smooth_all(k, l):
        if k < 0 or (k, l) in done:
            return
        for near in (l - 1, l, l + 1):
            smooth_all(k - 1, near)
        smooth(k, l)
        done.add((k, l))

    for t in range(depth):
        smooth_all(sweeps - 1, depth + t)
    gath[x, 0] = fold(jnp.concatenate([field[0, 3 * depth + g] for g in range(depth)], axis=1))
    for copy in [*over_y[:2], to_right[0], to_left[0], over_y[2]]:
        copy.start()

    from_left[0].wait_recv()
    relays[0].start()
    wait_g5(1)
    wait_g5(2)
    to_right[1].start()
    to_left[1].start()
    wait_g5(3)
    to_far.start()
    to_right[2].start()
    to_left[2].start()
    from_left[1].wait_recv()
    relays[1].start()
    from_right[0].wait_recv()
    from_right[1].wait_recv()
    relays[2].start()
    for copy in (from_left[2], from_right[2], *relayed):
        copy.wait_recv()

    @pl.when(x >= 2)
    def _():
        wait_loads()

    data_rows = groups * GROUP
    chunk = min(CHUNK, data_rows)
    chunks = data_rows // chunk
    blocks = chunk // (2 * out_rows)
    own_chunk = lax.div(chip, blocks)

    def copy_sibling(turn):
        return remote(
            product.at[turn, 1 - core], sibling_in.at[turn], sib_send.at[turn], sib_recv.at[turn], (dp, sibling)
        )

    def copy_part(to):
        return remote(part.at[to], out_ref.at[chip], rs_send.at[0], rs_recv.at[0], (dp, 2 * to + core))

    def chunk_of(turn):
        return lax.rem(own_chunk + 1 + turn, chunks)

    def multiply(turn):
        here = chunk_of(turn)
        part_of = pl.ds(here * (chunk // GROUP), chunk // GROUP)
        pieces = gath[...].reshape(2 * PANEL, half)
        first, second = [
            lax.dot_general(
                sens[part_of, :, h * half : (h + 1) * half].reshape(chunk, half),
                pieces,
                (((1,), (1,)), ((), ())),
                preferred_element_type=f32,
            )
            for h in range(2)
        ]
        lane = lax.broadcasted_iota(jnp.int32, (chunk, PANEL), 1)
        result = jnp.where(
            lax.rem(lane, 2 * PIECE) < PIECE,
            first[:, :PANEL] + pltpu.roll(second[:, :PANEL], PANEL - PIECE, 1),
            pltpu.roll(first[:, PANEL:], PIECE, 1) + second[:, PANEL:],
        )
        result = result.reshape(blocks, 2, out_rows, PANEL)
        for c in range(2):
            product[turn, c] = result[:, c]
        copy_sibling(turn).start()

    def send_parts(turn):
        here = chunk_of(turn)
        copy_sibling(turn).wait_recv()
        total = (product[turn, core] + sibling_in[turn]) * (1.0 / math.sqrt(layers * plane))
        lane = lax.broadcasted_iota(jnp.int32, (PANEL, PANEL), 0)
        wanted = lax.broadcasted_iota(jnp.int32, (PANEL, PANEL), 1)
        from_x = lax.div(wanted, GROUP)
        dj = lax.rem(lax.div(wanted, PIECE) + 4 - yh, 4)
        place = jnp.where(dj == 2, 3, jnp.where(dj == 3, 2, dj))
        held = 64 * lax.rem(from_x, 2) + 16 * place + 8 * lax.div(from_x, 2) + lax.rem(wanted, PIECE)
        total = jnp.dot(
            total.reshape(blocks * out_rows, PANEL),
            (lane == held).astype(f32),
            precision=lax.Precision.HIGHEST,
            preferred_element_type=f32,
        ).reshape(blocks, out_rows, PANEL)
        block = here * blocks + lax.broadcasted_iota(jnp.int32, total.shape, 0)
        row = dp * data_rows + (2 * block + core) * out_rows + lax.broadcasted_iota(jnp.int32, total.shape, 1)
        col = lax.broadcasted_iota(jnp.int32, total.shape, 2)
        part[pl.ds(here * blocks, blocks)] = jnp.where(row >= start * PANEL + col, total, 0.0).astype(bf16)
        for i in range(blocks):
            to = here * blocks + i

            @pl.when(to != chip)
            def _(to=to):
                copy_part(to).start()

    for turn in range(chunks):
        multiply(turn)
        if turn > 0:
            send_parts(turn - 1)
    send_parts(chunks - 1)
    own_part = pltpu.make_async_copy(part.at[chip], out_ref.at[chip], rs_send.at[1])
    own_part.start()

    class_after.wait_send()
    class_before.wait_send()
    halo_after.wait_send()
    halo_before.wait_send()

    @pl.when(x < 2)
    def _():
        for copy in (copy_far, copy_in, copy_mate, copy_out, copy_in_late, copy_chosen):
            copy.wait_send()

    @pl.when(x >= 2)
    def _():
        copy_on.wait_send()

    for dj in (1, 2, 3):
        copy_y(dj).wait_send()
    for copy in over_y + to_right + to_left + relays + [to_far]:
        copy.wait_send()
    for turn in range(chunks):
        copy_sibling(turn).wait_send()

    others = remote(
        part.at[0 : chips - 1], out_ref.at[0 : chips - 1], rs_send.at[0], rs_recv.at[0], (dp, sibling)
    )
    others.wait_send()
    others.wait_recv()
    own_part.wait()


def body(sensitivity, panel_index, cell_class, tear_layer, coef_table):
    rows, cells = sensitivity.shape
    depth, plane = cell_class.shape
    slabs = lax.axis_size("slab")
    out_rows = rows // slabs
    groups = rows // GROUP
    chips = slabs // 2
    chunks = max(1, rows // CHUNK)
    bf16 = jnp.bfloat16
    dma = pltpu.SemaphoreType.DMA
    sweeps = coef_table.shape[0]
    ext = -(-(depth + 4) // 8) * 8
    parts = pl.pallas_call(
        functools.partial(kernel, slabs),
        out_shape=jax.ShapeDtypeStruct((chips, out_rows, PANEL), bf16),
        in_specs=[pl.BlockSpec(memory_space=pltpu.HBM)] * 5,
        out_specs=pl.BlockSpec(memory_space=pltpu.HBM),
        scratch_shapes=[
            pltpu.SMEM(panel_index.shape, jnp.int32),
            pltpu.SMEM(coef_table.shape, jnp.float32),
            pltpu.VMEM((depth, plane), jnp.int32),
            pltpu.VMEM((1, plane), jnp.int32),
            pltpu.VMEM((groups, GROUP, cells), bf16),
            pltpu.VMEM((4, 4, 2 * PIECE, cells // 2), bf16),
            pltpu.VMEM((2, 2, 2 * PIECE, cells // 2), bf16),
            pltpu.VMEM((2, 2, 2 * PIECE, cells // 2), bf16),
            pltpu.VMEM((2, 2 * PIECE, cells // 2), bf16),
            pltpu.VMEM((2, 2, 2 * PIECE, cells // 2), bf16),
            pltpu.VMEM((2, 2 * PIECE, cells // 2), bf16),
            pltpu.VMEM((4, 2 * PIECE, cells // 2), bf16),
            pltpu.VMEM((4, 2 * PIECE, cells // 2), bf16),
            pltpu.VMEM((2 * PIECE, cells // 2), bf16),
            pltpu.VMEM((2, 2 * PIECE, cells // 2), bf16),
            pltpu.VMEM((2, depth, plane), jnp.int32),
            pltpu.VMEM((ext, plane), jnp.int32),
            pltpu.VMEM((sweeps, 4, ext, plane), jnp.float32),
            pltpu.VMEM((sweeps, 4 * depth, PIECE, plane), jnp.float32),
            pltpu.VMEM((4, 4, 2 * PIECE, cells // 2), bf16),
            pltpu.VMEM((chunks, 2, rows // chunks // (2 * out_rows), out_rows, PANEL), jnp.float32),
            pltpu.VMEM((chunks, rows // chunks // (2 * out_rows), out_rows, PANEL), jnp.float32),
            pltpu.VMEM((chips, out_rows, PANEL), bf16),
            dma((5,)),
            dma((2,)),
            dma((2,)),
            dma((6,)),
            dma((6,)),
            dma((4,)),
            dma((4,)),
            dma((2,)),
            dma((2,)),
            dma((4,)),
            dma((4,)),
            dma((10,)),
            dma((10,)),
            dma((chunks,)),
            dma((chunks,)),
            dma((2,)),
            dma((1,)),
        ],
        compiler_params=pltpu.CompilerParams(
            collective_id=0, has_side_effects=True, vmem_limit_bytes=VMEM_LIMIT
        ),
        cost_estimate=pl.CostEstimate(
            flops=2 * rows * cells * PANEL, bytes_accessed=2 * rows * cells, transcendentals=0
        ),
        name="panel",
    )(
        panel_index,
        coef_table,
        sensitivity.reshape(groups, GROUP, cells),
        cell_class,
        tear_layer.reshape(1, plane),
    )
    return parts.astype(jnp.float32).sum(axis=0)


def solution(mesh):
    return jax.shard_map(
        body,
        mesh=mesh,
        in_specs=(P("dp", "slab"), P(), P("slab", None), P(), P()),
        out_specs=P(("dp", "slab"), None),
        check_vma=False,
    )
```

```python
import functools
import math

import jax
import jax.numpy as jnp
from jax import lax
from jax.experimental import pallas as pl
from jax.experimental.pallas import tpu as pltpu
from jax.sharding import PartitionSpec as P

WIDTH_Y = 32
PANEL = 128
GROUP = 32
PIECE = 8
CHUNK = 192
VMEM_LIMIT = 63 * 1024 * 1024


def kernel(
    slabs,
    panel_hbm,
    table_hbm,
    sens_hbm,
    class_hbm,
    tear_hbm,
    out_ref,
    panel_ref,
    table_ref,
    class_ref,
    tear_ref,
    sens,
    send1,
    recv_early,
    recv_late,
    fwd1,
    pair1,
    chosen1,
    send2,
    recv2,
    raw,
    halo,
    class_halo,
    class_ext,
    coef,
    field,
    gath,
    product,
    sibling_in,
    part,
    load_sem,
    class_send,
    class_recv,
    s1_send,
    s1_recv,
    s2_send,
    s2_recv,
    h_send,
    h_recv,
    g5_send,
    g5_recv,
    g6_send,
    g6_recv,
    sib_send,
    sib_recv,
    rs_send,
    rs_recv,
):
    f32 = jnp.float32
    bf16 = jnp.bfloat16
    dp = lax.axis_index("dp")
    me = lax.axis_index("slab")
    x = lax.div(dp, 4)
    yh = lax.rem(dp, 4)
    groups, _, cells = sens.shape
    chips = slabs // 2
    core = lax.rem(me, 2)
    half = cells // 2
    chip = lax.div(me, 2)
    sibling = me + 1 - 2 * core
    depth, plane = class_ref.shape
    layers = depth * slabs
    out_rows = out_ref.shape[1]
    panels_dev = groups * GROUP // PANEL
    right = lax.rem(x + 1, 4)
    left = lax.rem(x + 3, 4)
    before = lax.rem(me + slabs - 1, slabs)
    after = lax.rem(me + 1, slabs)

    def at(x_to, y_to, slab_to):
        return (x_to * 4 + y_to, slab_to)

    def fold(rows):
        return jnp.concatenate([rows[:, :half], rows[:, half:]], axis=0).astype(bf16)

    def unfold(piece):
        piece = piece.astype(f32)
        return jnp.concatenate([piece[:PIECE], piece[PIECE:]], axis=1)

    def remote(src, dst, send_sem, recv_sem, target):
        return pltpu.make_async_remote_copy(
            src_ref=src,
            dst_ref=dst,
            send_sem=send_sem,
            recv_sem=recv_sem,
            device_id=target,
            device_id_type=pl.DeviceIdType.MESH,
        )

    loads = 4

    def load(i):
        part_of = pl.ds(i * (groups // loads), groups // loads)
        return pltpu.make_async_copy(sens_hbm.at[part_of], sens.at[part_of], load_sem.at[0])

    small = [
        pltpu.make_async_copy(source, target, load_sem.at[1 + i])
        for i, (source, target) in enumerate(
            [(class_hbm, class_ref), (tear_hbm, tear_ref), (table_hbm, table_ref), (panel_hbm, panel_ref)]
        )
    ]
    barrier = pltpu.get_barrier_semaphore()

    def start_loads():
        for i in range(loads):
            load(i).start()

    def wait_loads():
        pltpu.make_async_copy(sens_hbm, sens, load_sem.at[0]).wait()

    for copy in small:
        copy.start()

    @pl.when(x < 2)
    def _():
        start_loads()

    def greet(target):
        pl.semaphore_signal(
            barrier, inc=1, device_id=target, device_id_type=pl.DeviceIdType.MESH
        )

    for d in sorted(range(1, chips), key=lambda d: -min(d, chips - d)):
        greet((dp, lax.rem(me + 2 * d, slabs)))

    for dj in (2, 1, 3):
        greet(at(x, lax.rem(yh + dj, 4), me))
    greet((dp, before))
    greet((dp, after))
    greet(at(right, yh, me))
    greet(at(left, yh, me))
    greet(at(lax.rem(x + 2, 4), yh, me))

    @pl.when(x >= 2)
    def _():
        start_loads()

    for copy in small:
        copy.wait()

    start = panel_ref[0]
    owner = lax.div(start, panels_dev)
    x_owner = lax.div(owner, 4)
    y_owner = lax.rem(owner, 4)
    first_group = lax.rem(start, panels_dev) * 4

    @pl.when(x < 2)
    def _():
        wait_loads()
        for q in range(4):
            rows = sens[first_group + q].astype(f32)
            for j in range(4):
                send1[q, lax.rem(j - yh + 6, 4)] = fold(rows[j * PIECE : (j + 1) * PIECE])

    pl.semaphore_wait(barrier, 8 + chips - 1)

    def early(q):
        return send1.at[q, 0:2]

    def late(q):
        return send1.at[q, 2:4]

    mate = at(1 - x, yh, me)
    outer = at(3 - x, yh, me)
    copy_far = remote(early(x + 2), fwd1, s1_send.at[0], s1_recv.at[0], outer)
    copy_in = remote(early(1 - x), recv_early.at[x], s1_send.at[1], s1_recv.at[1], mate)
    copy_mate = remote(late(x + 2), pair1.at[x], s1_send.at[2], s1_recv.at[2], mate)
    copy_out = remote(early(3 - x), recv_early.at[x], s1_send.at[3], s1_recv.at[3], outer)
    copy_in_late = remote(late(1 - x), recv_late.at[x], s1_send.at[4], s1_recv.at[4], mate)
    copy_chosen = remote(chosen1, recv_late.at[0], s1_send.at[5], s1_recv.at[5], outer)
    copy_on = remote(fwd1, recv_early.at[3 - x], s1_send.at[1], s1_recv.at[1], at(5 - x, yh, me))

    def arrived(slot, to):
        remote(to, to, s1_send.at[slot], s1_recv.at[slot], at(right, yh, me)).wait_recv()

    @pl.when(x < 2)
    def _():
        for copy in (copy_far, copy_mate, copy_in, copy_out, copy_in_late):
            copy.start()
        recv_early[x] = send1[x, 0:2]
        recv_late[x] = send1[x, 2:4]
        pair1[x] = send1[3 - x, 2:4]

    class_after = remote(class_ref, class_halo.at[0], class_send.at[0], class_recv.at[0], (dp, after))
    class_before = remote(class_ref, class_halo.at[1], class_send.at[1], class_recv.at[1], (dp, before))
    class_after.start()
    class_before.start()

    class_after.wait_recv()
    class_before.wait_recv()
    class_ext[0:2] = class_halo[0, depth - 2 : depth]
    class_ext[2 : 2 + depth] = class_ref[...]
    class_ext[2 + depth : 4 + depth] = class_halo[1, 0:2]
    class_ext[4 + depth :] = jnp.zeros_like(class_ext[4 + depth :])
    classes = class_ext[...]
    layer = me * depth - 2 + lax.broadcasted_iota(jnp.int32, classes.shape, 0)
    valid = (layer >= 0) & (layer < layers)
    tear = jnp.broadcast_to(tear_ref[...], classes.shape)
    open_up = tear != layer
    open_down = tear != layer + 1
    for k in range(table_ref.shape[0]):
        a = jnp.zeros(classes.shape, f32)
        b = jnp.zeros(classes.shape, f32)
        for level in range(table_ref.shape[2]):
            a = jnp.where(classes == level, table_ref[k, 0, level], a)
            b = jnp.where(classes == level, table_ref[k, 1, level], b)
        a = jnp.where(valid, a, 0.0)
        b = jnp.where(valid, 4.0 * b, 0.0)
        up = jnp.where(open_up, b, 0.0)
        down = jnp.where(open_down, b, 0.0)
        coef[k, 0] = 1.0 - 4.0 * a - up - down
        coef[k, 1] = a
        coef[k, 2] = up
        coef[k, 3] = down

    def copy_y(dj):
        return remote(
            send2.at[dj], recv2.at[yh], s2_send.at[dj], s2_recv.at[yh], at(x, lax.rem(yh + dj, 4), me)
        )

    def wait_y(dj):
        j = lax.rem(yh + dj, 4)
        remote(send2.at[dj], recv2.at[j], s2_send.at[dj], s2_recv.at[j], at(x, j, me)).wait_recv()

    @pl.when(x >= 2)
    def _():
        arrived(0, fwd1)
        copy_on.start()
        arrived(3, recv_early.at[3 - x])

    arrived(1, recv_early.at[jnp.where(x < 2, 1 - x, x - 2)])
    chosen = recv_early[x_owner]
    send2[2] = chosen[0]
    copy_y(2).start()
    send2[3] = chosen[1]
    copy_y(3).start()

    @pl.when(x < 2)
    def _():
        arrived(2, pair1.at[1 - x])
        chosen1[...] = pair1[x_owner]
        copy_chosen.start()
        arrived(4, recv_late.at[1 - x])

    @pl.when(x >= 2)
    def _():
        arrived(5, recv_late.at[0])

    chosen = recv_late[jnp.where(x < 2, x_owner, 0)]
    send2[1] = chosen[1]
    copy_y(1).start()
    recv2[yh] = chosen[0]
    for dj in (2, 1, 3):
        wait_y(dj)

    raw[...] = recv2[y_owner]
    halo_after = remote(raw, halo.at[0], h_send.at[0], h_recv.at[0], (dp, after))
    halo_before = remote(raw, halo.at[1], h_send.at[1], h_recv.at[1], (dp, before))
    halo_after.start()
    halo_before.start()

    own_rows = unfold(raw[...])
    for g in range(depth):
        field[0, depth + g] = own_rows[:, g * plane : (g + 1) * plane]
    position = lax.broadcasted_iota(jnp.int32, (PIECE, plane), 1)
    column = lax.rem(position, WIDTH_Y)
    sweeps = table_ref.shape[0]

    def smooth(k, l):
        u = field[k, l]
        north = jnp.where(position >= WIDTH_Y, pltpu.roll(u, WIDTH_Y, 1), 0.0)
        south = jnp.where(position < plane - WIDTH_Y, pltpu.roll(u, plane - WIDTH_Y, 1), 0.0)
        west = jnp.where(column > 0, pltpu.roll(u, 1, 1), 0.0)
        east = jnp.where(column < WIDTH_Y - 1, pltpu.roll(u, plane - 1, 1), 0.0)
        e = l - depth + 2
        updated = (
            coef[k, 0, e : e + 1] * u
            + coef[k, 1, e : e + 1] * ((north + south) + (west + east))
            + coef[k, 2, e : e + 1] * field[k, l - 1]
            + coef[k, 3, e : e + 1] * field[k, l + 1]
        )
        if k + 1 < sweeps:
            field[k + 1, l] = updated
        else:
            g = l - depth
            field[0, 3 * depth + g] = updated

    def copy_g5(place, dj, lands):
        target = at(x, lax.rem(yh + dj, 4), me)
        return remote(gath.at[x, 0], gath.at[x, lands], g5_send.at[place], g5_recv.at[lands], target)

    over_y = [copy_g5(1, 1, 2), copy_g5(2, 3, 1), copy_g5(3, 2, 3)]

    def wait_g5(place):
        remote(gath.at[x, 0], gath.at[x, place], g5_send.at[place], g5_recv.at[place], at(right, yh, me)).wait_recv()

    def copy_g6(way, source, first, last, slot):
        part_of = gath.at[source, first:last]
        return remote(part_of, part_of, g6_send.at[slot], g6_recv.at[slot], at(way, yh, me))

    rounds = [(0, 1), (1, 3), (3, 4)]
    far = lax.rem(x + 2, 4)
    to_right = [copy_g6(right, x, *span, i) for i, span in enumerate(rounds)]
    to_left = [copy_g6(left, x, *span, 3 + i) for i, span in enumerate(rounds)]
    from_left = [copy_g6(right, left, *span, i) for i, span in enumerate(rounds)]
    from_right = [copy_g6(left, right, *span, 3 + i) for i, span in enumerate(rounds)]
    relays = [copy_g6(right, left, 0, 1, 6), copy_g6(right, left, 1, 2, 9), copy_g6(left, right, 2, 3, 7)]
    to_far = copy_g6(far, x, 3, 4, 8)
    relayed = [
        copy_g6(right, far, 0, 1, 6),
        copy_g6(right, far, 1, 2, 9),
        copy_g6(left, far, 2, 3, 7),
        copy_g6(far, far, 3, 4, 8),
    ]

    inner = [(0, l) for l in range(depth + 1, 2 * depth - 1)]
    done = set(inner)
    for k, l in inner:
        smooth(k, l)

    halo_after.wait_recv()
    halo_before.wait_recv()
    has_before = jnp.where(me > 0, 1.0, 0.0).astype(f32)
    has_after = jnp.where(me < slabs - 1, 1.0, 0.0).astype(f32)
    rows_before = unfold(halo[0]) * has_before
    rows_after = unfold(halo[1]) * has_after
    for g in range(depth):
        field[0, g] = rows_before[:, g * plane : (g + 1) * plane]
        field[0, 2 * depth + g] = rows_after[:, g * plane : (g + 1) * plane]

    def smooth_all(k, l):
        if k < 0 or (k, l) in done:
            return
        for near in (l - 1, l, l + 1):
            smooth_all(k - 1, near)
        smooth(k, l)
        done.add((k, l))

    for t in range(depth):
        smooth_all(sweeps - 1, depth + t)
    gath[x, 0] = fold(jnp.concatenate([field[0, 3 * depth + g] for g in range(depth)], axis=1))
    for copy in [*over_y, to_right[0], to_left[0]]:
        copy.start()

    from_left[0].wait_recv()
    relays[0].start()
    wait_g5(1)
    wait_g5(2)
    to_right[1].start()
    to_left[1].start()
    wait_g5(3)
    to_far.start()
    to_right[2].start()
    to_left[2].start()
    from_left[1].wait_recv()
    relays[1].start()
    from_right[0].wait_recv()
    from_right[1].wait_recv()
    relays[2].start()
    for copy in (from_left[2], from_right[2], *relayed):
        copy.wait_recv()

    @pl.when(x >= 2)
    def _():
        wait_loads()

    data_rows = groups * GROUP
    chunk = min(CHUNK, data_rows)
    chunks = data_rows // chunk
    blocks = chunk // (2 * out_rows)
    own_chunk = lax.div(chip, blocks)

    def copy_sibling(turn):
        return remote(
            product.at[turn, 1 - core], sibling_in.at[turn], sib_send.at[turn], sib_recv.at[turn], (dp, sibling)
        )

    def copy_part(to):
        return remote(part.at[to], out_ref.at[chip], rs_send.at[0], rs_recv.at[0], (dp, 2 * to + core))

    def chunk_of(turn):
        return lax.rem(own_chunk + 1 + turn, chunks)

    def multiply(turn):
        here = chunk_of(turn)
        part_of = pl.ds(here * (chunk // GROUP), chunk // GROUP)
        pieces = gath[...].reshape(2 * PANEL, half)
        first, second = [
            lax.dot_general(
                sens[part_of, :, h * half : (h + 1) * half].reshape(chunk, half),
                pieces,
                (((1,), (1,)), ((), ())),
                preferred_element_type=f32,
            )
            for h in range(2)
        ]
        lane = lax.broadcasted_iota(jnp.int32, (chunk, PANEL), 1)
        result = jnp.where(
            lax.rem(lane, 2 * PIECE) < PIECE,
            first[:, :PANEL] + pltpu.roll(second[:, :PANEL], PANEL - PIECE, 1),
            pltpu.roll(first[:, PANEL:], PIECE, 1) + second[:, PANEL:],
        )
        result = result.reshape(blocks, 2, out_rows, PANEL)
        for c in range(2):
            product[turn, c] = result[:, c]
        copy_sibling(turn).start()

    def send_parts(turn):
        here = chunk_of(turn)
        copy_sibling(turn).wait_recv()
        total = (product[turn, core] + sibling_in[turn]) * (1.0 / math.sqrt(layers * plane))
        lane = lax.broadcasted_iota(jnp.int32, (PANEL, PANEL), 0)
        wanted = lax.broadcasted_iota(jnp.int32, (PANEL, PANEL), 1)
        from_x = lax.div(wanted, GROUP)
        dj = lax.rem(lax.div(wanted, PIECE) + 4 - yh, 4)
        place = jnp.where(dj == 2, 3, jnp.where(dj == 3, 2, dj))
        held = 64 * lax.rem(from_x, 2) + 16 * place + 8 * lax.div(from_x, 2) + lax.rem(wanted, PIECE)
        total = jnp.dot(
            total.reshape(blocks * out_rows, PANEL),
            (lane == held).astype(f32),
            precision=lax.Precision.HIGHEST,
            preferred_element_type=f32,
        ).reshape(blocks, out_rows, PANEL)
        block = here * blocks + lax.broadcasted_iota(jnp.int32, total.shape, 0)
        row = dp * data_rows + (2 * block + core) * out_rows + lax.broadcasted_iota(jnp.int32, total.shape, 1)
        col = lax.broadcasted_iota(jnp.int32, total.shape, 2)
        part[pl.ds(here * blocks, blocks)] = jnp.where(row >= start * PANEL + col, total, 0.0).astype(bf16)
        for i in range(blocks):
            to = here * blocks + i

            @pl.when(to != chip)
            def _(to=to):
                copy_part(to).start()

    for turn in range(chunks):
        multiply(turn)
        if turn > 0:
            send_parts(turn - 1)
    send_parts(chunks - 1)
    own_part = pltpu.make_async_copy(part.at[chip], out_ref.at[chip], rs_send.at[1])
    own_part.start()

    class_after.wait_send()
    class_before.wait_send()
    halo_after.wait_send()
    halo_before.wait_send()

    @pl.when(x < 2)
    def _():
        for copy in (copy_far, copy_in, copy_mate, copy_out, copy_in_late, copy_chosen):
            copy.wait_send()

    @pl.when(x >= 2)
    def _():
        copy_on.wait_send()

    for dj in (1, 2, 3):
        copy_y(dj).wait_send()
    for copy in over_y + to_right + to_left + relays + [to_far]:
        copy.wait_send()
    for turn in range(chunks):
        copy_sibling(turn).wait_send()

    others = remote(
        part.at[0 : chips - 1], out_ref.at[0 : chips - 1], rs_send.at[0], rs_recv.at[0], (dp, sibling)
    )
    others.wait_send()
    others.wait_recv()
    own_part.wait()


def body(sensitivity, panel_index, cell_class, tear_layer, coef_table):
    rows, cells = sensitivity.shape
    depth, plane = cell_class.shape
    slabs = lax.axis_size("slab")
    out_rows = rows // slabs
    groups = rows // GROUP
    chips = slabs // 2
    chunks = max(1, rows // CHUNK)
    bf16 = jnp.bfloat16
    dma = pltpu.SemaphoreType.DMA
    sweeps = coef_table.shape[0]
    ext = -(-(depth + 4) // 8) * 8
    parts = pl.pallas_call(
        functools.partial(kernel, slabs),
        out_shape=jax.ShapeDtypeStruct((chips, out_rows, PANEL), bf16),
        in_specs=[pl.BlockSpec(memory_space=pltpu.HBM)] * 5,
        out_specs=pl.BlockSpec(memory_space=pltpu.HBM),
        scratch_shapes=[
            pltpu.SMEM(panel_index.shape, jnp.int32),
            pltpu.SMEM(coef_table.shape, jnp.float32),
            pltpu.VMEM((depth, plane), jnp.int32),
            pltpu.VMEM((1, plane), jnp.int32),
            pltpu.VMEM((groups, GROUP, cells), bf16),
            pltpu.VMEM((4, 4, 2 * PIECE, cells // 2), bf16),
            pltpu.VMEM((2, 2, 2 * PIECE, cells // 2), bf16),
            pltpu.VMEM((2, 2, 2 * PIECE, cells // 2), bf16),
            pltpu.VMEM((2, 2 * PIECE, cells // 2), bf16),
            pltpu.VMEM((2, 2, 2 * PIECE, cells // 2), bf16),
            pltpu.VMEM((2, 2 * PIECE, cells // 2), bf16),
            pltpu.VMEM((4, 2 * PIECE, cells // 2), bf16),
            pltpu.VMEM((4, 2 * PIECE, cells // 2), bf16),
            pltpu.VMEM((2 * PIECE, cells // 2), bf16),
            pltpu.VMEM((2, 2 * PIECE, cells // 2), bf16),
            pltpu.VMEM((2, depth, plane), jnp.int32),
            pltpu.VMEM((ext, plane), jnp.int32),
            pltpu.VMEM((sweeps, 4, ext, plane), jnp.float32),
            pltpu.VMEM((sweeps, 4 * depth, PIECE, plane), jnp.float32),
            pltpu.VMEM((4, 4, 2 * PIECE, cells // 2), bf16),
            pltpu.VMEM((chunks, 2, rows // chunks // (2 * out_rows), out_rows, PANEL), jnp.float32),
            pltpu.VMEM((chunks, rows // chunks // (2 * out_rows), out_rows, PANEL), jnp.float32),
            pltpu.VMEM((chips, out_rows, PANEL), bf16),
            dma((5,)),
            dma((2,)),
            dma((2,)),
            dma((6,)),
            dma((6,)),
            dma((4,)),
            dma((4,)),
            dma((2,)),
            dma((2,)),
            dma((4,)),
            dma((4,)),
            dma((10,)),
            dma((10,)),
            dma((chunks,)),
            dma((chunks,)),
            dma((2,)),
            dma((1,)),
        ],
        compiler_params=pltpu.CompilerParams(
            collective_id=0, has_side_effects=True, vmem_limit_bytes=VMEM_LIMIT
        ),
        cost_estimate=pl.CostEstimate(
            flops=2 * rows * cells * PANEL, bytes_accessed=2 * rows * cells, transcendentals=0
        ),
        name="panel",
    )(
        panel_index,
        coef_table,
        sensitivity.reshape(groups, GROUP, cells),
        cell_class,
        tear_layer.reshape(1, plane),
    )
    return parts.astype(jnp.float32).sum(axis=0)


def solution(mesh):
    return jax.shard_map(
        body,
        mesh=mesh,
        in_specs=(P("dp", "slab"), P(), P("slab", None), P(), P()),
        out_specs=P(("dp", "slab"), None),
        check_vma=False,
    )
```
